512 devices in a mesh: well: 64 (over z_lo, x, core), shot: 8 (over z_hi, y).
Axes of the slice: x: 4, y: 4, z: 16 (z_hi: 2, z_lo: 8; z = z_hi * 8 + z_lo), core: 2. Of those that a mesh axis runs over, the one named last changes fastest.
Arguments:
- traces: bfloat16 [64, 2048, 1024], P('shot', 'well'), may hold values from -6 to 6
- gate_starts: int32 [64, 2048], P('shot'), may hold values from 0 to 896
- section_offsets: int32 [128], P('well'), may hold values from 0 to 240, as said below
Outputs:
- cross_spectra: float32 [2048, 16, 1026], P(('well', 'shot'))
The draws below stay inside these ranges and needn't reach their ends.
Inputs may be any that keep to these rules, and one draw needn't show every extreme that they name: `section_offsets`: one offset a section; some section has offset 0 and some has 240.
All inputs are finite; a program needn't handle non-finite values.
Results may differ from the reference program's by a relative error of at most 0.007.
Values may be sent and summed in bfloat16 or wider, within the bound.
A program may use at most 64 MiB of HBM per device.

```python
import math
import jax
import jax.numpy as jnp
from jax import lax

NT = 1024
FREQS = 513
W = 128
SEC = 16
SPAN = 256
PARTNERS = 16
RECEIVERS = 2048
SHOTS = 64
SECTIONS = 128


def draw_section_offsets(key, part):
    key = jax.random.fold_in(key, 11)
    values_key, first_key, second_key = jax.random.split(key, 3)
    top_value = SPAN - PARTNERS
    values = jax.random.randint(values_key, (SECTIONS,), 0, top_value + 1)
    first_slot = jax.random.randint(first_key, (), 0, SECTIONS)
    second_slot = (first_slot + 1 + jax.random.randint(second_key, (), 0, SECTIONS - 1)) % SECTIONS
    values = values.at[first_slot].set(top_value).at[second_slot].set(0)
    return values.astype(jnp.int32)


def set_ends(values, rng, smallest, largest):
    longest = values.shape.index(max(values.shape))
    spots = []
    for shift in (0, 1):
        where = [jax.random.randint(jax.random.fold_in(rng, axis), (), 0, length) for axis, length in enumerate(values.shape)]
        where[longest] = (where[longest] + shift) % values.shape[longest]
        spots.append(tuple(where))
    return values.at[spots[0]].set(smallest).at[spots[1]].set(largest)


def block_scale(key, dims, cuts, smallest, largest):
    factor_of = 1.0
    for dim, blocks in cuts:
        draws = jax.random.uniform(jax.random.fold_in(jax.random.fold_in(key, 6), dim), (blocks,), jnp.float32, smallest / len(cuts), largest / len(cuts))
        factor_of = factor_of * jnp.repeat(jnp.exp(draws), dims[dim] // blocks).reshape((-1,) + (1,) * (len(dims) - 1 - dim))
    return factor_of


def centred(own_key, dims, spread, most, shards=(), kind=jnp.bfloat16):
    level = block_scale(own_key, dims, shards, -0.22, 0.18) if shards else 1.0
    entries = jax.random.normal(own_key, dims, jnp.float32) * spread * level
    return jnp.minimum(jnp.maximum(entries, -most), most).astype(kind)


def setup_inputs(seed: int = 0) -> dict:
    streams_of = jax.random.split(jax.random.key(seed), 4)
    traces = centred(streams_of[0], (SHOTS, RECEIVERS, NT), 1.0, 6.0, ((0, 8), (1, 64)))
    gate_starts = set_ends(jax.random.randint(streams_of[1], (SHOTS, RECEIVERS), 0, NT - W + 1), jax.random.fold_in(streams_of[1], 1), 0, NT - W).astype(jnp.int32)
    section_offsets = draw_section_offsets(jax.random.fold_in(streams_of[3], 71), 0)
    return dict(traces=traces, gate_starts=gate_starts, section_offsets=section_offsets)


two_pi = 2.0 * math.pi

def make_tables():
    sample_steps = jnp.arange(W, dtype=jnp.int32)
    window_taper = 0.5 - 0.5 * jnp.cos((sample_steps.astype(jnp.float32) + 0.5) * (two_pi / W))
    freq_count = NT // 2 + 1
    frequency = jnp.arange(freq_count, dtype=jnp.int32)
    phase_index = sample_steps[:, None] * frequency[None, :] % NT
    phase_angle = phase_index.astype(jnp.float32) * (two_pi / NT)
    scale_factor = 1.0 / math.sqrt(W)
    freq_table = (jnp.concatenate([jnp.cos(phase_angle), -jnp.sin(phase_angle)], axis=1) * scale_factor).astype(jnp.bfloat16)
    return (window_taper, freq_table)

def gate_windows(trace_rows, gate_rows, window_taper):
    sample_steps = jnp.arange(W, dtype=jnp.int32)
    positions = gate_rows[..., None] + sample_steps
    picked = jnp.take_along_axis(trace_rows, positions, axis=-1)
    return (window_taper * picked.astype(jnp.float32)).astype(jnp.bfloat16)

def spectra_of(windows, gate_rows, freq_table):
    lead_shape = windows.shape[:-1]
    freq_count = freq_table.shape[1] // 2
    unrotated = jnp.dot(windows.reshape(-1, W), freq_table, preferred_element_type=jnp.float32)
    unrotated = unrotated.reshape(lead_shape + (2 * freq_count,))
    frequency = jnp.arange(freq_count, dtype=jnp.int32)
    phase_angle = (gate_rows[..., None] * frequency % NT).astype(jnp.float32) * (two_pi / NT)
    cosine = jnp.cos(phase_angle)
    sine_part = jnp.sin(phase_angle)
    real_in = unrotated[..., :freq_count]
    imag_in = unrotated[..., freq_count:]
    rotated = jnp.concatenate([cosine * real_in + sine_part * imag_in, cosine * imag_in - sine_part * real_in], axis=-1)
    return rotated.astype(jnp.bfloat16)

def section_cross(own_spec, partner_block):
    freq_count = own_spec.shape[-1] // 2
    sec_rows = own_spec.shape[1]
    own_wide = own_spec.astype(jnp.float32)
    own_real = own_wide[..., :freq_count]
    own_imag = own_wide[..., freq_count:]
    rows_out = []
    for partner in range(PARTNERS):
        other = partner_block[:, partner:partner + sec_rows].astype(jnp.float32)
        other_real = other[..., :freq_count]
        other_imag = other[..., freq_count:]
        real_part = lax.optimization_barrier(jnp.sum(own_real * other_real + own_imag * other_imag, axis=0))
        imag_part = lax.optimization_barrier(jnp.sum(own_real * other_imag - own_imag * other_real, axis=0))
        rows_out.append(jnp.concatenate([real_part, imag_part], axis=-1))
    return jnp.stack(rows_out, axis=1)

def reference(traces, gate_starts, section_offsets):
    window_taper, freq_table = make_tables()

    def one_shot(inputs):
        trace_rows, gate_rows = inputs
        return spectra_of(gate_windows(trace_rows, gate_rows, window_taper), gate_rows, freq_table)
    spectra = lax.map(one_shot, (traces, gate_starts))
    padded = jnp.pad(spectra, ((0, 0), (0, SPAN), (0, 0)))

    def one_section(section):
        offset = section_offsets[section]
        own_spec = lax.dynamic_slice_in_dim(spectra, section * SEC, SEC, 1)
        partner_block = lax.dynamic_slice_in_dim(padded, section * SEC + offset, SEC + PARTNERS - 1, 1)
        return section_cross(own_spec, partner_block)
    result = lax.map(one_section, jnp.arange(SECTIONS, dtype=jnp.int32))
    return result.reshape(RECEIVERS, PARTNERS, 2 * FREQS)
```

```python
import functools
import math

import jax
import jax.numpy as jnp
import ml_dtypes
import numpy as np
from jax import lax
from jax.experimental import pallas as pl
from jax.experimental.pallas import tpu as pltpu
from jax.sharding import PartitionSpec as P

NT = 1024
W = 128
SEC = 16
PARTNERS = 16
PLANE = 8
RECV = 32
OWN_PAIRS = 2
REACH_PAIRS = 10
BLOCKS = REACH_PAIRS + OWN_PAIRS + 1
SLOTS = 2 * (REACH_PAIRS + OWN_PAIRS)
MESH = pl.DeviceIdType.MESH
f32 = jnp.float32
bf16 = jnp.bfloat16

SHOT_PEERS = [(1, 0), (1, 1), (1, 3), (1, 2), (0, 1), (0, 3), (0, 2)]


def packed_table():
    steps = np.arange(W)
    k = np.arange(NT // 2)
    angle = ((steps[:, None] * k[None, :]) % NT).astype(np.float32) * np.float32(2 * math.pi / NT)
    real = np.cos(angle)
    imag = -np.sin(angle)
    imag[:, 0] = np.cos(math.pi * steps)
    scale = np.float32(1.0 / math.sqrt(W))
    return (np.concatenate([real, imag], axis=1) * scale).astype(ml_dtypes.bfloat16)


def place():
    well = lax.axis_index("well")
    shot = lax.axis_index("shot")
    return well // PLANE, well % PLANE, shot // 4, shot % 4


def gather_kernel(
    off_ref, traces_hbm, gates_hbm, out_hbm,
    traces, gates, gate_cols, rows, reach, sending,
    load_sem, x_send, x_recv, z_send, z_recv, c_send, c_recv, s_send, s_recv,
):
    z, wp, zh, y = place()
    x, core = wp // 2, wp % 2
    well = z * PLANE + wp
    shot = zh * 4 + y

    def well_at(plane, column, which):
        return plane * PLANE + column * 2 + which

    x_peers = [(x + d) % 4 for d in (1, 3, 2)]
    other_core = (well_at(z, x, 1 - core), shot)
    shot_peers = [((zh + a) % 2 * 4 + (y + b) % 4) for a, b in SHOT_PEERS]

    barrier = pltpu.get_barrier_semaphore()
    for peer in shot_peers:
        pl.semaphore_signal(barrier, inc=1, device_id=(well, peer), device_id_type=MESH)
    for column in x_peers:
        pl.semaphore_signal(barrier, inc=1, device_id=(well_at(z, column, core), shot), device_id_type=MESH)
    pl.semaphore_signal(barrier, inc=1, device_id=other_core, device_id_type=MESH)

    @pl.when(z < 7)
    def _():
        for column in range(4):
            pl.semaphore_signal(barrier, inc=1, device_id=(well_at(z + 1, column, core), shot), device_id_type=MESH)

    load_traces = pltpu.make_async_copy(traces_hbm, traces, load_sem.at[0])
    load_traces.start()
    here = pl.multiple_of(z * 256, 256)
    ahead = pl.multiple_of(jnp.minimum(z + 1, 7) * 256, 256)
    load_here = pltpu.make_async_copy(gates_hbm.at[:, pl.ds(here, 256)], gates.at[:, pl.ds(0, 256)], load_sem.at[1])
    load_ahead = pltpu.make_async_copy(gates_hbm.at[:, pl.ds(ahead, 256)], gates.at[:, pl.ds(256, 256)], load_sem.at[2])
    load_here.start()
    load_ahead.start()

    @pl.when(z == 7)
    def _():
        reach[pl.ds(128, 128)] = jnp.zeros((128, 16, W), bf16)

    load_here.wait()
    load_ahead.wait()
    all_gates = gates[...]
    gate_cols[...] = jnp.transpose(all_gates[:, :256].astype(f32))
    lane = lax.broadcasted_iota(jnp.int32, (RECV, W), 1)
    taper = 0.5 - 0.5 * jnp.cos((lane[:8].astype(f32) + 0.5) * (2 * math.pi / W))
    taper = jnp.concatenate([taper] * (RECV // 8), axis=0)
    columns = gate_cols[pl.ds(pl.multiple_of(wp * RECV, RECV), RECV), :].astype(jnp.int32)
    load_traces.wait()
    for s in range(8):
        data = traces[s].astype(f32)
        gate = jnp.broadcast_to(columns[:, s : s + 1], (RECV, W))
        fine = gate & 127
        tiles = [data[:, k * W : (k + 1) * W] for k in range(8)]
        pick = (gate & 512) != 0
        four = [jnp.where(pick, tiles[k + 4], tiles[k]) for k in range(4)] + [tiles[4]]
        pick = (gate & 256) != 0
        three = [jnp.where(pick, four[k + 2], four[k]) for k in range(3)]
        pick = (gate & 128) != 0
        low = jnp.where(pick, three[1], three[0])
        high = jnp.where(pick, three[2], three[1])
        turned = jnp.where(lane >= fine, low, high)
        for bit in range(7):
            step = 1 << bit
            turned = jnp.where((fine & step) != 0, pltpu.roll(turned, W - step, 1), turned)
        rows[pl.ds(s, RECV, stride=8), :] = turned * taper
    own_first = pl.multiple_of(wp * 16, 16)
    reach[pl.ds(own_first, 16)] = rows[...].reshape(16, 16, W).astype(bf16)

    halves = jnp.concatenate([all_gates >> 3, all_gates & 7], axis=0).astype(f32).astype(bf16)
    lanes = lax.broadcasted_iota(jnp.int32, (512, W), 1)
    index = lax.broadcasted_iota(jnp.int32, (512, W), 0)
    members = [(a, b) for a, b in SHOT_PEERS] + [(0, 0)]
    for k, (a, b) in enumerate(members):
        to_zh, to_y = (zh + a) % 2, (y + b) % 4
        own = wp * RECV + to_zh * SEC + to_y * 4
        start = (own + off_ref[to_zh]) // 2 * 2
        wanted = jnp.where(lanes < 32, start + lanes, own - 32 + lanes)
        chosen = jnp.where(index == wanted, 1.0, 0.0).astype(bf16)
        block = jnp.dot(halves, chosen, preferred_element_type=f32)
        sending[k, BLOCKS - 1] = block.astype(bf16)

    @pl.when(z > 0)
    def _():
        pl.semaphore_wait(barrier, 15)

    @pl.when(z == 0)
    def _():
        pl.semaphore_wait(barrier, 11)

    def slot(plane, column, which):
        first = pl.multiple_of((plane * PLANE + column * 2 + which) * 16, 16)
        return reach.at[pl.ds(first, 16)]

    mine = slot(0, x, core)
    x_copies = []
    for i, column in enumerate(x_peers):
        copy = pltpu.make_async_remote_copy(
            src_ref=mine, dst_ref=mine, send_sem=x_send.at[i], recv_sem=x_recv.at[i],
            device_id=(well_at(z, column, core), shot), device_id_type=MESH,
        )
        copy.start()
        x_copies.append(copy)

    def z_copy(i):
        return pltpu.make_async_remote_copy(
            src_ref=mine, dst_ref=slot(1, x, core), send_sem=z_send.at[i], recv_sem=z_recv.at[i],
            device_id=(well_at(jnp.maximum(z - 1, 0), (x + i) % 4, core), shot), device_id_type=MESH,
        )

    @pl.when(z > 0)
    def _():
        for i in range(4):
            z_copy(i).start()

    def c_copy(plane, column, i):
        block = slot(plane, column, core)
        return pltpu.make_async_remote_copy(
            src_ref=block, dst_ref=block, send_sem=c_send.at[i], recv_sem=c_recv.at[i],
            device_id=other_core, device_id_type=MESH,
        )

    c_copies = [c_copy(0, x, 0)]
    c_copies[0].start()
    for i, d in enumerate((1, 3, 2)):
        x_copies[i].wait_recv()
        copy = c_copy(0, (x - d + 4) % 4, 1 + i)
        copy.start()
        c_copies.append(copy)

    @pl.when(z < 7)
    def _():
        for i in range(4):
            z_copy(i).wait_recv()
            c_copy(1, (x - i + 4) % 4, 4 + i).start()

    for i in range(4):
        c_copies[i].wait()

    @pl.when(z < 7)
    def _():
        for i in range(4):
            c_copy(1, (x - i + 4) % 4, 4 + i).wait()

    s_copies = []
    for k, (a, b) in enumerate(members):
        to_zh, to_y = (zh + a) % 2, (y + b) % 4
        own = wp * 16 + to_zh * 8 + to_y * 2
        first = own + off_ref[to_zh] // 2
        sending[k, :REACH_PAIRS] = reach[pl.ds(first, REACH_PAIRS)]
        sending[k, REACH_PAIRS : REACH_PAIRS + OWN_PAIRS] = reach[pl.ds(own, OWN_PAIRS)]
        if k < 7:
            copy = pltpu.make_async_remote_copy(
                src_ref=sending.at[k], dst_ref=out_hbm.at[shot], send_sem=s_send.at[k], recv_sem=s_recv.at[k],
                device_id=(well, shot_peers[k]), device_id_type=MESH,
            )
        else:
            copy = pltpu.make_async_copy(sending.at[k], out_hbm.at[shot], load_sem.at[3])
        copy.start()
        s_copies.append(copy)
    for copy in x_copies:
        copy.wait_send()

    @pl.when(z > 0)
    def _():
        for i in range(4):
            z_copy(i).wait_send()

    for copy in s_copies:
        copy.wait()


def turn(angle):
    half = angle * math.pi
    sq = half * half
    sine = half * (1.0 + sq * (-1 / 6 + sq * (1 / 120 + sq * (-1 / 5040 + sq * (1 / 362880 - sq * (1 / 39916800))))))
    cosine = 1.0 + sq * (
        -0.5 + sq * (1 / 24 + sq * (-1 / 720 + sq * (1 / 40320 + sq * (-1 / 3628800 + sq * (1 / 479001600)))))
    )
    return 1.0 - 2.0 * sine * sine, 2.0 * sine * cosine


def fraction(value):
    return value - jnp.round(value)


def fold(parts):
    row = lax.broadcasted_iota(jnp.int32, (8, W), 0)
    while len(parts) > 1:
        half = len(parts) // 2
        upper = (row & half) == 0
        merged = []
        for i in range(half):
            first, second = parts[i], parts[i + half]
            kept = jnp.where(upper, first, second)
            moved = jnp.where(upper, second, first)
            if half == 4:
                moved = pltpu.roll(moved, 4, 0)
            else:
                moved = jnp.where(upper, pltpu.roll(moved, 8 - half, 0), pltpu.roll(moved, half, 0))
            merged.append(kept + moved)
        parts = merged
    return parts[0]


def cross_kernel(off_ref, data, table, out, flat, gate_vals, spectra):
    z, wp, zh, y = place()
    odd = off_ref[zh] & 1
    lane = lax.broadcasted_iota(jnp.int32, (8, W), 1)
    lane_f = lane.astype(f32)

    for k in range(8):
        block = data[k, BLOCKS - 1].astype(f32)
        gate = block[:8] * 8.0 + block[8:]
        step_cos, step_sin = turn(fraction(gate * 0.125))
        for slot in range(SLOTS):
            column = slot if slot < 20 else 12 + slot
            for i, value in enumerate((gate, step_cos, step_sin)):
                gate_vals[slot, k, i] = jnp.broadcast_to(value[:, column : column + 1], (8, W))

    @pl.loop(0, SLOTS // 2)
    def _(p):
        left = data[:, p].reshape(8 * 16, W)
        flat[...] = jnp.dot(left, table[...], preferred_element_type=f32)
        for par in range(2):
            slot = 2 * p + par
            for k in range(8):
                first = k * 16 + par * 8
                gate = gate_vals[slot, k, 0]
                step_cos = gate_vals[slot, k, 1]
                step_sin = gate_vals[slot, k, 2]
                cosine, sine = turn(fraction(gate * (lane_f * (1.0 / NT))))
                for t in range(4):
                    real = flat[first : first + 8, t * W : (t + 1) * W]
                    imag = flat[first : first + 8, (4 + t) * W : (5 + t) * W]
                    if t == 0:
                        alternating = 1.0 - 2.0 * jnp.abs(gate - 2.0 * jnp.floor(gate * 0.5))
                        imag_cos = jnp.where(lane == 0, alternating, cosine)
                    else:
                        imag_cos = cosine
                    new_real = cosine * real + sine * imag
                    new_imag = imag_cos * imag - sine * real
                    rows = slice(k * 8, k * 8 + 8)
                    spectra[slot, t, 0, rows, :] = new_real.astype(bf16).astype(f32)
                    spectra[slot, t, 1, rows, :] = new_imag.astype(bf16).astype(f32)
                    if t < 3:
                        cosine, sine = (
                            cosine * step_cos - sine * step_sin,
                            sine * step_cos + cosine * step_sin,
                        )

    @pl.loop(0, 4)
    def _(a):
        imags = []
        for t in range(4):
            own = [(spectra[20 + a, t, 0, k * 8 : k * 8 + 8, :], spectra[20 + a, t, 1, k * 8 : k * 8 + 8, :]) for k in range(8)]
            for group in range(2):
                sums = []
                for j in range(8):
                    slot = a + odd + group * 8 + j
                    one = two = three = None
                    for k in range(8):
                        re = spectra[slot, t, 0, k * 8 : k * 8 + 8, :]
                        im = spectra[slot, t, 1, k * 8 : k * 8 + 8, :]
                        first = own[k][0] * re
                        second = own[k][1] * im
                        third = own[k][0] * im - own[k][1] * re
                        one = first if one is None else one + first
                        two = second if two is None else two + second
                        three = third if three is None else three + third
                    sums.append((one, two, three))
                rows = pl.ds(group * 8, 8)
                if t == 0:
                    ones = fold([s[0] for s in sums])
                    twos = fold([s[1] for s in sums])
                    threes = fold([s[2] for s in sums])
                    out[a, rows, :W] = jnp.where(lane == 0, ones, ones + twos)
                    imags.append((twos, jnp.where(lane == 0, 0.0, threes)))
                else:
                    out[a, rows, t * W : (t + 1) * W] = fold([s[0] + s[1] for s in sums])
                    threes = fold([s[2] for s in sums])
                    imags.append((None, threes))
        for group in range(2):
            rows = pl.ds(group * 8, 8)
            before = imags[group][0]
            for t in range(4):
                turned = pltpu.roll(imags[2 * t + group][1], 1, 1)
                out[a, rows, (4 + t) * W : (5 + t) * W] = jnp.where(lane == 0, before, turned)
                before = turned
            out[a, rows, 8 * W : 8 * W + 2] = jnp.where(lane == 0, before, 0.0)[:, :2]


def local(traces, gate_starts, section_offsets):
    any_space = pl.BlockSpec(memory_space=pl.ANY)
    smem = pl.BlockSpec(memory_space=pltpu.SMEM)
    vmem = pl.BlockSpec(memory_space=pltpu.VMEM)
    dma = pltpu.SemaphoreType.DMA
    arrived = pl.pallas_call(
        gather_kernel,
        out_shape=jax.ShapeDtypeStruct((8, BLOCKS, 16, W), bf16),
        in_specs=[smem, any_space, any_space],
        out_specs=any_space,
        scratch_shapes=[
            pltpu.VMEM((8, RECV, NT), bf16),
            pltpu.VMEM((8, 512), jnp.int32),
            pltpu.VMEM((256, 8), f32),
            pltpu.VMEM((RECV * 8, W), f32),
            pltpu.VMEM((256, 16, W), bf16),
            pltpu.VMEM((8, BLOCKS, 16, W), bf16),
            dma((4,)), dma((3,)), dma((3,)), dma((4,)), dma((4,)), dma((8,)), dma((8,)), dma((7,)), dma((7,)),
        ],
        compiler_params=pltpu.CompilerParams(
            collective_id=0, has_side_effects=True, vmem_limit_bytes=16 * 2**20
        ),
        name="gather",
    )(section_offsets, traces, gate_starts)
    return pl.pallas_call(
        cross_kernel,
        out_shape=jax.ShapeDtypeStruct((4, PARTNERS, NT + 2), f32),
        in_specs=[smem, vmem, vmem],
        out_specs=vmem,
        scratch_shapes=[
            pltpu.VMEM((128, NT), f32),
            pltpu.VMEM((SLOTS, 8, 3, 8, W), f32),
            pltpu.VMEM((SLOTS, 4, 2, 64, W), f32),
        ],
        compiler_params=pltpu.CompilerParams(vmem_limit_bytes=32 * 2**20),
        name="cross",
    )(section_offsets, arrived, jnp.asarray(packed_table()))


def solution(mesh):
    in_specs = (P("shot", "well", None), P("shot", None), P("well"))
    out_specs = P(("well", "shot"), None, None)
    return jax.shard_map(local, mesh=mesh, in_specs=in_specs, out_specs=out_specs, check_vma=False)
```

```python
import functools
import math

import jax
import jax.numpy as jnp
import ml_dtypes
import numpy as np
from jax import lax
from jax.experimental import pallas as pl
from jax.experimental.pallas import tpu as pltpu
from jax.sharding import PartitionSpec as P

NT = 1024
W = 128
SEC = 16
PARTNERS = 16
PLANE = 8
RECV = 32
OWN_PAIRS = 2
REACH_PAIRS = 10
BLOCKS = REACH_PAIRS + OWN_PAIRS + 1
SEC_REACH = 16
SEC_OWN = 8
SEC_BLOCKS = SEC_REACH + SEC_OWN + 1
SLOTS = 2 * (REACH_PAIRS + OWN_PAIRS)
MESH = pl.DeviceIdType.MESH
f32 = jnp.float32
bf16 = jnp.bfloat16

def packed_table():
    steps = np.arange(W)
    k = np.arange(NT // 2)
    angle = ((steps[:, None] * k[None, :]) % NT).astype(np.float32) * np.float32(2 * math.pi / NT)
    real = np.cos(angle)
    imag = -np.sin(angle)
    imag[:, 0] = np.cos(math.pi * steps)
    scale = np.float32(1.0 / math.sqrt(W))
    return (np.concatenate([real, imag], axis=1) * scale).astype(ml_dtypes.bfloat16)


def place():
    well = lax.axis_index("well")
    shot = lax.axis_index("shot")
    return well // PLANE, well % PLANE, shot // 4, shot % 4


def gather_kernel(
    off_hbm, traces_hbm, gates_hbm, out_hbm,
    off_ref, traces, gates, gate_cols, rows, reach, chosen, far,
    load_sem, trace_sem, x_send, x_recv, z_send, z_recv, c_send, c_recv,
    far_send, far_recv, y_send, y_recv, keep_sem,
):
    z, wp, zh, y = place()
    x, core = wp // 2, wp % 2
    well = z * PLANE + wp
    shot = zh * 4 + y
    far_shot = (1 - zh) * 4 + y

    def well_at(plane, column, which):
        return plane * PLANE + column * 2 + which

    x_peers = [(x + d) % 4 for d in (1, 3, 2)]
    y_peers = [(y + d) % 4 for d in (1, 3, 2)]
    other_core = (well_at(z, x, 1 - core), shot)
    across = (well, far_shot)

    barrier = pltpu.get_barrier_semaphore()
    pl.semaphore_signal(barrier, inc=1, device_id=across, device_id_type=MESH)
    for column in x_peers:
        pl.semaphore_signal(barrier, inc=1, device_id=(well_at(z, column, core), shot), device_id_type=MESH)

    @pl.when(z < 7)
    def _():
        for column in range(4):
            pl.semaphore_signal(barrier, inc=1, device_id=(well_at(z + 1, column, core), shot), device_id_type=MESH)

    for peer in y_peers:
        pl.semaphore_signal(barrier, inc=1, device_id=(well, zh * 4 + peer), device_id_type=MESH)
    pl.semaphore_signal(barrier, inc=1, device_id=other_core, device_id_type=MESH)

    here = pl.multiple_of(z * 256, 256)
    ahead = pl.multiple_of(jnp.minimum(z + 1, 7) * 256, 256)
    load_here = pltpu.make_async_copy(gates_hbm.at[:, pl.ds(here, 256)], gates.at[:, pl.ds(0, 256)], load_sem.at[0])
    load_ahead = pltpu.make_async_copy(gates_hbm.at[:, pl.ds(ahead, 256)], gates.at[:, pl.ds(256, 256)], load_sem.at[1])
    load_off = pltpu.make_async_copy(off_hbm, off_ref, load_sem.at[2])
    load_here.start()
    load_traces = [pltpu.make_async_copy(traces_hbm.at[s], traces.at[s], trace_sem.at[s]) for s in range(8)]
    for copy in load_traces:
        copy.start()
    load_ahead.start()
    load_off.start()

    @pl.when(z == 7)
    def _():
        reach[pl.ds(128, 128)] = jnp.zeros((128, 16, W), bf16)

    lane = lax.broadcasted_iota(jnp.int32, (RECV, W), 1)
    taper = 0.5 - 0.5 * jnp.cos((lane[:8].astype(f32) + 0.5) * (2 * math.pi / W))
    taper = jnp.concatenate([taper] * (RECV // 8), axis=0)
    load_here.wait()
    gate_cols[...] = jnp.transpose(gates[:, :256].astype(f32))
    columns = gate_cols[pl.ds(pl.multiple_of(wp * RECV, RECV), RECV), :].astype(jnp.int32)
    for s in range(8):
        load_traces[s].wait()
        data = traces[s].astype(f32)
        gate = jnp.broadcast_to(columns[:, s : s + 1], (RECV, W))
        fine = gate & 127
        tiles = [data[:, k * W : (k + 1) * W] for k in range(8)]
        pick = (gate & 512) != 0
        four = [jnp.where(pick, tiles[k + 4], tiles[k]) for k in range(4)] + [tiles[4]]
        pick = (gate & 256) != 0
        three = [jnp.where(pick, four[k + 2], four[k]) for k in range(3)]
        pick = (gate & 128) != 0
        low = jnp.where(pick, three[1], three[0])
        high = jnp.where(pick, three[2], three[1])
        turned = jnp.where(lane >= fine, low, high)
        for bit in range(7):
            step = 1 << bit
            turned = jnp.where((fine & step) != 0, pltpu.roll(turned, W - step, 1), turned)
        rows[pl.ds(s, RECV, stride=8), :] = turned * taper
    own_first = pl.multiple_of(wp * 16, 16)
    reach[pl.ds(own_first, 16)] = rows[...].reshape(16, 16, W).astype(bf16)

    @pl.when(z > 0)
    def _():
        pl.semaphore_wait(barrier, 12)

    @pl.when(z == 0)
    def _():
        pl.semaphore_wait(barrier, 8)

    def slot(plane, column, which):
        first = pl.multiple_of((plane * PLANE + column * 2 + which) * 16, 16)
        return reach.at[pl.ds(first, 16)]

    mine = slot(0, x, core)
    x_copies = []
    for i, column in enumerate(x_peers):
        copy = pltpu.make_async_remote_copy(
            src_ref=mine, dst_ref=mine, send_sem=x_send.at[i], recv_sem=x_recv.at[i],
            device_id=(well_at(z, column, core), shot), device_id_type=MESH,
        )
        copy.start()
        x_copies.append(copy)

    def z_copy(i):
        return pltpu.make_async_remote_copy(
            src_ref=mine, dst_ref=slot(1, x, core), send_sem=z_send.at[i], recv_sem=z_recv.at[i],
            device_id=(well_at(jnp.maximum(z - 1, 0), (x + i) % 4, core), shot), device_id_type=MESH,
        )

    @pl.when(z > 0)
    def _():
        for i in range(4):
            z_copy(i).start()

    def c_copy(plane, column, i):
        block = slot(plane, column, core)
        return pltpu.make_async_remote_copy(
            src_ref=block, dst_ref=block, send_sem=c_send.at[i], recv_sem=c_recv.at[i],
            device_id=other_core, device_id_type=MESH,
        )

    c_copies = [c_copy(0, x, 0)]
    c_copies[0].start()

    load_ahead.wait()
    load_off.wait()
    all_gates = gates[...]
    halves = jnp.concatenate([all_gates >> 3, all_gates & 7], axis=0).astype(f32).astype(bf16)
    lanes = lax.broadcasted_iota(jnp.int32, (512, W), 1)
    index = lax.broadcasted_iota(jnp.int32, (512, W), 0)
    for h in (1, 0):
        own = wp * RECV + (zh + h) % 2 * SEC
        start = (own + off_ref[(zh + h) % 2]) // 2 * 2
        wanted = jnp.where(lanes < 32, start + lanes, own - 32 + lanes)
        one_hot = jnp.where(index == wanted, 1.0, 0.0).astype(bf16)
        block = jnp.dot(halves, one_hot, preferred_element_type=f32)
        chosen[h, SEC_BLOCKS - 1] = block.astype(bf16)
        chosen[h, SEC_REACH : SEC_REACH + SEC_OWN] = reach[pl.ds(own // 2, SEC_OWN)]

    def far_copy(first, last, i):
        return pltpu.make_async_remote_copy(
            src_ref=chosen.at[1, pl.ds(first, last - first)], dst_ref=far.at[pl.ds(first, last - first)],
            send_sem=far_send.at[i], recv_sem=far_recv.at[i], device_id=across, device_id_type=MESH,
        )

    far_early = far_copy(SEC_REACH, SEC_BLOCKS, 0)
    far_early.start()

    for i, d in enumerate((1, 3, 2)):
        x_copies[i].wait_recv()
        copy = c_copy(0, (x - d + 4) % 4, 1 + i)
        copy.start()
        c_copies.append(copy)

    @pl.when(z < 7)
    def _():
        for i in range(4):
            z_copy(i).wait_recv()
            c_copy(1, (x - i + 4) % 4, 4 + i).start()

    for i in range(4):
        c_copies[i].wait()

    @pl.when(z < 7)
    def _():
        for i in range(4):
            c_copy(1, (x - i + 4) % 4, 4 + i).wait()

    for h in (1, 0):
        first = wp * 16 + (zh + h) % 2 * 8 + off_ref[(zh + h) % 2] // 2
        chosen[h, :SEC_REACH] = reach[pl.ds(first, SEC_REACH)]
        if h == 1:
            far_late = far_copy(0, SEC_REACH, 1)
            far_late.start()

    def parts(source, from_shot, to_y):
        return [
            (source.at[pl.ds(2 * to_y, REACH_PAIRS)], out_hbm.at[from_shot, pl.ds(0, REACH_PAIRS)]),
            (source.at[pl.ds(SEC_REACH + 2 * to_y, OWN_PAIRS)], out_hbm.at[from_shot, pl.ds(REACH_PAIRS, OWN_PAIRS)]),
            (source.at[pl.ds(SEC_BLOCKS - 1, 1)], out_hbm.at[from_shot, pl.ds(BLOCKS - 1, 1)]),
        ]

    waiting = []

    def pass_on(source, from_shot, h, kinds):
        for i, peer in enumerate(y_peers):
            pieces = parts(source, from_shot, peer)
            for kind in kinds:
                n = (h * 3 + i) * 3 + kind
                copy = pltpu.make_async_remote_copy(
                    src_ref=pieces[kind][0], dst_ref=pieces[kind][1], send_sem=y_send.at[n], recv_sem=y_recv.at[n],
                    device_id=(well, zh * 4 + peer), device_id_type=MESH,
                )
                copy.start()
                waiting.append(copy)
        pieces = parts(source, from_shot, y)
        for kind in kinds:
            copy = pltpu.make_async_copy(pieces[kind][0], pieces[kind][1], keep_sem.at[h * 3 + kind])
            copy.start()
            waiting.append(copy)

    pass_on(chosen.at[0], shot, 0, (0, 1, 2))
    far_early.wait_recv()
    pass_on(far, far_shot, 1, (1, 2))
    far_late.wait_recv()
    pass_on(far, far_shot, 1, (0,))
    for copy in x_copies:
        copy.wait_send()

    @pl.when(z > 0)
    def _():
        for i in range(4):
            z_copy(i).wait_send()

    far_early.wait_send()
    far_late.wait_send()
    for copy in waiting:
        copy.wait()


def turn(angle):
    half = angle * math.pi
    sq = half * half
    sine = half * (1.0 + sq * (-1 / 6 + sq * (1 / 120 + sq * (-1 / 5040 + sq * (1 / 362880 - sq * (1 / 39916800))))))
    cosine = 1.0 + sq * (
        -0.5 + sq * (1 / 24 + sq * (-1 / 720 + sq * (1 / 40320 + sq * (-1 / 3628800 + sq * (1 / 479001600)))))
    )
    return 1.0 - 2.0 * sine * sine, 2.0 * sine * cosine


def fraction(value):
    return value - jnp.round(value)


def fold(parts):
    row = lax.broadcasted_iota(jnp.int32, (8, W), 0)
    while len(parts) > 1:
        half = len(parts) // 2
        upper = (row & half) == 0
        merged = []
        for i in range(half):
            first, second = parts[i], parts[i + half]
            kept = jnp.where(upper, first, second)
            moved = jnp.where(upper, second, first)
            if half == 4:
                moved = pltpu.roll(moved, 4, 0)
            else:
                moved = jnp.where(upper, pltpu.roll(moved, 8 - half, 0), pltpu.roll(moved, half, 0))
            merged.append(kept + moved)
        parts = merged
    return parts[0]


def cross_kernel(off_hbm, data, table, out, off_ref, flat, gate_vals, spectra, sem):
    z, wp, zh, y = place()
    load_off = pltpu.make_async_copy(off_hbm, off_ref, sem)
    load_off.start()
    lane = lax.broadcasted_iota(jnp.int32, (8, W), 1)
    lane_f = lane.astype(f32)

    for k in range(8):
        block = pltpu.roll(data[k, BLOCKS - 1].astype(f32), (W - 4 * y) % W, 1)
        gate = block[:8] * 8.0 + block[8:]
        step_cos, step_sin = turn(fraction(gate * 0.125))
        for slot in range(SLOTS):
            column = slot if slot < 20 else 12 + slot
            for i, value in enumerate((gate, step_cos, step_sin)):
                gate_vals[slot, k, i] = jnp.broadcast_to(value[:, column : column + 1], (8, W))

    @pl.loop(0, SLOTS // 2)
    def _(p):
        left = data[:, p].reshape(8 * 16, W)
        flat[...] = jnp.dot(left, table[...], preferred_element_type=f32)
        for par in range(2):
            slot = 2 * p + par
            for k in range(8):
                first = k * 16 + par * 8
                gate = gate_vals[slot, k, 0]
                step_cos = gate_vals[slot, k, 1]
                step_sin = gate_vals[slot, k, 2]
                cosine, sine = turn(fraction(gate * (lane_f * (1.0 / NT))))
                for t in range(4):
                    real = flat[first : first + 8, t * W : (t + 1) * W]
                    imag = flat[first : first + 8, (4 + t) * W : (5 + t) * W]
                    if t == 0:
                        alternating = 1.0 - 2.0 * jnp.abs(gate - 2.0 * jnp.floor(gate * 0.5))
                        imag_cos = jnp.where(lane == 0, alternating, cosine)
                    else:
                        imag_cos = cosine
                    new_real = cosine * real + sine * imag
                    new_imag = imag_cos * imag - sine * real
                    rows = slice(k * 8, k * 8 + 8)
                    spectra[slot, t, 0, rows, :] = new_real.astype(bf16).astype(f32)
                    spectra[slot, t, 1, rows, :] = new_imag.astype(bf16).astype(f32)
                    if t < 3:
                        cosine, sine = (
                            cosine * step_cos - sine * step_sin,
                            sine * step_cos + cosine * step_sin,
                        )

    load_off.wait()
    odd = off_ref[zh] & 1

    @pl.loop(0, 4)
    def _(a):
        imags = []
        for t in range(4):
            own = [(spectra[20 + a, t, 0, k * 8 : k * 8 + 8, :], spectra[20 + a, t, 1, k * 8 : k * 8 + 8, :]) for k in range(8)]
            for group in range(2):
                sums = []
                for j in range(8):
                    slot = a + odd + group * 8 + j
                    one = two = three = None
                    for k in range(8):
                        re = spectra[slot, t, 0, k * 8 : k * 8 + 8, :]
                        im = spectra[slot, t, 1, k * 8 : k * 8 + 8, :]
                        first = own[k][0] * re
                        second = own[k][1] * im
                        third = own[k][0] * im - own[k][1] * re
                        one = first if one is None else one + first
                        two = second if two is None else two + second
                        three = third if three is None else three + third
                    sums.append((one, two, three))
                rows = pl.ds(group * 8, 8)
                if t == 0:
                    ones = fold([s[0] for s in sums])
                    twos = fold([s[1] for s in sums])
                    threes = fold([s[2] for s in sums])
                    out[a, rows, :W] = jnp.where(lane == 0, ones, ones + twos)
                    imags.append((twos, jnp.where(lane == 0, 0.0, threes)))
                else:
                    out[a, rows, t * W : (t + 1) * W] = fold([s[0] + s[1] for s in sums])
                    threes = fold([s[2] for s in sums])
                    imags.append((None, threes))
        for group in range(2):
            rows = pl.ds(group * 8, 8)
            before = imags[group][0]
            for t in range(4):
                turned = pltpu.roll(imags[2 * t + group][1], 1, 1)
                out[a, rows, (4 + t) * W : (5 + t) * W] = jnp.where(lane == 0, before, turned)
                before = turned
            out[a, rows, 8 * W : 8 * W + 2] = jnp.where(lane == 0, before, 0.0)[:, :2]


def local(traces, gate_starts, section_offsets):
    any_space = pl.BlockSpec(memory_space=pl.ANY)
    vmem = pl.BlockSpec(memory_space=pltpu.VMEM)
    dma = pltpu.SemaphoreType.DMA
    arrived = pl.pallas_call(
        gather_kernel,
        out_shape=jax.ShapeDtypeStruct((8, BLOCKS, 16, W), bf16),
        in_specs=[any_space, any_space, any_space],
        out_specs=any_space,
        scratch_shapes=[
            pltpu.SMEM((2,), jnp.int32),
            pltpu.VMEM((8, RECV, NT), bf16),
            pltpu.VMEM((8, 512), jnp.int32),
            pltpu.VMEM((256, 8), f32),
            pltpu.VMEM((RECV * 8, W), f32),
            pltpu.VMEM((256, 16, W), bf16),
            pltpu.VMEM((2, SEC_BLOCKS, 16, W), bf16),
            pltpu.VMEM((SEC_BLOCKS, 16, W), bf16),
            dma((3,)), dma((8,)), dma((3,)), dma((3,)), dma((4,)), dma((4,)), dma((8,)), dma((8,)),
            dma((2,)), dma((2,)), dma((18,)), dma((18,)), dma((6,)),
        ],
        compiler_params=pltpu.CompilerParams(
            collective_id=0, has_side_effects=True, vmem_limit_bytes=60 * 2**20
        ),
        name="gather",
    )(section_offsets, traces, gate_starts)
    return pl.pallas_call(
        cross_kernel,
        out_shape=jax.ShapeDtypeStruct((4, PARTNERS, NT + 2), f32),
        in_specs=[any_space, vmem, vmem],
        out_specs=vmem,
        scratch_shapes=[
            pltpu.SMEM((2,), jnp.int32),
            pltpu.VMEM((128, NT), f32),
            pltpu.VMEM((SLOTS, 8, 3, 8, W), f32),
            pltpu.VMEM((SLOTS, 4, 2, 64, W), f32),
            dma,
        ],
        compiler_params=pltpu.CompilerParams(vmem_limit_bytes=32 * 2**20),
        name="cross",
    )(section_offsets, arrived, jnp.asarray(packed_table()))


def solution(mesh):
    in_specs = (P("shot", "well", None), P("shot", None), P("well"))
    out_specs = P(("well", "shot"), None, None)
    return jax.shard_map(local, mesh=mesh, in_specs=in_specs, out_specs=out_specs, check_vma=False)
```

```python
import functools
import math

import jax
import jax.numpy as jnp
import ml_dtypes
import numpy as np
from jax import lax
from jax.experimental import pallas as pl
from jax.experimental.pallas import tpu as pltpu
from jax.sharding import PartitionSpec as P

NT = 1024
W = 128
SEC = 16
PARTNERS = 16
PLANE = 8
RECV = 32
OWN_PAIRS = 2
REACH_PAIRS = 10
BLOCKS = REACH_PAIRS + OWN_PAIRS + 1
SEC_REACH = 16
SEC_OWN = 8
CLASSES = 8
SLOTS = 2 * (REACH_PAIRS + OWN_PAIRS)
MESH = pl.DeviceIdType.MESH
f32 = jnp.float32
bf16 = jnp.bfloat16

def packed_table():
    steps = np.arange(W)
    k = np.arange(NT // 2)
    angle = ((steps[:, None] * k[None, :]) % NT).astype(np.float32) * np.float32(2 * math.pi / NT)
    real = np.cos(angle)
    imag = -np.sin(angle)
    imag[:, 0] = np.cos(math.pi * steps)
    scale = np.float32(1.0 / math.sqrt(W))
    return (np.concatenate([real, imag], axis=1) * scale).astype(ml_dtypes.bfloat16)


def place():
    well = lax.axis_index("well")
    shot = lax.axis_index("shot")
    return well // PLANE, well % PLANE, shot // 4, shot % 4


def gather_kernel(
    off_hbm, traces_hbm, gates_hbm, out_hbm,
    offs, traces, gates, gate_cols, rows, unit, dealt, held, picked, landed, far_landed, ordered, extra, far_extra,
    load_sem, o_send, o_recv, a_send, a_recv, z_send, z_recv, n_send, n_recv,
    f_send, f_recv, e_send, e_recv, y_send, y_recv, keep_sem,
):
    z, wp, zh, y = place()
    x, core = wp // 2, wp % 2
    well = z * PLANE + wp
    shot = zh * 4 + y
    far_shot = (1 - zh) * 4 + y
    before = jnp.maximum(z - 1, 0)

    steps = [(dx, dc) for dx in (0, 1, 3, 2) for dc in (0, 1)]
    near = [(x + dx) % 4 * 2 + (core + dc) % 2 for dx, dc in steps]
    y_peers = [(y + d) % 4 for d in (1, 3, 2)]

    barrier = pltpu.get_barrier_semaphore()

    def greet(to_well, to_shot):
        pl.semaphore_signal(barrier, inc=1, device_id=(to_well, to_shot), device_id_type=MESH)

    for peer in near:
        greet(z * PLANE + peer, far_shot)

    @pl.when(z < 7)
    def _():
        for peer in near:
            greet((z + 1) * PLANE + peer, shot)

    for peer in near[1:]:
        greet(z * PLANE + peer, shot)
    for peer in y_peers:
        greet(well, zh * 4 + peer)

    here = pl.multiple_of(z * 256, 256)
    ahead = pl.multiple_of(jnp.minimum(z + 1, 7) * 256, 256)
    load_here = pltpu.make_async_copy(gates_hbm.at[:, pl.ds(here, 256)], gates.at[:, pl.ds(0, 256)], load_sem.at[0])
    load_ahead = pltpu.make_async_copy(gates_hbm.at[:, pl.ds(ahead, 256)], gates.at[:, pl.ds(256, 256)], load_sem.at[1])
    load_off = pltpu.make_async_copy(off_hbm, offs.at[wp], load_sem.at[2])
    load_here.start()
    load_traces = pltpu.make_async_copy(traces_hbm, traces, load_sem.at[3])
    load_traces.start()
    load_off.start()
    load_ahead.start()

    @pl.when(z == 7)
    def _():
        held[pl.ds(16, 16)] = jnp.zeros((16, 16, W), bf16)

    lane = lax.broadcasted_iota(jnp.int32, (RECV, W), 1)
    taper = 0.5 - 0.5 * jnp.cos((lane[:8].astype(f32) + 0.5) * (2 * math.pi / W))
    taper = jnp.concatenate([taper] * (RECV // 8), axis=0)
    load_here.wait()
    gate_cols[...] = jnp.transpose(gates[:, :256].astype(f32))
    columns = gate_cols[pl.ds(pl.multiple_of(wp * RECV, RECV), RECV), :].astype(jnp.int32)
    load_traces.wait()
    for s in range(8):
        data = traces[s].astype(f32)
        gate = jnp.broadcast_to(columns[:, s : s + 1], (RECV, W))
        fine = gate & 127
        tiles = [data[:, k * W : (k + 1) * W] for k in range(8)]
        pick = (gate & 512) != 0
        four = [jnp.where(pick, tiles[k + 4], tiles[k]) for k in range(4)] + [tiles[4]]
        pick = (gate & 256) != 0
        three = [jnp.where(pick, four[k + 2], four[k]) for k in range(3)]
        pick = (gate & 128) != 0
        low = jnp.where(pick, three[1], three[0])
        high = jnp.where(pick, three[2], three[1])
        turned = jnp.where(lane >= fine, low, high)
        for bit in range(7):
            step = 1 << bit
            turned = jnp.where((fine & step) != 0, pltpu.roll(turned, W - step, 1), turned)
        rows[pl.ds(s, RECV, stride=8), :] = turned * taper
    pairs = rows[...].reshape(16, 16, W).astype(bf16)
    unit[...] = pairs
    for i in range(2):
        for m in range(CLASSES):
            dealt[m, i] = pairs[i * CLASSES + m]

    @pl.when(z > 0)
    def _():
        pl.semaphore_wait(barrier, 26)

    @pl.when(z == 0)
    def _():
        pl.semaphore_wait(barrier, 18)

    def remote(source, target, send, receive, to_well, to_shot):
        return pltpu.make_async_remote_copy(
            src_ref=source, dst_ref=target, send_sem=send, recv_sem=receive,
            device_id=(to_well, to_shot), device_id_type=MESH,
        )

    mine = pl.ds(wp * 2, 2)
    mine_ahead = pl.ds(16 + wp * 2, 2)

    def z_copy(k):
        return remote(
            dealt.at[near[k]], held.at[mine_ahead], z_send.at[k], z_recv.at[k], before * PLANE + near[k], shot
        )

    @pl.when(z > 0)
    def _():
        for k in range(8):
            z_copy(k).start()

    a_copies = []
    o_copies = []
    for k in range(1, 8):
        to_well = z * PLANE + near[k]
        copy = remote(dealt.at[near[k]], held.at[mine], a_send.at[k], a_recv.at[k], to_well, shot)
        copy.start()
        a_copies.append(copy)
    load_off.wait()
    for k in range(1, 8):
        copy = remote(offs.at[wp], offs.at[wp], o_send.at[k], o_recv.at[k], z * PLANE + near[k], shot)
        copy.start()
        o_copies.append(copy)
    held[mine] = dealt[wp]

    load_ahead.wait()
    all_gates = gates[...]
    halves = jnp.concatenate([all_gates >> 3, all_gates & 7], axis=0).astype(f32).astype(bf16)
    lanes = lax.broadcasted_iota(jnp.int32, (512, W), 1)
    index = lax.broadcasted_iota(jnp.int32, (512, W), 0)
    for h in (1, 0):
        section = (zh + h) % 2
        own = wp * RECV + section * SEC
        start = (own + offs[wp, section]) // 2 * 2
        wanted = jnp.where(lanes < 32, start + lanes, own - 32 + lanes)
        one_hot = jnp.where(index == wanted, 1.0, 0.0).astype(bf16)
        block = jnp.dot(halves, one_hot, preferred_element_type=f32)
        extra[h, :SEC_OWN] = unit[pl.ds(section * SEC_OWN, SEC_OWN)]
        extra[h, SEC_OWN] = block.astype(bf16)

    e_copy = remote(extra.at[1], far_extra, e_send, e_recv, well, far_shot)
    e_copy.start()
    for copy in o_copies:
        copy.wait_recv()
    for copy in a_copies:
        copy.wait_recv()

    @pl.when(z < 7)
    def _():
        for k in range(8):
            z_copy(k).wait_recv()

    for h in (1, 0):
        section = (zh + h) % 2
        for k in range(8):
            first = near[k] * 16 + section * SEC_OWN + offs[near[k], section] // 2
            at = (first + (wp + 512 - first) % CLASSES) // CLASSES
            picked[h, k] = held[pl.ds(at, 2)]
    f_copies = []
    n_copies = []
    for k in range(8):
        to_well = z * PLANE + near[k]
        copy = remote(picked.at[1, k], far_landed.at[wp], f_send.at[k], f_recv.at[k], to_well, far_shot)
        copy.start()
        f_copies.append(copy)
    for k in range(1, 8):
        to_well = z * PLANE + near[k]
        copy = remote(picked.at[0, k], landed.at[wp], n_send.at[k], n_recv.at[k], to_well, shot)
        copy.start()
        n_copies.append(copy)
    landed[wp] = picked[0, 0]

    own_first = wp * 16 + zh * SEC_OWN + offs[wp, zh] // 2
    waiting = []

    def pass_on(h, kinds):
        from_shot = (far_shot if h else shot)
        more = far_extra if h else extra.at[0]

        def pieces(to_y):
            return [
                (ordered.at[h, pl.ds(2 * to_y, REACH_PAIRS)], out_hbm.at[from_shot, pl.ds(0, REACH_PAIRS)]),
                (more.at[pl.ds(2 * to_y, OWN_PAIRS)], out_hbm.at[from_shot, pl.ds(REACH_PAIRS, OWN_PAIRS)]),
                (more.at[pl.ds(SEC_OWN, 1)], out_hbm.at[from_shot, pl.ds(BLOCKS - 1, 1)]),
            ]

        for i, peer in enumerate(y_peers):
            for kind in kinds:
                n = (h * 3 + i) * 3 + kind
                source, target = pieces(peer)[kind]
                copy = remote(source, target, y_send.at[n], y_recv.at[n], well, zh * 4 + peer)
                copy.start()
                waiting.append(copy)
        for kind in kinds:
            source, target = pieces(y)[kind]
            copy = pltpu.make_async_copy(source, target, keep_sem.at[h * 3 + kind])
            copy.start()
            waiting.append(copy)

    def put_in_order(h, arrived):
        for i in range(SEC_REACH):
            ordered[h, i] = arrived[(own_first + i) % CLASSES, i // CLASSES]

    pass_on(0, (1, 2))
    for copy in n_copies:
        copy.wait_recv()
    put_in_order(0, landed)
    pass_on(0, (0,))
    e_copy.wait_recv()
    pass_on(1, (1, 2))
    for copy in f_copies:
        copy.wait_recv()
    put_in_order(1, far_landed)
    pass_on(1, (0,))

    @pl.when(z > 0)
    def _():
        for k in range(8):
            z_copy(k).wait_send()

    for copy in a_copies + o_copies + n_copies + f_copies + [e_copy]:
        copy.wait_send()
    for copy in waiting:
        copy.wait()


def turn(angle):
    half = angle * math.pi
    sq = half * half
    sine = half * (1.0 + sq * (-1 / 6 + sq * (1 / 120 + sq * (-1 / 5040 + sq * (1 / 362880 - sq * (1 / 39916800))))))
    cosine = 1.0 + sq * (
        -0.5 + sq * (1 / 24 + sq * (-1 / 720 + sq * (1 / 40320 + sq * (-1 / 3628800 + sq * (1 / 479001600)))))
    )
    return 1.0 - 2.0 * sine * sine, 2.0 * sine * cosine


def fraction(value):
    return value - jnp.round(value)


def fold(parts):
    row = lax.broadcasted_iota(jnp.int32, (8, W), 0)
    while len(parts) > 1:
        half = len(parts) // 2
        upper = (row & half) == 0
        merged = []
        for i in range(half):
            first, second = parts[i], parts[i + half]
            kept = jnp.where(upper, first, second)
            moved = jnp.where(upper, second, first)
            if half == 4:
                moved = pltpu.roll(moved, 4, 0)
            else:
                moved = jnp.where(upper, pltpu.roll(moved, 8 - half, 0), pltpu.roll(moved, half, 0))
            merged.append(kept + moved)
        parts = merged
    return parts[0]


def cross_kernel(off_hbm, data, table, out, off_ref, flat, gate_vals, spectra, sem):
    z, wp, zh, y = place()
    load_off = pltpu.make_async_copy(off_hbm, off_ref, sem)
    load_off.start()
    lane = lax.broadcasted_iota(jnp.int32, (8, W), 1)
    lane_f = lane.astype(f32)

    for k in range(8):
        block = pltpu.roll(data[k, BLOCKS - 1].astype(f32), (W - 4 * y) % W, 1)
        gate = block[:8] * 8.0 + block[8:]
        step_cos, step_sin = turn(fraction(gate * 0.125))
        for slot in range(SLOTS):
            column = slot if slot < 20 else 12 + slot
            for i, value in enumerate((gate, step_cos, step_sin)):
                gate_vals[slot, k, i] = jnp.broadcast_to(value[:, column : column + 1], (8, W))

    @pl.loop(0, SLOTS // 2)
    def _(p):
        left = data[:, p].reshape(8 * 16, W)
        flat[...] = jnp.dot(left, table[...], preferred_element_type=f32)
        for par in range(2):
            slot = 2 * p + par
            for k in range(8):
                first = k * 16 + par * 8
                gate = gate_vals[slot, k, 0]
                step_cos = gate_vals[slot, k, 1]
                step_sin = gate_vals[slot, k, 2]
                cosine, sine = turn(fraction(gate * (lane_f * (1.0 / NT))))
                for t in range(4):
                    real = flat[first : first + 8, t * W : (t + 1) * W]
                    imag = flat[first : first + 8, (4 + t) * W : (5 + t) * W]
                    if t == 0:
                        alternating = 1.0 - 2.0 * jnp.abs(gate - 2.0 * jnp.floor(gate * 0.5))
                        imag_cos = jnp.where(lane == 0, alternating, cosine)
                    else:
                        imag_cos = cosine
                    new_real = cosine * real + sine * imag
                    new_imag = imag_cos * imag - sine * real
                    rows = slice(k * 8, k * 8 + 8)
                    spectra[slot, t, 0, rows, :] = new_real.astype(bf16).astype(f32)
                    spectra[slot, t, 1, rows, :] = new_imag.astype(bf16).astype(f32)
                    if t < 3:
                        cosine, sine = (
                            cosine * step_cos - sine * step_sin,
                            sine * step_cos + cosine * step_sin,
                        )

    load_off.wait()
    odd = off_ref[zh] & 1

    @pl.loop(0, 4)
    def _(a):
        imags = []
        for t in range(4):
            own = [(spectra[20 + a, t, 0, k * 8 : k * 8 + 8, :], spectra[20 + a, t, 1, k * 8 : k * 8 + 8, :]) for k in range(8)]
            for group in range(2):
                sums = []
                for j in range(8):
                    slot = a + odd + group * 8 + j
                    one = two = three = None
                    for k in range(8):
                        re = spectra[slot, t, 0, k * 8 : k * 8 + 8, :]
                        im = spectra[slot, t, 1, k * 8 : k * 8 + 8, :]
                        first = own[k][0] * re
                        second = own[k][1] * im
                        third = own[k][0] * im - own[k][1] * re
                        one = first if one is None else one + first
                        two = second if two is None else two + second
                        three = third if three is None else three + third
                    sums.append((one, two, three))
                rows = pl.ds(group * 8, 8)
                if t == 0:
                    ones = fold([s[0] for s in sums])
                    twos = fold([s[1] for s in sums])
                    threes = fold([s[2] for s in sums])
                    out[a, rows, :W] = jnp.where(lane == 0, ones, ones + twos)
                    imags.append((twos, jnp.where(lane == 0, 0.0, threes)))
                else:
                    out[a, rows, t * W : (t + 1) * W] = fold([s[0] + s[1] for s in sums])
                    threes = fold([s[2] for s in sums])
                    imags.append((None, threes))
        for group in range(2):
            rows = pl.ds(group * 8, 8)
            before = imags[group][0]
            for t in range(4):
                turned = pltpu.roll(imags[2 * t + group][1], 1, 1)
                out[a, rows, (4 + t) * W : (5 + t) * W] = jnp.where(lane == 0, before, turned)
                before = turned
            out[a, rows, 8 * W : 8 * W + 2] = jnp.where(lane == 0, before, 0.0)[:, :2]


def local(traces, gate_starts, section_offsets):
    any_space = pl.BlockSpec(memory_space=pl.ANY)
    vmem = pl.BlockSpec(memory_space=pltpu.VMEM)
    dma = pltpu.SemaphoreType.DMA
    arrived = pl.pallas_call(
        gather_kernel,
        out_shape=jax.ShapeDtypeStruct((8, BLOCKS, 16, W), bf16),
        in_specs=[any_space, any_space, any_space],
        out_specs=any_space,
        scratch_shapes=[
            pltpu.SMEM((PLANE, 2), jnp.int32),
            pltpu.VMEM((8, RECV, NT), bf16),
            pltpu.VMEM((8, 512), jnp.int32),
            pltpu.VMEM((256, 8), f32),
            pltpu.VMEM((RECV * 8, W), f32),
            pltpu.VMEM((16, 16, W), bf16),
            pltpu.VMEM((CLASSES, 2, 16, W), bf16),
            pltpu.VMEM((32, 16, W), bf16),
            pltpu.VMEM((2, PLANE, 2, 16, W), bf16),
            pltpu.VMEM((CLASSES, 2, 16, W), bf16),
            pltpu.VMEM((CLASSES, 2, 16, W), bf16),
            pltpu.VMEM((2, SEC_REACH, 16, W), bf16),
            pltpu.VMEM((2, SEC_OWN + 1, 16, W), bf16),
            pltpu.VMEM((SEC_OWN + 1, 16, W), bf16),
            dma((4,)), dma((8,)), dma((8,)), dma((8,)), dma((8,)), dma((8,)), dma((8,)),
            dma((8,)), dma((8,)), dma((8,)), dma((8,)), dma, dma, dma((18,)), dma((18,)), dma((6,)),
        ],
        compiler_params=pltpu.CompilerParams(
            collective_id=0, has_side_effects=True, vmem_limit_bytes=60 * 2**20
        ),
        name="gather",
    )(section_offsets, traces, gate_starts)
    return pl.pallas_call(
        cross_kernel,
        out_shape=jax.ShapeDtypeStruct((4, PARTNERS, NT + 2), f32),
        in_specs=[any_space, vmem, vmem],
        out_specs=vmem,
        scratch_shapes=[
            pltpu.SMEM((2,), jnp.int32),
            pltpu.VMEM((128, NT), f32),
            pltpu.VMEM((SLOTS, 8, 3, 8, W), f32),
            pltpu.VMEM((SLOTS, 4, 2, 64, W), f32),
            dma,
        ],
        compiler_params=pltpu.CompilerParams(vmem_limit_bytes=32 * 2**20),
        name="cross",
    )(section_offsets, arrived, jnp.asarray(packed_table()))


def solution(mesh):
    in_specs = (P("shot", "well", None), P("shot", None), P("well"))
    out_specs = P(("well", "shot"), None, None)
    return jax.shard_map(local, mesh=mesh, in_specs=in_specs, out_specs=out_specs, check_vma=False)
```

```python
import functools
import math

import jax
import jax.numpy as jnp
import ml_dtypes
import numpy as np
from jax import lax
from jax.experimental import pallas as pl
from jax.experimental.pallas import tpu as pltpu
from jax.sharding import PartitionSpec as P

NT = 1024
W = 128
SEC = 16
PARTNERS = 16
PLANE = 8
RECV = 32
OWN_PAIRS = 2
REACH_PAIRS = 10
BLOCKS = REACH_PAIRS + OWN_PAIRS + 1
SEC_REACH = 16
SEC_OWN = 8
CLASSES = 8
SLOTS = 2 * (REACH_PAIRS + OWN_PAIRS)
MESH = pl.DeviceIdType.MESH
f32 = jnp.float32
bf16 = jnp.bfloat16

def packed_table():
    steps = np.arange(2 * W)
    k = np.arange(NT // 2)
    angle = ((steps[:, None] * k[None, :]) % NT).astype(np.float32) * np.float32(2 * math.pi / NT)
    real = np.cos(angle)
    imag = -np.sin(angle)
    imag[:, 0] = np.cos(math.pi * steps)
    scale = np.float32(1.0 / math.sqrt(W))
    return (np.concatenate([real, imag], axis=1) * scale).astype(ml_dtypes.bfloat16)


def place():
    well = lax.axis_index("well")
    shot = lax.axis_index("shot")
    return well // PLANE, well % PLANE, shot // 4, shot % 4


def gather_kernel(
    off_hbm, traces_hbm, gates_hbm, table_hbm, far_hbm, part_hbm,
    near_in, table, gate_vals, spectra, part,
    offs, traces, gates, gate_cols, rows, unit, dealt, held, picked, landed, far_landed, ordered, extra, far_extra,
    load_sem, o_send, o_recv, a_send, a_recv, z_send, z_recv, n_send, n_recv,
    f_send, f_recv, e_send, e_recv, y_send, y_recv, keep_sem,
):
    z, wp, zh, y = place()
    x, core = wp // 2, wp % 2
    well = z * PLANE + wp
    shot = zh * 4 + y
    far_shot = (1 - zh) * 4 + y
    before = jnp.maximum(z - 1, 0)

    steps = [(dx, dc) for dx in (0, 1, 3, 2) for dc in (0, 1)]
    near = [(x + dx) % 4 * 2 + (core + dc) % 2 for dx, dc in steps]
    y_peers = [(y + d) % 4 for d in (1, 3, 2)]

    barrier = pltpu.get_barrier_semaphore()

    def greet(to_well, to_shot):
        pl.semaphore_signal(barrier, inc=1, device_id=(to_well, to_shot), device_id_type=MESH)

    for peer in near:
        greet(z * PLANE + peer, far_shot)

    @pl.when(z < 7)
    def _():
        for peer in near:
            greet((z + 1) * PLANE + peer, shot)

    for peer in near[1:]:
        greet(z * PLANE + peer, shot)
    for peer in y_peers:
        greet(well, zh * 4 + peer)

    here = pl.multiple_of(z * 256, 256)
    ahead = pl.multiple_of(jnp.minimum(z + 1, 7) * 256, 256)
    load_here = pltpu.make_async_copy(gates_hbm.at[:, pl.ds(here, 256)], gates.at[:, pl.ds(0, 256)], load_sem.at[0])
    load_ahead = pltpu.make_async_copy(gates_hbm.at[:, pl.ds(ahead, 256)], gates.at[:, pl.ds(256, 256)], load_sem.at[1])
    load_off = pltpu.make_async_copy(off_hbm, offs.at[wp], load_sem.at[2])
    load_here.start()
    load_traces = pltpu.make_async_copy(traces_hbm, traces, load_sem.at[3])
    load_traces.start()
    load_off.start()
    load_ahead.start()
    load_table = pltpu.make_async_copy(table_hbm, table, load_sem.at[4])
    load_table.start()

    @pl.when(z == 7)
    def _():
        held[pl.ds(16, 16)] = jnp.zeros((16, 16, W), bf16)

    lane = lax.broadcasted_iota(jnp.int32, (RECV, W), 1)
    taper = 0.5 - 0.5 * jnp.cos((lane[:8].astype(f32) + 0.5) * (2 * math.pi / W))
    taper = jnp.concatenate([taper] * (RECV // 8), axis=0)
    load_here.wait()
    gate_cols[...] = jnp.transpose(gates[:, :256].astype(f32))
    columns = gate_cols[pl.ds(pl.multiple_of(wp * RECV, RECV), RECV), :].astype(jnp.int32)
    load_traces.wait()
    for s in range(8):
        data = traces[s].astype(f32)
        gate = jnp.broadcast_to(columns[:, s : s + 1], (RECV, W))
        fine = gate & 127
        tiles = [data[:, k * W : (k + 1) * W] for k in range(8)]
        pick = (gate & 512) != 0
        four = [jnp.where(pick, tiles[k + 4], tiles[k]) for k in range(4)] + [tiles[4]]
        pick = (gate & 256) != 0
        three = [jnp.where(pick, four[k + 2], four[k]) for k in range(3)]
        pick = (gate & 128) != 0
        low = jnp.where(pick, three[1], three[0])
        high = jnp.where(pick, three[2], three[1])
        turned = jnp.where(lane >= fine, low, high)
        for bit in range(3, 7):
            step = 1 << bit
            turned = jnp.where((fine & step) != 0, pltpu.roll(turned, W - step, 1), turned)
        rows[pl.ds(s, RECV, stride=8), :] = turned * jnp.take_along_axis(taper, (lane - (gate & 7)) & 127, axis=1)
    pairs = rows[...].reshape(16, 16, W).astype(bf16)
    unit[...] = pairs
    for i in range(2):
        for m in range(CLASSES):
            dealt[m, i] = pairs[i * CLASSES + m]

    @pl.when(z > 0)
    def _():
        pl.semaphore_wait(barrier, 26)

    @pl.when(z == 0)
    def _():
        pl.semaphore_wait(barrier, 18)

    def remote(source, target, send, receive, to_well, to_shot):
        return pltpu.make_async_remote_copy(
            src_ref=source, dst_ref=target, send_sem=send, recv_sem=receive,
            device_id=(to_well, to_shot), device_id_type=MESH,
        )

    mine = pl.ds(wp * 2, 2)
    mine_ahead = pl.ds(16 + wp * 2, 2)

    def z_copy(k):
        return remote(
            dealt.at[near[k]], held.at[mine_ahead], z_send.at[k], z_recv.at[k], before * PLANE + near[k], shot
        )

    @pl.when(z > 0)
    def _():
        for k in range(8):
            z_copy(k).start()

    a_copies = []
    o_copies = []
    for k in range(1, 8):
        to_well = z * PLANE + near[k]
        copy = remote(dealt.at[near[k]], held.at[mine], a_send.at[k], a_recv.at[k], to_well, shot)
        copy.start()
        a_copies.append(copy)
    load_off.wait()
    for k in range(1, 8):
        copy = remote(offs.at[wp], offs.at[wp], o_send.at[k], o_recv.at[k], z * PLANE + near[k], shot)
        copy.start()
        o_copies.append(copy)
    held[mine] = dealt[wp]

    load_ahead.wait()
    all_gates = gates[...]
    halves = jnp.concatenate([all_gates >> 3, all_gates & 7], axis=0).astype(f32).astype(bf16)
    lanes = lax.broadcasted_iota(jnp.int32, (512, W), 1)
    index = lax.broadcasted_iota(jnp.int32, (512, W), 0)
    for h in (1, 0):
        section = (zh + h) % 2
        own = wp * RECV + section * SEC
        start = (own + offs[wp, section]) // 2 * 2
        wanted = jnp.where(lanes < 32, start + lanes, own - 32 + lanes)
        one_hot = jnp.where(index == wanted, 1.0, 0.0).astype(bf16)
        block = jnp.dot(halves, one_hot, preferred_element_type=f32)
        extra[h, :SEC_OWN] = unit[pl.ds(section * SEC_OWN, SEC_OWN)]
        extra[h, SEC_OWN] = block.astype(bf16)

    e_copy = remote(extra.at[1], far_extra, e_send, e_recv, well, far_shot)
    e_copy.start()
    for copy in o_copies:
        copy.wait_recv()
    for copy in a_copies:
        copy.wait_recv()

    @pl.when(z < 7)
    def _():
        for k in range(8):
            z_copy(k).wait_recv()

    for h in (1, 0):
        section = (zh + h) % 2
        for k in range(8):
            first = near[k] * 16 + section * SEC_OWN + offs[near[k], section] // 2
            at = (first + (wp + 512 - first) % CLASSES) // CLASSES
            picked[h, k] = held[pl.ds(at, 2)]
    f_copies = []
    n_copies = []
    for k in range(8):
        to_well = z * PLANE + near[k]
        copy = remote(picked.at[1, k], far_landed.at[wp], f_send.at[k], f_recv.at[k], to_well, far_shot)
        copy.start()
        f_copies.append(copy)
    for k in range(1, 8):
        to_well = z * PLANE + near[k]
        copy = remote(picked.at[0, k], landed.at[wp], n_send.at[k], n_recv.at[k], to_well, shot)
        copy.start()
        n_copies.append(copy)
    landed[wp] = picked[0, 0]

    own_first = wp * 16 + zh * SEC_OWN + offs[wp, zh] // 2

    def pass_on(h, kinds):
        target = (far_hbm if h else near_in).at[y]
        more = far_extra if h else extra.at[0]

        def pieces(to_y):
            return [
                (ordered.at[h, pl.ds(2 * to_y, REACH_PAIRS)], target.at[pl.ds(0, REACH_PAIRS)]),
                (more.at[pl.ds(2 * to_y, OWN_PAIRS)], target.at[pl.ds(REACH_PAIRS, OWN_PAIRS)]),
                (more.at[pl.ds(SEC_OWN, 1)], target.at[pl.ds(BLOCKS - 1, 1)]),
            ]

        copies = []
        for i, peer in enumerate(y_peers):
            for kind in kinds:
                n = (h * 3 + i) * 3 + kind
                source, to = pieces(peer)[kind]
                copies.append(remote(source, to, y_send.at[n], y_recv.at[n], well, zh * 4 + peer))
        for kind in kinds:
            source, to = pieces(y)[kind]
            copies.append(pltpu.make_async_copy(source, to, keep_sem.at[h * 3 + kind]))
        for copy in copies:
            copy.start()
        return copies

    def put_in_order(h, arrived):
        for i in range(SEC_REACH):
            ordered[h, i] = arrived[(own_first + i) % CLASSES, i // CLASSES]

    near_copies = pass_on(0, (1, 2))
    for copy in n_copies:
        copy.wait_recv()
    put_in_order(0, landed)
    near_copies += pass_on(0, (0,))
    e_copy.wait_recv()
    far_copies = pass_on(1, (1, 2))
    for copy in f_copies:
        copy.wait_recv()
    put_in_order(1, far_landed)
    far_copies += pass_on(1, (0,))

    for copy in near_copies:
        copy.wait()
    load_table.wait()
    make_spectra(near_in, table, gate_vals, spectra, y)

    def keep(a, group, reals, imags):
        rows = pl.ds(group * 8, 8)
        for t in range(4):
            part[a, t, rows] = reals[t]
        for t in range(5):
            part[a, 4 + t, rows] = imags[t]

    pair_sums(spectra, offs[wp, zh] % 2, keep)
    keep_part = pltpu.make_async_copy(part, part_hbm, load_sem.at[5])
    keep_part.start()
    keep_part.wait()

    @pl.when(z > 0)
    def _():
        for k in range(8):
            z_copy(k).wait_send()

    for copy in a_copies + o_copies + n_copies + f_copies + [e_copy]:
        copy.wait_send()
    for copy in far_copies:
        copy.wait()


def fold(parts):
    row = lax.broadcasted_iota(jnp.int32, (8, W), 0)
    while len(parts) > 1:
        half = len(parts) // 2
        upper = (row & half) == 0
        merged = []
        for i in range(half):
            first, second = parts[i], parts[i + half]
            kept = jnp.where(upper, first, second)
            moved = jnp.where(upper, second, first)
            if half == 4:
                moved = pltpu.roll(moved, 4, 0)
            else:
                moved = jnp.where(upper, pltpu.roll(moved, 8 - half, 0), pltpu.roll(moved, half, 0))
            merged.append(kept + moved)
        parts = merged
    return parts[0]


def make_spectra(data, table, gate_vals, spectra, y):
    lane = lax.broadcasted_iota(jnp.int32, (8, W), 1)
    angle = lane.astype(f32) * (2 * math.pi / W)
    cosines = jnp.cos(angle)
    sines = jnp.sin(angle)

    for k in range(4):
        block = pltpu.roll(data[k, BLOCKS - 1].astype(f32), (W - 4 * y) % W, 1)
        gate = (block[:8] * 8.0 + block[8:]).astype(jnp.int32)
        for slot in range(SLOTS):
            column = slot if slot < 20 else 12 + slot
            gate_vals[slot, k] = jnp.broadcast_to(gate[:, column : column + 1], (8, W))

    @pl.loop(0, SLOTS // 4)
    def _(step):
        lefts = []
        for p in range(2):
            for k in range(4):
                both = data[k, 2 * step + p].astype(f32)
                halves = []
                for par in range(2):
                    window = both[par * 8 : par * 8 + 8]
                    low = jnp.where(lane >= (gate_vals[4 * step + 2 * p + par, k] & 7), window, 0.0)
                    halves.append(jnp.concatenate([low, window - low], axis=1))
                lefts.append(jnp.concatenate(halves, axis=0).astype(bf16))
        flat = jnp.dot(jnp.concatenate(lefts, axis=0), table[...], preferred_element_type=f32)
        for p in range(2):
            for par in range(2):
                slot = 4 * step + 2 * p + par
                for k in range(4):
                    first = p * 64 + k * 16 + par * 8
                    index = ((gate_vals[slot, k] >> 3) * lane) & 127
                    cosine = jnp.take_along_axis(cosines, index, axis=1)
                    sine = jnp.take_along_axis(sines, index, axis=1)
                    rows = slice(k * 8, k * 8 + 8)
                    for t in range(4):
                        real = flat[first : first + 8, t * W : (t + 1) * W]
                        imag = flat[first : first + 8, (4 + t) * W : (5 + t) * W]
                        spectra[slot, t, 0, rows, :] = cosine * real + sine * imag
                        spectra[slot, t, 1, rows, :] = cosine * imag - sine * real


def pair_sums(spectra, odd, emit):
    lane = lax.broadcasted_iota(jnp.int32, (8, W), 1)

    @pl.loop(0, 4)
    def _(a):
        reals = [[], []]
        imags = [[], []]
        for t in range(4):
            own = [[spectra[20 + a, t, c, k * 8 : k * 8 + 8, :] for c in range(2)] for k in range(4)]
            for group in range(2):
                sums = []
                for j in range(8):
                    slot = a + odd + group * 8 + j
                    one = two = three = None
                    for k in range(4):
                        re = spectra[slot, t, 0, k * 8 : k * 8 + 8, :]
                        im = spectra[slot, t, 1, k * 8 : k * 8 + 8, :]
                        first = own[k][0] * re
                        second = own[k][1] * im
                        third = own[k][0] * im - own[k][1] * re
                        one = first if one is None else one + first
                        two = second if two is None else two + second
                        three = third if three is None else three + third
                    sums.append((one, two, three))
                threes = fold([s[2] for s in sums])
                if t == 0:
                    ones = fold([s[0] for s in sums])
                    twos = fold([s[1] for s in sums])
                    reals[group].append(jnp.where(lane == 0, ones, ones + twos))
                    imags[group].append(twos)
                    imags[group].append(jnp.where(lane == 0, 0.0, threes))
                else:
                    reals[group].append(fold([s[0] + s[1] for s in sums]))
                    imags[group].append(threes)
        for group in range(2):
            emit(a, group, reals[group], imags[group])


def cross_kernel(off_hbm, data, part_hbm, table, out, off_ref, gate_vals, spectra, part, sem):
    z, wp, zh, y = place()
    load_off = pltpu.make_async_copy(off_hbm, off_ref, sem.at[0])
    load_off.start()
    load_part = pltpu.make_async_copy(part_hbm, part, sem.at[1])
    load_part.start()
    lane = lax.broadcasted_iota(jnp.int32, (8, W), 1)
    make_spectra(data, table, gate_vals, spectra, y)

    def finish(a, group, reals, imags):
        rows = pl.ds(group * 8, 8)
        for t in range(4):
            out[a, rows, t * W : (t + 1) * W] = reals[t] + part[a, t, rows]
        imags = [imags[t] + part[a, 4 + t, rows] for t in range(5)]
        before = imags[0]
        for t in range(4):
            turned = pltpu.roll(imags[1 + t], 1, 1)
            out[a, rows, (4 + t) * W : (5 + t) * W] = jnp.where(lane == 0, before, turned)
            before = turned
        out[a, rows, 8 * W : 8 * W + 2] = jnp.where(lane == 0, before, 0.0)[:, :2]

    load_off.wait()
    load_part.wait()
    pair_sums(spectra, off_ref[zh] & 1, finish)


def local(traces, gate_starts, section_offsets):
    hbm = pl.BlockSpec(memory_space=pltpu.HBM)
    any_space = pl.BlockSpec(memory_space=pl.ANY)
    dma = pltpu.SemaphoreType.DMA
    table = jnp.asarray(packed_table())
    far, part = pl.pallas_call(
        gather_kernel,
        out_shape=(
            jax.ShapeDtypeStruct((4, BLOCKS, 16, W), bf16),
            jax.ShapeDtypeStruct((4, 9, PARTNERS, W), f32),
        ),
        in_specs=[hbm, hbm, hbm, any_space],
        out_specs=(any_space, any_space),
        scratch_shapes=[
            pltpu.VMEM((4, BLOCKS, 16, W), bf16),
            pltpu.VMEM((2 * W, NT), bf16),
            pltpu.VMEM((SLOTS, 4, 8, W), jnp.int32),
            pltpu.VMEM((SLOTS, 4, 2, 32, W), f32),
            pltpu.VMEM((4, 9, PARTNERS, W), f32),
            pltpu.SMEM((PLANE, 2), jnp.int32),
            pltpu.VMEM((8, RECV, NT), bf16),
            pltpu.VMEM((8, 512), jnp.int32),
            pltpu.VMEM((256, 8), f32),
            pltpu.VMEM((RECV * 8, W), f32),
            pltpu.VMEM((16, 16, W), bf16),
            pltpu.VMEM((CLASSES, 2, 16, W), bf16),
            pltpu.VMEM((32, 16, W), bf16),
            pltpu.VMEM((2, PLANE, 2, 16, W), bf16),
            pltpu.VMEM((CLASSES, 2, 16, W), bf16),
            pltpu.VMEM((CLASSES, 2, 16, W), bf16),
            pltpu.VMEM((2, SEC_REACH, 16, W), bf16),
            pltpu.VMEM((2, SEC_OWN + 1, 16, W), bf16),
            pltpu.VMEM((SEC_OWN + 1, 16, W), bf16),
            dma((6,)), dma((8,)), dma((8,)), dma((8,)), dma((8,)), dma((8,)), dma((8,)),
            dma((8,)), dma((8,)), dma((8,)), dma((8,)), dma, dma, dma((18,)), dma((18,)), dma((6,)),
        ],
        compiler_params=pltpu.CompilerParams(
            collective_id=0, has_side_effects=True, vmem_limit_bytes=60 * 2**20
        ),
        name="gather",
    )(section_offsets, traces, gate_starts, table)
    return cross_call(section_offsets, far, part, table)


def cross_call(section_offsets, far, part, table):
    any_space = pl.BlockSpec(memory_space=pl.ANY)
    vmem = pl.BlockSpec(memory_space=pltpu.VMEM)
    dma = pltpu.SemaphoreType.DMA
    return pl.pallas_call(
        cross_kernel,
        out_shape=jax.ShapeDtypeStruct((4, PARTNERS, NT + 2), f32),
        in_specs=[any_space, vmem, any_space, vmem],
        out_specs=vmem,
        scratch_shapes=[
            pltpu.SMEM((2,), jnp.int32),
            pltpu.VMEM((SLOTS, 4, 8, W), jnp.int32),
            pltpu.VMEM((SLOTS, 4, 2, 32, W), f32),
            pltpu.VMEM((4, 9, PARTNERS, W), f32),
            dma((2,)),
        ],
        compiler_params=pltpu.CompilerParams(vmem_limit_bytes=24 * 2**20),
        name="cross",
    )(section_offsets, far, part, table)


def solution(mesh):
    in_specs = (P("shot", "well", None), P("shot", None), P("well"))
    out_specs = P(("well", "shot"), None, None)
    return jax.shard_map(local, mesh=mesh, in_specs=in_specs, out_specs=out_specs, check_vma=False)
```

```python
import functools
import math

import jax
import jax.numpy as jnp
import ml_dtypes
import numpy as np
from jax import lax
from jax.experimental import pallas as pl
from jax.experimental.pallas import tpu as pltpu
from jax.sharding import PartitionSpec as P

NT = 1024
W = 128
SEC = 16
PARTNERS = 16
PLANE = 8
RECV = 32
OWN_PAIRS = 2
REACH_PAIRS = 10
BLOCKS = REACH_PAIRS + OWN_PAIRS + 1
SEC_REACH = 16
SEC_OWN = 8
CLASSES = 8
SLOTS = 2 * (REACH_PAIRS + OWN_PAIRS)
MESH = pl.DeviceIdType.MESH
f32 = jnp.float32
bf16 = jnp.bfloat16

def packed_table():
    steps = np.arange(2 * W)
    k = np.arange(NT // 2)
    angle = ((steps[:, None] * k[None, :]) % NT).astype(np.float32) * np.float32(2 * math.pi / NT)
    real = np.cos(angle)
    imag = -np.sin(angle)
    imag[:, 0] = np.cos(math.pi * steps)
    scale = np.float32(1.0 / math.sqrt(W))
    return (np.concatenate([real, imag], axis=1) * scale).astype(ml_dtypes.bfloat16)


def place():
    well = lax.axis_index("well")
    shot = lax.axis_index("shot")
    return well // PLANE, well % PLANE, shot // 4, shot % 4


def gather_kernel(
    off_hbm, traces_hbm, gates_hbm, table_hbm, far_hbm, part_hbm,
    near_in, table, gate_vals, spectra, part,
    offs, traces, gates, gate_cols, rows, unit, dealt, held, picked, landed, far_landed, ordered, extra, far_extra,
    load_sem, o_send, o_recv, a_send, a_recv, z_send, z_recv, n_send, n_recv,
    f_send, f_recv, e_send, e_recv, y_send, y_recv, keep_sem,
):
    z, wp, zh, y = place()
    x, core = wp // 2, wp % 2
    well = z * PLANE + wp
    shot = zh * 4 + y
    far_shot = (1 - zh) * 4 + y
    before = jnp.maximum(z - 1, 0)

    steps = [(dx, dc) for dx in (0, 1, 3, 2) for dc in (0, 1)]
    near = [(x + dx) % 4 * 2 + (core + dc) % 2 for dx, dc in steps]
    y_peers = [(y + d) % 4 for d in (1, 3, 2)]

    load_traces = pltpu.make_async_copy(traces_hbm, traces, load_sem.at[3])
    load_traces.start()
    here = pl.multiple_of(z * 256, 256)
    ahead = pl.multiple_of(jnp.minimum(z + 1, 7) * 256, 256)
    load_here = pltpu.make_async_copy(gates_hbm.at[:, pl.ds(here, 256)], gates.at[:, pl.ds(0, 256)], load_sem.at[0])
    load_ahead = pltpu.make_async_copy(gates_hbm.at[:, pl.ds(ahead, 256)], gates.at[:, pl.ds(256, 256)], load_sem.at[1])
    load_off = pltpu.make_async_copy(off_hbm, offs.at[wp], load_sem.at[2])
    load_table = pltpu.make_async_copy(table_hbm, table, load_sem.at[4])
    load_here.start()

    barrier = pltpu.get_barrier_semaphore()

    def greet(to_well, to_shot):
        pl.semaphore_signal(barrier, inc=1, device_id=(to_well, to_shot), device_id_type=MESH)

    @pl.when(z < 7)
    def _():
        for peer in near:
            greet((z + 1) * PLANE + peer, shot)

    for peer in near[1:]:
        greet(z * PLANE + peer, shot)
    for peer in y_peers:
        greet(well, zh * 4 + peer)

    def greet_far():
        for peer in near:
            greet(z * PLANE + peer, far_shot)

    def wait_for(more):
        @pl.when(z > 0)
        def _():
            pl.semaphore_wait(barrier, 18 + more)

        @pl.when(z == 0)
        def _():
            pl.semaphore_wait(barrier, 10 + more)

    load_off.start()
    load_ahead.start()
    load_table.start()

    @pl.when(z == 7)
    def _():
        held[pl.ds(16, 16)] = jnp.zeros((16, 16, W), bf16)

    lane = lax.broadcasted_iota(jnp.int32, (RECV, W), 1)
    taper = 0.5 - 0.5 * jnp.cos((lane[:8].astype(f32) + 0.5) * (2 * math.pi / W))
    taper = jnp.concatenate([taper] * (RECV // 8), axis=0)
    load_here.wait()
    gate_cols[...] = jnp.transpose(gates[:, :256].astype(f32))
    columns = gate_cols[pl.ds(pl.multiple_of(wp * RECV, RECV), RECV), :].astype(jnp.int32)
    load_ahead.wait()
    load_off.wait()
    all_gates = gates[...]
    halves = jnp.concatenate([all_gates >> 3, all_gates & 7], axis=0).astype(f32).astype(bf16)
    lanes = lax.broadcasted_iota(jnp.int32, (512, W), 1)
    index = lax.broadcasted_iota(jnp.int32, (512, W), 0)
    for h in (1, 0):
        own = wp * RECV + (zh + h) % 2 * SEC
        start = (own + offs[wp, (zh + h) % 2]) // 2 * 2
        wanted = jnp.where(lanes < 32, start + lanes, own - 32 + lanes)
        one_hot = jnp.where(index == wanted, 1.0, 0.0).astype(bf16)
        block = jnp.dot(halves, one_hot, preferred_element_type=f32)
        extra[h, SEC_OWN] = block.astype(bf16)

    @pl.when(zh == 0)
    def _():
        wait_for(0)
        greet_far()

    load_traces.wait()
    for s in range(8):
        data = traces[s].astype(f32)
        gate = jnp.broadcast_to(columns[:, s : s + 1], (RECV, W))
        fine = gate & 127
        tiles = [data[:, k * W : (k + 1) * W] for k in range(8)]
        pick = (gate & 512) != 0
        four = [jnp.where(pick, tiles[k + 4], tiles[k]) for k in range(4)] + [tiles[4]]
        pick = (gate & 256) != 0
        three = [jnp.where(pick, four[k + 2], four[k]) for k in range(3)]
        pick = (gate & 128) != 0
        low = jnp.where(pick, three[1], three[0])
        high = jnp.where(pick, three[2], three[1])
        turned = jnp.where(lane >= fine, low, high)
        for bit in range(3, 7):
            step = 1 << bit
            turned = jnp.where((fine & step) != 0, pltpu.roll(turned, W - step, 1), turned)
        rows[pl.ds(s, RECV, stride=8), :] = turned * jnp.take_along_axis(taper, (lane - (gate & 7)) & 127, axis=1)
    pairs = rows[...].reshape(16, 16, W).astype(bf16)
    unit[...] = pairs
    for i in range(2):
        for m in range(CLASSES):
            dealt[m, i] = pairs[i * CLASSES + m]
    for h in (1, 0):
        extra[h, :SEC_OWN] = unit[pl.ds((zh + h) % 2 * SEC_OWN, SEC_OWN)]

    @pl.when(zh == 1)
    def _():
        wait_for(8)
        greet_far()

    def remote(source, target, send, receive, to_well, to_shot):
        return pltpu.make_async_remote_copy(
            src_ref=source, dst_ref=target, send_sem=send, recv_sem=receive,
            device_id=(to_well, to_shot), device_id_type=MESH,
        )

    e_copy = remote(extra.at[1], far_extra, e_send, e_recv, well, far_shot)

    mine = pl.ds(wp * 2, 2)
    mine_ahead = pl.ds(16 + wp * 2, 2)

    def z_copy(k):
        return remote(
            dealt.at[near[k]], held.at[mine_ahead], z_send.at[k], z_recv.at[k], before * PLANE + near[k], shot
        )

    @pl.when(z > 0)
    def _():
        for k in range(8):
            z_copy(k).start()

    a_copies = []
    o_copies = []
    for k in range(1, 8):
        to_well = z * PLANE + near[k]
        copy = remote(dealt.at[near[k]], held.at[mine], a_send.at[k], a_recv.at[k], to_well, shot)
        copy.start()
        a_copies.append(copy)
    for k in range(1, 8):
        copy = remote(offs.at[wp], offs.at[wp], o_send.at[k], o_recv.at[k], z * PLANE + near[k], shot)
        copy.start()
        o_copies.append(copy)
    held[mine] = dealt[wp]

    @pl.when(zh == 1)
    def _():
        e_copy.start()

    for copy in o_copies:
        copy.wait_recv()
    for copy in a_copies:
        copy.wait_recv()

    @pl.when(z < 7)
    def _():
        for k in range(8):
            z_copy(k).wait_recv()

    for h in (1, 0):
        section = (zh + h) % 2
        for k in range(8):
            first = near[k] * 16 + section * SEC_OWN + offs[near[k], section] // 2
            at = (first + (wp + 512 - first) % CLASSES) // CLASSES
            picked[h, k] = held[pl.ds(at, 2)]
    f_copies = []
    n_copies = []
    for k in range(8):
        to_well = z * PLANE + near[k]
        f_copies.append(remote(picked.at[1, k], far_landed.at[wp], f_send.at[k], f_recv.at[k], to_well, far_shot))

    @pl.when(zh == 1)
    def _():
        for copy in f_copies:
            copy.start()

    for k in range(1, 8):
        to_well = z * PLANE + near[k]
        copy = remote(picked.at[0, k], landed.at[wp], n_send.at[k], n_recv.at[k], to_well, shot)
        copy.start()
        n_copies.append(copy)
    landed[wp] = picked[0, 0]

    @pl.when(zh == 0)
    def _():
        pl.semaphore_wait(barrier, 8)
        for copy in f_copies:
            copy.start()
        e_copy.start()

    own_first = wp * 16 + zh * SEC_OWN + offs[wp, zh] // 2

    def pass_on(h, kinds):
        target = (far_hbm if h else near_in).at[y]
        more = far_extra if h else extra.at[0]

        def pieces(to_y):
            return [
                (ordered.at[h, pl.ds(2 * to_y, REACH_PAIRS)], target.at[pl.ds(0, REACH_PAIRS)]),
                (more.at[pl.ds(2 * to_y, OWN_PAIRS)], target.at[pl.ds(REACH_PAIRS, OWN_PAIRS)]),
                (more.at[pl.ds(SEC_OWN, 1)], target.at[pl.ds(BLOCKS - 1, 1)]),
            ]

        copies = []
        for i, peer in enumerate(y_peers):
            for kind in kinds:
                n = (h * 3 + i) * 3 + kind
                source, to = pieces(peer)[kind]
                copies.append(remote(source, to, y_send.at[n], y_recv.at[n], well, zh * 4 + peer))
        for kind in kinds:
            source, to = pieces(y)[kind]
            copies.append(pltpu.make_async_copy(source, to, keep_sem.at[h * 3 + kind]))
        for copy in copies:
            copy.start()
        return copies

    def put_in_order(h, arrived):
        for i in range(SEC_REACH):
            ordered[h, i] = arrived[(own_first + i) % CLASSES, i // CLASSES]

    near_copies = pass_on(0, (1, 2))
    for copy in n_copies:
        copy.wait_recv()
    put_in_order(0, landed)
    near_copies += pass_on(0, (0,))

    for copy in near_copies:
        copy.wait()
    load_table.wait()
    make_spectra(near_in, table, gate_vals, spectra, y)

    def keep(a, group, reals, imags):
        rows = pl.ds(group * 8, 8)
        for t in range(4):
            part[a, t, rows] = reals[t]
        for t in range(5):
            part[a, 4 + t, rows] = imags[t]

    e_copy.wait_recv()
    far_copies = pass_on(1, (1, 2))
    for copy in f_copies:
        copy.wait_recv()
    put_in_order(1, far_landed)
    far_copies += pass_on(1, (0,))

    pair_sums(spectra, offs[wp, zh] % 2, keep)
    keep_part = pltpu.make_async_copy(part, part_hbm, load_sem.at[5])
    keep_part.start()
    keep_part.wait()

    @pl.when(z > 0)
    def _():
        for k in range(8):
            z_copy(k).wait_send()

    for copy in a_copies + o_copies + n_copies + f_copies + [e_copy]:
        copy.wait_send()
    for copy in far_copies:
        copy.wait()


def fold(parts):
    row = lax.broadcasted_iota(jnp.int32, (8, W), 0)
    while len(parts) > 1:
        half = len(parts) // 2
        upper = (row & half) == 0
        merged = []
        for i in range(half):
            first, second = parts[i], parts[i + half]
            kept = jnp.where(upper, first, second)
            moved = jnp.where(upper, second, first)
            if half == 4:
                moved = pltpu.roll(moved, 4, 0)
            else:
                moved = jnp.where(upper, pltpu.roll(moved, 8 - half, 0), pltpu.roll(moved, half, 0))
            merged.append(kept + moved)
        parts = merged
    return parts[0]


def make_spectra(data, table, gate_vals, spectra, y):
    lane = lax.broadcasted_iota(jnp.int32, (8, W), 1)
    angle = lane.astype(f32) * (2 * math.pi / W)
    cosines = jnp.cos(angle)
    sines = jnp.sin(angle)

    for k in range(4):
        block = pltpu.roll(data[k, BLOCKS - 1].astype(f32), (W - 4 * y) % W, 1)
        gate = (block[:8] * 8.0 + block[8:]).astype(jnp.int32)
        for slot in range(SLOTS):
            column = slot if slot < 20 else 12 + slot
            gate_vals[slot, k] = jnp.broadcast_to(gate[:, column : column + 1], (8, W))

    @pl.loop(0, SLOTS // 4)
    def _(step):
        lefts = []
        for p in range(2):
            for k in range(4):
                both = data[k, 2 * step + p].astype(f32)
                halves = []
                for par in range(2):
                    window = both[par * 8 : par * 8 + 8]
                    low = jnp.where(lane >= (gate_vals[4 * step + 2 * p + par, k] & 7), window, 0.0)
                    halves.append(jnp.concatenate([low, window - low], axis=1))
                lefts.append(jnp.concatenate(halves, axis=0).astype(bf16))
        flat = jnp.dot(jnp.concatenate(lefts, axis=0), table[...], preferred_element_type=f32)
        for p in range(2):
            for par in range(2):
                slot = 4 * step + 2 * p + par
                for k in range(4):
                    first = p * 64 + k * 16 + par * 8
                    index = ((gate_vals[slot, k] >> 3) * lane) & 127
                    cosine = jnp.take_along_axis(cosines, index, axis=1)
                    sine = jnp.take_along_axis(sines, index, axis=1)
                    rows = slice(k * 8, k * 8 + 8)
                    for t in range(4):
                        real = flat[first : first + 8, t * W : (t + 1) * W]
                        imag = flat[first : first + 8, (4 + t) * W : (5 + t) * W]
                        spectra[slot, t, 0, rows, :] = cosine * real + sine * imag
                        spectra[slot, t, 1, rows, :] = cosine * imag - sine * real


def pair_sums(spectra, odd, emit):
    lane = lax.broadcasted_iota(jnp.int32, (8, W), 1)

    @pl.loop(0, 4)
    def _(a):
        reals = [[], []]
        imags = [[], []]
        for t in range(4):
            own = [[spectra[20 + a, t, c, k * 8 : k * 8 + 8, :] for c in range(2)] for k in range(4)]
            for group in range(2):
                sums = []
                for j in range(8):
                    slot = a + odd + group * 8 + j
                    one = two = three = None
                    for k in range(4):
                        re = spectra[slot, t, 0, k * 8 : k * 8 + 8, :]
                        im = spectra[slot, t, 1, k * 8 : k * 8 + 8, :]
                        first = own[k][0] * re
                        second = own[k][1] * im
                        third = own[k][0] * im - own[k][1] * re
                        one = first if one is None else one + first
                        two = second if two is None else two + second
                        three = third if three is None else three + third
                    sums.append((one, two, three))
                threes = fold([s[2] for s in sums])
                if t == 0:
                    ones = fold([s[0] for s in sums])
                    twos = fold([s[1] for s in sums])
                    reals[group].append(jnp.where(lane == 0, ones, ones + twos))
                    imags[group].append(twos)
                    imags[group].append(jnp.where(lane == 0, 0.0, threes))
                else:
                    reals[group].append(fold([s[0] + s[1] for s in sums]))
                    imags[group].append(threes)
        for group in range(2):
            emit(a, group, reals[group], imags[group])


def cross_kernel(
    off_hbm, data_hbm, part_hbm, table_hbm, out_hbm, off_ref, data, table, gate_vals, spectra, part, out, sem, out_sem
):
    z, wp, zh, y = place()
    load_data = pltpu.make_async_copy(data_hbm, data, sem.at[0])
    load_data.start()
    load_table = pltpu.make_async_copy(table_hbm, table, sem.at[1])
    load_table.start()
    load_off = pltpu.make_async_copy(off_hbm, off_ref, sem.at[2])
    load_off.start()
    load_part = pltpu.make_async_copy(part_hbm, part, sem.at[3])
    load_part.start()
    load_data.wait()
    load_table.wait()
    lane = lax.broadcasted_iota(jnp.int32, (8, W), 1)
    make_spectra(data, table, gate_vals, spectra, y)

    def finish(a, group, reals, imags):
        rows = pl.ds(group * 8, 8)
        for t in range(4):
            out[a, rows, t * W : (t + 1) * W] = reals[t] + part[a, t, rows]
        imags = [imags[t] + part[a, 4 + t, rows] for t in range(5)]
        before = imags[0]
        for t in range(4):
            turned = pltpu.roll(imags[1 + t], 1, 1)
            out[a, rows, (4 + t) * W : (5 + t) * W] = jnp.where(lane == 0, before, turned)
            before = turned
        out[a, rows, 8 * W : 8 * W + 2] = jnp.where(lane == 0, before, 0.0)[:, :2]
        if group == 1:
            pltpu.make_async_copy(out.at[a], out_hbm.at[a], out_sem.at[a]).start()

    load_off.wait()
    load_part.wait()
    pair_sums(spectra, off_ref[zh] & 1, finish)
    for a in range(4):
        pltpu.make_async_copy(out.at[a], out_hbm.at[a], out_sem.at[a]).wait()


def local(traces, gate_starts, section_offsets):
    hbm = pl.BlockSpec(memory_space=pltpu.HBM)
    any_space = pl.BlockSpec(memory_space=pl.ANY)
    dma = pltpu.SemaphoreType.DMA
    table = jnp.asarray(packed_table())
    far, part = pl.pallas_call(
        gather_kernel,
        out_shape=(
            jax.ShapeDtypeStruct((4, BLOCKS, 16, W), bf16),
            jax.ShapeDtypeStruct((4, 9, PARTNERS, W), f32),
        ),
        in_specs=[hbm, hbm, hbm, any_space],
        out_specs=(any_space, any_space),
        scratch_shapes=[
            pltpu.VMEM((4, BLOCKS, 16, W), bf16),
            pltpu.VMEM((2 * W, NT), bf16),
            pltpu.VMEM((SLOTS, 4, 8, W), jnp.int32),
            pltpu.VMEM((SLOTS, 4, 2, 32, W), f32),
            pltpu.VMEM((4, 9, PARTNERS, W), f32),
            pltpu.SMEM((PLANE, 2), jnp.int32),
            pltpu.VMEM((8, RECV, NT), bf16),
            pltpu.VMEM((8, 512), jnp.int32),
            pltpu.VMEM((256, 8), f32),
            pltpu.VMEM((RECV * 8, W), f32),
            pltpu.VMEM((16, 16, W), bf16),
            pltpu.VMEM((CLASSES, 2, 16, W), bf16),
            pltpu.VMEM((32, 16, W), bf16),
            pltpu.VMEM((2, PLANE, 2, 16, W), bf16),
            pltpu.VMEM((CLASSES, 2, 16, W), bf16),
            pltpu.VMEM((CLASSES, 2, 16, W), bf16),
            pltpu.VMEM((2, SEC_REACH, 16, W), bf16),
            pltpu.VMEM((2, SEC_OWN + 1, 16, W), bf16),
            pltpu.VMEM((SEC_OWN + 1, 16, W), bf16),
            dma((6,)), dma((8,)), dma((8,)), dma((8,)), dma((8,)), dma((8,)), dma((8,)),
            dma((8,)), dma((8,)), dma((8,)), dma((8,)), dma, dma, dma((18,)), dma((18,)), dma((6,)),
        ],
        compiler_params=pltpu.CompilerParams(
            collective_id=0, has_side_effects=True, vmem_limit_bytes=60 * 2**20
        ),
        name="gather",
    )(section_offsets, traces, gate_starts, table)
    return cross_call(section_offsets, far, part, table)


def cross_call(section_offsets, far, part, table):
    any_space = pl.BlockSpec(memory_space=pl.ANY)
    dma = pltpu.SemaphoreType.DMA
    return pl.pallas_call(
        cross_kernel,
        out_shape=jax.ShapeDtypeStruct((4, PARTNERS, NT + 2), f32),
        in_specs=[any_space, any_space, any_space, any_space],
        out_specs=any_space,
        scratch_shapes=[
            pltpu.SMEM((2,), jnp.int32),
            pltpu.VMEM((4, BLOCKS, 16, W), bf16),
            pltpu.VMEM((2 * W, NT), bf16),
            pltpu.VMEM((SLOTS, 4, 8, W), jnp.int32),
            pltpu.VMEM((SLOTS, 4, 2, 32, W), f32),
            pltpu.VMEM((4, 9, PARTNERS, W), f32),
            pltpu.VMEM((4, PARTNERS, NT + 2), f32),
            dma((4,)), dma((4,)),
        ],
        compiler_params=pltpu.CompilerParams(vmem_limit_bytes=60 * 2**20),
        name="cross",
    )(section_offsets, far, part, table)


def solution(mesh):
    in_specs = (P("shot", "well", None), P("shot", None), P("well"))
    out_specs = P(("well", "shot"), None, None)
    return jax.shard_map(local, mesh=mesh, in_specs=in_specs, out_specs=out_specs, check_vma=False)
```

```python
import functools
import math

import jax
import jax.numpy as jnp
import ml_dtypes
import numpy as np
from jax import lax
from jax.experimental import pallas as pl
from jax.experimental.pallas import tpu as pltpu
from jax.sharding import PartitionSpec as P

NT = 1024
W = 128
SEC = 16
PARTNERS = 16
PLANE = 8
RECV = 32
OWN_PAIRS = 2
REACH_PAIRS = 10
BLOCKS = REACH_PAIRS + OWN_PAIRS + 1
SEC_REACH = 16
SEC_OWN = 8
CLASSES = 8
SLOTS = 2 * (REACH_PAIRS + OWN_PAIRS)
MESH = pl.DeviceIdType.MESH
f32 = jnp.float32
bf16 = jnp.bfloat16

def packed_table():
    steps = np.arange(2 * W)
    k = np.arange(NT // 2)
    angle = ((steps[:, None] * k[None, :]) % NT).astype(np.float32) * np.float32(2 * math.pi / NT)
    real = np.cos(angle)
    imag = -np.sin(angle)
    imag[:, 0] = np.cos(math.pi * steps)
    scale = np.float32(1.0 / math.sqrt(W))
    return (np.concatenate([real, imag], axis=1) * scale).astype(ml_dtypes.bfloat16)


def place():
    well = lax.axis_index("well")
    shot = lax.axis_index("shot")
    return well // PLANE, well % PLANE, shot // 4, shot % 4


def gather_kernel(
    off_hbm, traces_hbm, gates_hbm, table_hbm, far_hbm, part_hbm,
    near_in, table, gate_vals, spectra, part,
    offs, traces, gates, gate_cols, rows, unit, dealt, held, picked, landed, far_landed, ordered, extra, far_extra,
    load_sem, o_send, o_recv, a_send, a_recv, z_send, z_recv, n_send, n_recv,
    f_send, f_recv, e_send, e_recv, y_send, y_recv, keep_sem,
):
    z, wp, zh, y = place()
    x, core = wp // 2, wp % 2
    well = z * PLANE + wp
    shot = zh * 4 + y
    far_shot = (1 - zh) * 4 + y
    before = jnp.maximum(z - 1, 0)

    steps = [(dx, dc) for dx in (0, 1, 3, 2) for dc in (0, 1)]
    near = [(x + dx) % 4 * 2 + (core + dc) % 2 for dx, dc in steps]
    y_peers = [(y + d) % 4 for d in (1, 3, 2)]

    load_traces = pltpu.make_async_copy(traces_hbm, traces, load_sem.at[3])
    load_traces.start()
    here = pl.multiple_of(z * 256, 256)
    ahead = pl.multiple_of(jnp.minimum(z + 1, 7) * 256, 256)
    load_here = pltpu.make_async_copy(gates_hbm.at[:, pl.ds(here, 256)], gates.at[:, pl.ds(0, 256)], load_sem.at[0])
    load_ahead = pltpu.make_async_copy(gates_hbm.at[:, pl.ds(ahead, 256)], gates.at[:, pl.ds(256, 256)], load_sem.at[1])
    load_off = pltpu.make_async_copy(off_hbm, offs.at[wp], load_sem.at[2])
    load_table = pltpu.make_async_copy(table_hbm, table, load_sem.at[4])
    load_here.start()

    barrier = pltpu.get_barrier_semaphore()

    def greet(to_well, to_shot):
        pl.semaphore_signal(barrier, inc=1, device_id=(to_well, to_shot), device_id_type=MESH)

    @pl.when(z < 7)
    def _():
        for peer in near:
            greet((z + 1) * PLANE + peer, shot)

    for peer in near[1:]:
        greet(z * PLANE + peer, shot)
    for peer in y_peers:
        greet(well, zh * 4 + peer)

    def greet_far():
        for peer in near:
            greet(z * PLANE + peer, far_shot)

    def wait_for(more):
        @pl.when(z > 0)
        def _():
            pl.semaphore_wait(barrier, 18 + more)

        @pl.when(z == 0)
        def _():
            pl.semaphore_wait(barrier, 10 + more)

    load_off.start()
    load_ahead.start()
    load_table.start()

    @pl.when(z == 7)
    def _():
        held[pl.ds(16, 16)] = jnp.zeros((16, 16, W), bf16)

    lane = lax.broadcasted_iota(jnp.int32, (RECV, W), 1)
    taper = 0.5 - 0.5 * jnp.cos((lane[:8].astype(f32) + 0.5) * (2 * math.pi / W))
    taper = jnp.concatenate([taper] * (RECV // 8), axis=0)
    load_here.wait()
    gate_cols[...] = jnp.transpose(gates[:, :256].astype(f32))
    columns = gate_cols[pl.ds(pl.multiple_of(wp * RECV, RECV), RECV), :].astype(jnp.int32)
    load_ahead.wait()
    load_off.wait()
    all_gates = gates[...]
    halves = jnp.concatenate([all_gates >> 3, all_gates & 7], axis=0).astype(f32).astype(bf16)
    lanes = lax.broadcasted_iota(jnp.int32, (512, W), 1)
    index = lax.broadcasted_iota(jnp.int32, (512, W), 0)
    for h in (1, 0):
        own = wp * RECV + (zh + h) % 2 * SEC
        start = (own + offs[wp, (zh + h) % 2]) // 2 * 2
        wanted = jnp.where(lanes < 32, start + lanes, own - 32 + lanes)
        one_hot = jnp.where(index == wanted, 1.0, 0.0).astype(bf16)
        block = jnp.dot(halves, one_hot, preferred_element_type=f32)
        extra[h, SEC_OWN] = block.astype(bf16)

    @pl.when(zh == 0)
    def _():
        wait_for(0)
        greet_far()

    def remote(source, target, send, receive, to_well, to_shot):
        return pltpu.make_async_remote_copy(
            src_ref=source, dst_ref=target, send_sem=send, recv_sem=receive,
            device_id=(to_well, to_shot), device_id_type=MESH,
        )

    load_traces.wait()

    @pl.when(zh == 1)
    def _():
        wait_for(8)
        greet_far()

    o_copies = []
    for k in range(1, 8):
        copy = remote(offs.at[wp], offs.at[wp], o_send.at[k], o_recv.at[k], z * PLANE + near[k], shot)
        copy.start()
        o_copies.append(copy)
    for s in range(8):
        data = traces[s].astype(f32)
        gate = jnp.broadcast_to(columns[:, s : s + 1], (RECV, W))
        fine = gate & 127
        tiles = [data[:, k * W : (k + 1) * W] for k in range(8)]
        pick = (gate & 512) != 0
        four = [jnp.where(pick, tiles[k + 4], tiles[k]) for k in range(4)] + [tiles[4]]
        pick = (gate & 256) != 0
        three = [jnp.where(pick, four[k + 2], four[k]) for k in range(3)]
        pick = (gate & 128) != 0
        low = jnp.where(pick, three[1], three[0])
        high = jnp.where(pick, three[2], three[1])
        turned = jnp.where(lane >= fine, low, high)
        for bit in range(3, 7):
            step = 1 << bit
            turned = jnp.where((fine & step) != 0, pltpu.roll(turned, W - step, 1), turned)
        rows[pl.ds(s, RECV, stride=8), :] = turned * jnp.take_along_axis(taper, (lane - (gate & 7)) & 127, axis=1)
    pairs = rows[...].reshape(16, 16, W).astype(bf16)
    unit[...] = pairs
    for i in range(2):
        for m in range(CLASSES):
            dealt[m, i] = pairs[i * CLASSES + m]
    for h in (1, 0):
        extra[h, :SEC_OWN] = unit[pl.ds((zh + h) % 2 * SEC_OWN, SEC_OWN)]

    e_copy = remote(extra.at[1], far_extra, e_send, e_recv, well, far_shot)

    mine = pl.ds(wp * 2, 2)
    mine_ahead = pl.ds(16 + wp * 2, 2)

    def z_copy(k):
        return remote(
            dealt.at[near[k]], held.at[mine_ahead], z_send.at[k], z_recv.at[k], before * PLANE + near[k], shot
        )

    @pl.when(z > 0)
    def _():
        for k in (7, 6, 5, 4, 3, 2, 1, 0):
            z_copy(k).start()

    a_copies = []
    for k in (7, 6, 5, 4, 3, 2, 1):
        to_well = z * PLANE + near[k]
        copy = remote(dealt.at[near[k]], held.at[mine], a_send.at[k], a_recv.at[k], to_well, shot)
        copy.start()
        a_copies.append(copy)
    held[mine] = dealt[wp]

    @pl.when(zh == 1)
    def _():
        e_copy.start()

    for copy in o_copies:
        copy.wait_recv()
    for copy in a_copies:
        copy.wait_recv()

    @pl.when(z < 7)
    def _():
        for k in range(8):
            z_copy(k).wait_recv()

    def pick(h):
        section = (zh + h) % 2
        for k in range(8):
            first = near[k] * 16 + section * SEC_OWN + offs[near[k], section] // 2
            at = (first + (wp + 512 - first) % CLASSES) // CLASSES
            picked[h, k] = held[pl.ds(at, 2)]

    f_copies = []
    for k in (7, 6, 5, 4, 3, 2, 1, 0):
        to_well = z * PLANE + near[k]
        f_copies.append(remote(picked.at[1, k], far_landed.at[wp], f_send.at[k], f_recv.at[k], to_well, far_shot))
    pick(1)

    @pl.when(zh == 1)
    def _():
        for copy in f_copies:
            copy.start()

    pick(0)
    n_copies = []
    for k in (7, 6, 5, 4, 3, 2, 1):
        to_well = z * PLANE + near[k]
        copy = remote(picked.at[0, k], landed.at[wp], n_send.at[k], n_recv.at[k], to_well, shot)
        copy.start()
        n_copies.append(copy)
    landed[wp] = picked[0, 0]

    @pl.when(zh == 0)
    def _():
        pl.semaphore_wait(barrier, 8)
        for copy in f_copies:
            copy.start()
        e_copy.start()

    own_first = wp * 16 + zh * SEC_OWN + offs[wp, zh] // 2

    def pass_on(h, kinds):
        more = far_extra if h else extra.at[0]

        def pieces(to_y, target):
            return [
                (ordered.at[h, pl.ds(2 * to_y, REACH_PAIRS)], target.at[pl.ds(0, REACH_PAIRS)]),
                (more.at[pl.ds(2 * to_y, OWN_PAIRS)], target.at[pl.ds(REACH_PAIRS, OWN_PAIRS)]),
                (more.at[pl.ds(SEC_OWN, 1)], target.at[pl.ds(BLOCKS - 1, 1)]),
            ]

        copies = []
        for i, peer in enumerate(y_peers):
            for kind in kinds:
                n = (h * 3 + i) * 3 + kind
                source, to = pieces(peer, far_hbm.at[i] if h else near_in.at[y])[kind]
                copies.append(remote(source, to, y_send.at[n], y_recv.at[n], well, zh * 4 + peer))
        kept = []
        for kind in kinds:
            source, to = pieces(y, near_in.at[4 if h else y])[kind]
            kept.append(pltpu.make_async_copy(source, to, keep_sem.at[h * 3 + kind]))
        for copy in copies + kept:
            copy.start()
        return copies, kept

    def put_in_order(h, arrived):
        for i in range(SEC_REACH):
            ordered[h, i] = arrived[(own_first + i) % CLASSES, i // CLASSES]

    some, kept = pass_on(0, (1, 2))
    for copy in n_copies:
        copy.wait_recv()
    put_in_order(0, landed)
    more, kept_more = pass_on(0, (0,))
    near_copies = some + kept + more + kept_more

    for copy in near_copies:
        copy.wait()
    load_table.wait()
    make_spectra(near_in, (0, 1, 2, 3), table, gate_vals, spectra, y)

    def keep(a, group, reals, imags):
        rows = pl.ds(group * 8, 8)
        for t in range(4):
            part[a, t, rows] = reals[t]
        for t in range(5):
            part[a, 4 + t, rows] = imags[t]

    e_copy.wait_recv()
    some, kept = pass_on(1, (1, 2))
    for copy in f_copies:
        copy.wait_recv()
    put_in_order(1, far_landed)
    more, kept_more = pass_on(1, (0,))
    far_copies = some + more

    for copy in kept + kept_more:
        copy.wait()
    make_spectra(near_in, (4,), table, gate_vals, spectra, y)
    pair_sums(spectra, 5, offs[wp, zh] % 2, keep)
    keep_part = pltpu.make_async_copy(part, part_hbm, load_sem.at[5])
    keep_part.start()
    keep_part.wait()

    @pl.when(z > 0)
    def _():
        for k in range(8):
            z_copy(k).wait_send()

    for copy in a_copies + o_copies + n_copies + f_copies + [e_copy]:
        copy.wait_send()
    for copy in far_copies:
        copy.wait()


def fold(parts):
    row = lax.broadcasted_iota(jnp.int32, (8, W), 0)
    while len(parts) > 1:
        half = len(parts) // 2
        upper = (row & half) == 0
        merged = []
        for i in range(half):
            first, second = parts[i], parts[i + half]
            kept = jnp.where(upper, first, second)
            moved = jnp.where(upper, second, first)
            if half == 4:
                moved = pltpu.roll(moved, 4, 0)
            else:
                moved = jnp.where(upper, pltpu.roll(moved, 8 - half, 0), pltpu.roll(moved, half, 0))
            merged.append(kept + moved)
        parts = merged
    return parts[0]


def make_spectra(data, groups, table, gate_vals, spectra, y):
    lane = lax.broadcasted_iota(jnp.int32, (8, W), 1)
    angle = lane.astype(f32) * (2 * math.pi / W)
    cosines = jnp.cos(angle)
    sines = jnp.sin(angle)
    pairs = {1: 6, 3: 3, 4: 2}[len(groups)]

    for k in groups:
        block = pltpu.roll(data[k, BLOCKS - 1].astype(f32), (W - 4 * y) % W, 1)
        gate = (block[:8] * 8.0 + block[8:]).astype(jnp.int32)
        for slot in range(SLOTS):
            column = slot if slot < 20 else 12 + slot
            gate_vals[slot, k] = jnp.broadcast_to(gate[:, column : column + 1], (8, W))

    @pl.loop(0, SLOTS // 2 // pairs)
    def _(step):
        lefts = []
        for p in range(pairs):
            for k in groups:
                both = data[k, pairs * step + p].astype(f32)
                halves = []
                for par in range(2):
                    window = both[par * 8 : par * 8 + 8]
                    fine = gate_vals[2 * (pairs * step + p) + par, k] & 7
                    low = jnp.where(lane >= fine, window, 0.0)
                    halves.append(jnp.concatenate([low, window - low], axis=1))
                lefts.append(jnp.concatenate(halves, axis=0).astype(bf16))
        flat = jnp.dot(jnp.concatenate(lefts, axis=0), table[...], preferred_element_type=f32)
        first = 0
        for p in range(pairs):
            for k in groups:
                for par in range(2):
                    slot = 2 * (pairs * step + p) + par
                    index = ((gate_vals[slot, k] >> 3) * lane) & 127
                    cosine = jnp.take_along_axis(cosines, index, axis=1)
                    sine = jnp.take_along_axis(sines, index, axis=1)
                    rows = slice(k * 8, k * 8 + 8)
                    for t in range(4):
                        real = flat[first : first + 8, t * W : (t + 1) * W]
                        imag = flat[first : first + 8, (4 + t) * W : (5 + t) * W]
                        spectra[slot, t, 0, rows, :] = cosine * real + sine * imag
                        spectra[slot, t, 1, rows, :] = cosine * imag - sine * real
                    first += 8


def pair_sums(spectra, groups, odd, emit):
    lane = lax.broadcasted_iota(jnp.int32, (8, W), 1)

    @pl.loop(0, 4)
    def _(a):
        reals = [[], []]
        imags = [[], []]
        for t in range(4):
            own = [[spectra[20 + a, t, c, k * 8 : k * 8 + 8, :] for c in range(2)] for k in range(groups)]
            for group in range(2):
                sums = []
                for j in range(8):
                    slot = a + odd + group * 8 + j
                    one = two = three = None
                    for k in range(groups):
                        re = spectra[slot, t, 0, k * 8 : k * 8 + 8, :]
                        im = spectra[slot, t, 1, k * 8 : k * 8 + 8, :]
                        first = own[k][0] * re
                        second = own[k][1] * im
                        third = own[k][0] * im - own[k][1] * re
                        one = first if one is None else one + first
                        two = second if two is None else two + second
                        three = third if three is None else three + third
                    sums.append((one, two, three))
                threes = fold([s[2] for s in sums])
                if t == 0:
                    ones = fold([s[0] for s in sums])
                    twos = fold([s[1] for s in sums])
                    reals[group].append(jnp.where(lane == 0, ones, ones + twos))
                    imags[group].append(twos)
                    imags[group].append(jnp.where(lane == 0, 0.0, threes))
                else:
                    reals[group].append(fold([s[0] + s[1] for s in sums]))
                    imags[group].append(threes)
        for group in range(2):
            emit(a, group, reals[group], imags[group])


def cross_kernel(
    off_hbm, data_hbm, part_hbm, table_hbm, out_hbm, off_ref, data, table, gate_vals, spectra, part, out, sem, out_sem
):
    z, wp, zh, y = place()
    load_data = pltpu.make_async_copy(data_hbm, data, sem.at[0])
    load_data.start()
    load_table = pltpu.make_async_copy(table_hbm, table, sem.at[1])
    load_table.start()
    load_off = pltpu.make_async_copy(off_hbm, off_ref, sem.at[2])
    load_off.start()
    load_part = pltpu.make_async_copy(part_hbm, part, sem.at[3])
    load_part.start()
    load_data.wait()
    load_table.wait()
    lane = lax.broadcasted_iota(jnp.int32, (8, W), 1)
    make_spectra(data, (0, 1, 2), table, gate_vals, spectra, y)

    def finish(a, group, reals, imags):
        rows = pl.ds(group * 8, 8)
        for t in range(4):
            out[a, rows, t * W : (t + 1) * W] = reals[t] + part[a, t, rows]
        imags = [imags[t] + part[a, 4 + t, rows] for t in range(5)]
        before = imags[0]
        for t in range(4):
            turned = pltpu.roll(imags[1 + t], 1, 1)
            out[a, rows, (4 + t) * W : (5 + t) * W] = jnp.where(lane == 0, before, turned)
            before = turned
        out[a, rows, 8 * W : 8 * W + 2] = jnp.where(lane == 0, before, 0.0)[:, :2]
        if group == 1:
            pltpu.make_async_copy(out.at[a], out_hbm.at[a], out_sem.at[a]).start()

    load_off.wait()
    load_part.wait()
    pair_sums(spectra, 3, off_ref[zh] & 1, finish)
    for a in range(4):
        pltpu.make_async_copy(out.at[a], out_hbm.at[a], out_sem.at[a]).wait()


def local(traces, gate_starts, section_offsets):
    hbm = pl.BlockSpec(memory_space=pltpu.HBM)
    any_space = pl.BlockSpec(memory_space=pl.ANY)
    dma = pltpu.SemaphoreType.DMA
    table = jnp.asarray(packed_table())
    far, part = pl.pallas_call(
        gather_kernel,
        out_shape=(
            jax.ShapeDtypeStruct((3, BLOCKS, 16, W), bf16),
            jax.ShapeDtypeStruct((4, 9, PARTNERS, W), f32),
        ),
        in_specs=[hbm, hbm, hbm, any_space],
        out_specs=(any_space, any_space),
        scratch_shapes=[
            pltpu.VMEM((5, BLOCKS, 16, W), bf16),
            pltpu.VMEM((2 * W, NT), bf16),
            pltpu.VMEM((SLOTS, 5, 8, W), jnp.int32),
            pltpu.VMEM((SLOTS, 4, 2, 40, W), f32),
            pltpu.VMEM((4, 9, PARTNERS, W), f32),
            pltpu.SMEM((PLANE, 2), jnp.int32),
            pltpu.VMEM((8, RECV, NT), bf16),
            pltpu.VMEM((8, 512), jnp.int32),
            pltpu.VMEM((256, 8), f32),
            pltpu.VMEM((RECV * 8, W), f32),
            pltpu.VMEM((16, 16, W), bf16),
            pltpu.VMEM((CLASSES, 2, 16, W), bf16),
            pltpu.VMEM((32, 16, W), bf16),
            pltpu.VMEM((2, PLANE, 2, 16, W), bf16),
            pltpu.VMEM((CLASSES, 2, 16, W), bf16),
            pltpu.VMEM((CLASSES, 2, 16, W), bf16),
            pltpu.VMEM((2, SEC_REACH, 16, W), bf16),
            pltpu.VMEM((2, SEC_OWN + 1, 16, W), bf16),
            pltpu.VMEM((SEC_OWN + 1, 16, W), bf16),
            dma((6,)), dma((8,)), dma((8,)), dma((8,)), dma((8,)), dma((8,)), dma((8,)),
            dma((8,)), dma((8,)), dma((8,)), dma((8,)), dma, dma, dma((18,)), dma((18,)), dma((6,)),
        ],
        compiler_params=pltpu.CompilerParams(
            collective_id=0, has_side_effects=True, vmem_limit_bytes=60 * 2**20
        ),
        name="gather",
    )(section_offsets, traces, gate_starts, table)
    return cross_call(section_offsets, far, part, table)


def cross_call(section_offsets, far, part, table):
    any_space = pl.BlockSpec(memory_space=pl.ANY)
    dma = pltpu.SemaphoreType.DMA
    return pl.pallas_call(
        cross_kernel,
        out_shape=jax.ShapeDtypeStruct((4, PARTNERS, NT + 2), f32),
        in_specs=[any_space, any_space, any_space, any_space],
        out_specs=any_space,
        scratch_shapes=[
            pltpu.SMEM((2,), jnp.int32),
            pltpu.VMEM((3, BLOCKS, 16, W), bf16),
            pltpu.VMEM((2 * W, NT), bf16),
            pltpu.VMEM((SLOTS, 3, 8, W), jnp.int32),
            pltpu.VMEM((SLOTS, 4, 2, 24, W), f32),
            pltpu.VMEM((4, 9, PARTNERS, W), f32),
            pltpu.VMEM((4, PARTNERS, NT + 2), f32),
            dma((4,)), dma((4,)),
        ],
        compiler_params=pltpu.CompilerParams(vmem_limit_bytes=60 * 2**20),
        name="cross",
    )(section_offsets, far, part, table)


def solution(mesh):
    in_specs = (P("shot", "well", None), P("shot", None), P("well"))
    out_specs = P(("well", "shot"), None, None)
    return jax.shard_map(local, mesh=mesh, in_specs=in_specs, out_specs=out_specs, check_vma=False)
```

```python
import functools
import math

import jax
import jax.numpy as jnp
import ml_dtypes
import numpy as np
from jax import lax
from jax.experimental import pallas as pl
from jax.experimental.pallas import tpu as pltpu
from jax.sharding import PartitionSpec as P

NT = 1024
W = 128
SEC = 16
PARTNERS = 16
PLANE = 8
RECV = 32
OWN_PAIRS = 2
REACH_PAIRS = 10
BLOCKS = REACH_PAIRS + OWN_PAIRS + 1
SEC_REACH = 16
SEC_OWN = 8
CLASSES = 8
SLOTS = 2 * (REACH_PAIRS + OWN_PAIRS)
MESH = pl.DeviceIdType.MESH
f32 = jnp.float32
bf16 = jnp.bfloat16

def packed_table():
    steps = np.arange(2 * W)
    k = np.arange(NT // 2)
    angle = ((steps[:, None] * k[None, :]) % NT).astype(np.float32) * np.float32(2 * math.pi / NT)
    real = np.cos(angle)
    imag = -np.sin(angle)
    imag[:, 0] = np.cos(math.pi * steps)
    scale = np.float32(1.0 / math.sqrt(W))
    return (np.concatenate([real, imag], axis=1) * scale).astype(ml_dtypes.bfloat16)


def place():
    well = lax.axis_index("well")
    shot = lax.axis_index("shot")
    return well // PLANE, well % PLANE, shot // 4, shot % 4


def gather_kernel(
    off_hbm, traces_hbm, gates_hbm, table_hbm, far_hbm, part_hbm,
    near_in, table, gate_vals, spectra, part,
    offs, traces, gates, gate_cols, rows, unit, dealt, held, picked, landed, far_landed, ordered, extra, far_extra,
    load_sem, o_send, o_recv, a_send, a_recv, z_send, z_recv, n_send, n_recv,
    f_send, f_recv, e_send, e_recv, y_send, y_recv, keep_sem, answered,
):
    z, wp, zh, y = place()
    x, core = wp // 2, wp % 2
    well = z * PLANE + wp
    shot = zh * 4 + y
    far_shot = (1 - zh) * 4 + y
    before = jnp.maximum(z - 1, 0)

    steps = [(dx, dc) for dx in (0, 1, 3, 2) for dc in (0, 1)]
    near = [(x + dx) % 4 * 2 + (core + dc) % 2 for dx, dc in steps]
    y_peers = [(y + d) % 4 for d in (1, 3, 2)]

    load_traces = pltpu.make_async_copy(traces_hbm, traces, load_sem.at[3])
    load_traces.start()
    here = pl.multiple_of(z * 256, 256)
    ahead = pl.multiple_of(jnp.minimum(z + 1, 7) * 256, 256)
    load_here = pltpu.make_async_copy(gates_hbm.at[:, pl.ds(here, 256)], gates.at[:, pl.ds(0, 256)], load_sem.at[0])
    load_ahead = pltpu.make_async_copy(gates_hbm.at[:, pl.ds(ahead, 256)], gates.at[:, pl.ds(256, 256)], load_sem.at[1])
    load_off = pltpu.make_async_copy(off_hbm, offs.at[wp], load_sem.at[2])
    load_table = pltpu.make_async_copy(table_hbm, table, load_sem.at[4])
    load_here.start()

    barrier = pltpu.get_barrier_semaphore()

    def greet(to_well, to_shot):
        pl.semaphore_signal(barrier, inc=1, device_id=(to_well, to_shot), device_id_type=MESH)

    @pl.when(z < 7)
    def _():
        for peer in near:
            greet((z + 1) * PLANE + peer, shot)

    for peer in near[1:]:
        greet(z * PLANE + peer, shot)
    for peer in y_peers:
        greet(well, zh * 4 + peer)

    @pl.when(zh == 0)
    def _():
        for peer in near:
            greet(z * PLANE + peer, far_shot)

    def wait_for(more):
        @pl.when(z > 0)
        def _():
            pl.semaphore_wait(barrier, 18 + more)

        @pl.when(z == 0)
        def _():
            pl.semaphore_wait(barrier, 10 + more)

    load_off.start()
    load_ahead.start()
    load_table.start()

    @pl.when(z == 7)
    def _():
        held[pl.ds(16, 16)] = jnp.zeros((16, 16, W), bf16)

    lane = lax.broadcasted_iota(jnp.int32, (RECV, W), 1)
    taper = 0.5 - 0.5 * jnp.cos((lane[:8].astype(f32) + 0.5) * (2 * math.pi / W))
    taper = jnp.concatenate([taper] * (RECV // 8), axis=0)
    load_here.wait()
    gate_cols[...] = jnp.transpose(gates[:, :256].astype(f32))
    columns = gate_cols[pl.ds(pl.multiple_of(wp * RECV, RECV), RECV), :].astype(jnp.int32)
    load_ahead.wait()
    load_off.wait()
    all_gates = gates[...]
    halves = jnp.concatenate([all_gates >> 3, all_gates & 7], axis=0).astype(f32).astype(bf16)
    lanes = lax.broadcasted_iota(jnp.int32, (512, W), 1)
    index = lax.broadcasted_iota(jnp.int32, (512, W), 0)
    for h in (1, 0):
        own = wp * RECV + (zh + h) % 2 * SEC
        start = (own + offs[wp, (zh + h) % 2]) // 2 * 2
        wanted = jnp.where(lanes < 32, start + lanes, own - 32 + lanes)
        one_hot = jnp.where(index == wanted, 1.0, 0.0).astype(bf16)
        block = jnp.dot(halves, one_hot, preferred_element_type=f32)
        extra[h, SEC_OWN] = block.astype(bf16)

    @pl.when(zh == 0)
    def _():
        wait_for(0)

    def remote(source, target, send, receive, to_well, to_shot):
        return pltpu.make_async_remote_copy(
            src_ref=source, dst_ref=target, send_sem=send, recv_sem=receive,
            device_id=(to_well, to_shot), device_id_type=MESH,
        )

    load_traces.wait()

    @pl.when(zh == 1)
    def _():
        wait_for(8)
        for peer in near:
            pl.semaphore_signal(answered, inc=1, device_id=(z * PLANE + peer, far_shot), device_id_type=MESH)

    o_copies = []
    for k in range(1, 8):
        copy = remote(offs.at[wp], offs.at[wp], o_send.at[k], o_recv.at[k], z * PLANE + near[k], shot)
        copy.start()
        o_copies.append(copy)
    for s in range(8):
        data = traces[s].astype(f32)
        gate = jnp.broadcast_to(columns[:, s : s + 1], (RECV, W))
        fine = gate & 127
        tiles = [data[:, k * W : (k + 1) * W] for k in range(8)]
        pick = (gate & 512) != 0
        four = [jnp.where(pick, tiles[k + 4], tiles[k]) for k in range(4)] + [tiles[4]]
        pick = (gate & 256) != 0
        three = [jnp.where(pick, four[k + 2], four[k]) for k in range(3)]
        pick = (gate & 128) != 0
        low = jnp.where(pick, three[1], three[0])
        high = jnp.where(pick, three[2], three[1])
        turned = jnp.where(lane >= fine, low, high)
        for bit in range(3, 7):
            step = 1 << bit
            turned = jnp.where((fine & step) != 0, pltpu.roll(turned, W - step, 1), turned)
        rows[pl.ds(s, RECV, stride=8), :] = turned * jnp.take_along_axis(taper, (lane - (gate & 7)) & 127, axis=1)
    pairs = rows[...].reshape(16, 16, W).astype(bf16)
    unit[...] = pairs
    for i in range(2):
        for m in range(CLASSES):
            dealt[m, i] = pairs[i * CLASSES + m]
    for h in (1, 0):
        extra[h, :SEC_OWN] = unit[pl.ds((zh + h) % 2 * SEC_OWN, SEC_OWN)]

    e_copy = remote(extra.at[1], far_extra, e_send, e_recv, well, far_shot)

    mine = pl.ds(wp * 2, 2)
    mine_ahead = pl.ds(16 + wp * 2, 2)

    def z_copy(k):
        return remote(
            dealt.at[near[k]], held.at[mine_ahead], z_send.at[k], z_recv.at[k], before * PLANE + near[k], shot
        )

    @pl.when(z > 0)
    def _():
        for k in (7, 6, 5, 4, 3, 2, 1, 0):
            z_copy(k).start()

    a_copies = []
    for k in (7, 6, 5, 4, 3, 2, 1):
        to_well = z * PLANE + near[k]
        copy = remote(dealt.at[near[k]], held.at[mine], a_send.at[k], a_recv.at[k], to_well, shot)
        copy.start()
        a_copies.append(copy)
    held[mine] = dealt[wp]

    @pl.when(zh == 1)
    def _():
        e_copy.start()

    for copy in o_copies:
        copy.wait_recv()
    for copy in a_copies:
        copy.wait_recv()

    @pl.when(z < 7)
    def _():
        for k in range(8):
            z_copy(k).wait_recv()

    def pick(h):
        section = (zh + h) % 2
        for k in range(8):
            first = near[k] * 16 + section * SEC_OWN + offs[near[k], section] // 2
            at = (first + (wp + 512 - first) % CLASSES) // CLASSES
            picked[h, k] = held[pl.ds(at, 2)]

    f_copies = []
    for k in (7, 6, 5, 4, 3, 2, 1, 0):
        to_well = z * PLANE + near[k]
        f_copies.append(remote(picked.at[1, k], far_landed.at[wp], f_send.at[k], f_recv.at[k], to_well, far_shot))
    pick(1)

    @pl.when(zh == 1)
    def _():
        for copy in f_copies:
            copy.start()

    pick(0)
    n_copies = []
    for k in (7, 6, 5, 4, 3, 2, 1):
        to_well = z * PLANE + near[k]
        copy = remote(picked.at[0, k], landed.at[wp], n_send.at[k], n_recv.at[k], to_well, shot)
        copy.start()
        n_copies.append(copy)
    landed[wp] = picked[0, 0]

    @pl.when(zh == 0)
    def _():
        pl.semaphore_wait(answered, 8)
        for copy in f_copies:
            copy.start()
        e_copy.start()

    own_first = wp * 16 + zh * SEC_OWN + offs[wp, zh] // 2

    def pass_on(h, kinds):
        more = far_extra if h else extra.at[0]

        def pieces(to_y, target):
            return [
                (ordered.at[h, pl.ds(2 * to_y, REACH_PAIRS)], target.at[pl.ds(0, REACH_PAIRS)]),
                (more.at[pl.ds(2 * to_y, OWN_PAIRS)], target.at[pl.ds(REACH_PAIRS, OWN_PAIRS)]),
                (more.at[pl.ds(SEC_OWN, 1)], target.at[pl.ds(BLOCKS - 1, 1)]),
            ]

        copies = []
        for i, peer in enumerate(y_peers):
            for kind in kinds:
                n = (h * 3 + i) * 3 + kind
                source, to = pieces(peer, far_hbm.at[i] if h else near_in.at[y])[kind]
                copies.append(remote(source, to, y_send.at[n], y_recv.at[n], well, zh * 4 + peer))
        kept = []
        for kind in kinds:
            source, to = pieces(y, near_in.at[4 if h else y])[kind]
            kept.append(pltpu.make_async_copy(source, to, keep_sem.at[h * 3 + kind]))
        for copy in copies + kept:
            copy.start()
        return copies, kept

    def put_in_order(h, arrived):
        for i in range(SEC_REACH):
            ordered[h, i] = arrived[(own_first + i) % CLASSES, i // CLASSES]

    some, kept = pass_on(0, (1, 2))
    for copy in n_copies:
        copy.wait_recv()
    put_in_order(0, landed)
    more, kept_more = pass_on(0, (0,))
    near_copies = some + kept + more + kept_more

    for copy in near_copies:
        copy.wait()
    load_table.wait()
    make_spectra(near_in, (0, 1, 2, 3), table, gate_vals, spectra, y)

    def keep(a, group, reals, imags):
        rows = pl.ds(group * 8, 8)
        for t in range(4):
            part[a, t, rows] = reals[t]
        for t in range(5):
            part[a, 4 + t, rows] = imags[t]

    e_copy.wait_recv()
    some, kept = pass_on(1, (1, 2))
    for copy in f_copies:
        copy.wait_recv()
    put_in_order(1, far_landed)
    more, kept_more = pass_on(1, (0,))
    far_copies = some + more

    for copy in kept + kept_more:
        copy.wait()
    make_spectra(near_in, (4,), table, gate_vals, spectra, y)
    pair_sums(spectra, 5, offs[wp, zh] % 2, keep)
    keep_part = pltpu.make_async_copy(part, part_hbm, load_sem.at[5])
    keep_part.start()
    keep_part.wait()

    @pl.when(z > 0)
    def _():
        for k in range(8):
            z_copy(k).wait_send()

    for copy in a_copies + o_copies + n_copies + f_copies + [e_copy]:
        copy.wait_send()
    for copy in far_copies:
        copy.wait()


def fold(parts):
    row = lax.broadcasted_iota(jnp.int32, (8, W), 0)
    while len(parts) > 1:
        half = len(parts) // 2
        upper = (row & half) == 0
        merged = []
        for i in range(half):
            first, second = parts[i], parts[i + half]
            kept = jnp.where(upper, first, second)
            moved = jnp.where(upper, second, first)
            if half == 4:
                moved = pltpu.roll(moved, 4, 0)
            else:
                moved = jnp.where(upper, pltpu.roll(moved, 8 - half, 0), pltpu.roll(moved, half, 0))
            merged.append(kept + moved)
        parts = merged
    return parts[0]


def make_spectra(data, groups, table, gate_vals, spectra, y):
    lane = lax.broadcasted_iota(jnp.int32, (8, W), 1)
    angle = lane.astype(f32) * (2 * math.pi / W)
    cosines = jnp.cos(angle)
    sines = jnp.sin(angle)
    pairs = {1: 6, 3: 3, 4: 2}[len(groups)]

    for k in groups:
        block = pltpu.roll(data[k, BLOCKS - 1].astype(f32), (W - 4 * y) % W, 1)
        gate = (block[:8] * 8.0 + block[8:]).astype(jnp.int32)
        for slot in range(SLOTS):
            column = slot if slot < 20 else 12 + slot
            gate_vals[slot, k] = jnp.broadcast_to(gate[:, column : column + 1], (8, W))

    @pl.loop(0, SLOTS // 2 // pairs)
    def _(step):
        lefts = []
        for p in range(pairs):
            for k in groups:
                both = data[k, pairs * step + p].astype(f32)
                halves = []
                for par in range(2):
                    window = both[par * 8 : par * 8 + 8]
                    fine = gate_vals[2 * (pairs * step + p) + par, k] & 7
                    low = jnp.where(lane >= fine, window, 0.0)
                    halves.append(jnp.concatenate([low, window - low], axis=1))
                lefts.append(jnp.concatenate(halves, axis=0).astype(bf16))
        flat = jnp.dot(jnp.concatenate(lefts, axis=0), table[...], preferred_element_type=f32)
        first = 0
        for p in range(pairs):
            for k in groups:
                for par in range(2):
                    slot = 2 * (pairs * step + p) + par
                    index = ((gate_vals[slot, k] >> 3) * lane) & 127
                    cosine = jnp.take_along_axis(cosines, index, axis=1)
                    sine = jnp.take_along_axis(sines, index, axis=1)
                    rows = slice(k * 8, k * 8 + 8)
                    for t in range(4):
                        real = flat[first : first + 8, t * W : (t + 1) * W]
                        imag = flat[first : first + 8, (4 + t) * W : (5 + t) * W]
                        spectra[slot, t, 0, rows, :] = cosine * real + sine * imag
                        spectra[slot, t, 1, rows, :] = cosine * imag - sine * real
                    first += 8


def pair_sums(spectra, groups, odd, emit):
    lane = lax.broadcasted_iota(jnp.int32, (8, W), 1)

    @pl.loop(0, 4)
    def _(a):
        reals = [[], []]
        imags = [[], []]
        for t in range(4):
            own = [[spectra[20 + a, t, c, k * 8 : k * 8 + 8, :] for c in range(2)] for k in range(groups)]
            for group in range(2):
                sums = []
                for j in range(8):
                    slot = a + odd + group * 8 + j
                    one = two = three = None
                    for k in range(groups):
                        re = spectra[slot, t, 0, k * 8 : k * 8 + 8, :]
                        im = spectra[slot, t, 1, k * 8 : k * 8 + 8, :]
                        first = own[k][0] * re
                        second = own[k][1] * im
                        third = own[k][0] * im - own[k][1] * re
                        one = first if one is None else one + first
                        two = second if two is None else two + second
                        three = third if three is None else three + third
                    sums.append((one, two, three))
                threes = fold([s[2] for s in sums])
                if t == 0:
                    ones = fold([s[0] for s in sums])
                    twos = fold([s[1] for s in sums])
                    reals[group].append(jnp.where(lane == 0, ones, ones + twos))
                    imags[group].append(twos)
                    imags[group].append(jnp.where(lane == 0, 0.0, threes))
                else:
                    reals[group].append(fold([s[0] + s[1] for s in sums]))
                    imags[group].append(threes)
        for group in range(2):
            emit(a, group, reals[group], imags[group])


def cross_kernel(
    off_hbm, data_hbm, part_hbm, table_hbm, out_hbm, off_ref, data, table, gate_vals, spectra, part, out, sem, out_sem
):
    z, wp, zh, y = place()
    load_data = pltpu.make_async_copy(data_hbm, data, sem.at[0])
    load_data.start()
    load_table = pltpu.make_async_copy(table_hbm, table, sem.at[1])
    load_table.start()
    load_off = pltpu.make_async_copy(off_hbm, off_ref, sem.at[2])
    load_off.start()
    load_part = pltpu.make_async_copy(part_hbm, part, sem.at[3])
    load_part.start()
    load_data.wait()
    load_table.wait()
    lane = lax.broadcasted_iota(jnp.int32, (8, W), 1)
    make_spectra(data, (0, 1, 2), table, gate_vals, spectra, y)

    def finish(a, group, reals, imags):
        rows = pl.ds(group * 8, 8)
        for t in range(4):
            out[a, rows, t * W : (t + 1) * W] = reals[t] + part[a, t, rows]
        imags = [imags[t] + part[a, 4 + t, rows] for t in range(5)]
        before = imags[0]
        for t in range(4):
            turned = pltpu.roll(imags[1 + t], 1, 1)
            out[a, rows, (4 + t) * W : (5 + t) * W] = jnp.where(lane == 0, before, turned)
            before = turned
        out[a, rows, 8 * W : 8 * W + 2] = jnp.where(lane == 0, before, 0.0)[:, :2]
        if group == 1:
            pltpu.make_async_copy(out.at[a], out_hbm.at[a], out_sem.at[a]).start()

    load_off.wait()
    load_part.wait()
    pair_sums(spectra, 3, off_ref[zh] & 1, finish)
    for a in range(4):
        pltpu.make_async_copy(out.at[a], out_hbm.at[a], out_sem.at[a]).wait()


def local(traces, gate_starts, section_offsets):
    hbm = pl.BlockSpec(memory_space=pltpu.HBM)
    any_space = pl.BlockSpec(memory_space=pl.ANY)
    dma = pltpu.SemaphoreType.DMA
    table = jnp.asarray(packed_table())
    far, part = pl.pallas_call(
        gather_kernel,
        out_shape=(
            jax.ShapeDtypeStruct((3, BLOCKS, 16, W), bf16),
            jax.ShapeDtypeStruct((4, 9, PARTNERS, W), f32),
        ),
        in_specs=[hbm, hbm, hbm, any_space],
        out_specs=(any_space, any_space),
        scratch_shapes=[
            pltpu.VMEM((5, BLOCKS, 16, W), bf16),
            pltpu.VMEM((2 * W, NT), bf16),
            pltpu.VMEM((SLOTS, 5, 8, W), jnp.int32),
            pltpu.VMEM((SLOTS, 4, 2, 40, W), f32),
            pltpu.VMEM((4, 9, PARTNERS, W), f32),
            pltpu.SMEM((PLANE, 2), jnp.int32),
            pltpu.VMEM((8, RECV, NT), bf16),
            pltpu.VMEM((8, 512), jnp.int32),
            pltpu.VMEM((256, 8), f32),
            pltpu.VMEM((RECV * 8, W), f32),
            pltpu.VMEM((16, 16, W), bf16),
            pltpu.VMEM((CLASSES, 2, 16, W), bf16),
            pltpu.VMEM((32, 16, W), bf16),
            pltpu.VMEM((2, PLANE, 2, 16, W), bf16),
            pltpu.VMEM((CLASSES, 2, 16, W), bf16),
            pltpu.VMEM((CLASSES, 2, 16, W), bf16),
            pltpu.VMEM((2, SEC_REACH, 16, W), bf16),
            pltpu.VMEM((2, SEC_OWN + 1, 16, W), bf16),
            pltpu.VMEM((SEC_OWN + 1, 16, W), bf16),
            dma((6,)), dma((8,)), dma((8,)), dma((8,)), dma((8,)), dma((8,)), dma((8,)),
            dma((8,)), dma((8,)), dma((8,)), dma((8,)), dma, dma, dma((18,)), dma((18,)), dma((6,)),
            pltpu.SemaphoreType.REGULAR,
        ],
        compiler_params=pltpu.CompilerParams(
            collective_id=0, has_side_effects=True, vmem_limit_bytes=60 * 2**20
        ),
        name="gather",
    )(section_offsets, traces, gate_starts, table)
    return cross_call(section_offsets, far, part, table)


def cross_call(section_offsets, far, part, table):
    any_space = pl.BlockSpec(memory_space=pl.ANY)
    dma = pltpu.SemaphoreType.DMA
    return pl.pallas_call(
        cross_kernel,
        out_shape=jax.ShapeDtypeStruct((4, PARTNERS, NT + 2), f32),
        in_specs=[any_space, any_space, any_space, any_space],
        out_specs=any_space,
        scratch_shapes=[
            pltpu.SMEM((2,), jnp.int32),
            pltpu.VMEM((3, BLOCKS, 16, W), bf16),
            pltpu.VMEM((2 * W, NT), bf16),
            pltpu.VMEM((SLOTS, 3, 8, W), jnp.int32),
            pltpu.VMEM((SLOTS, 4, 2, 24, W), f32),
            pltpu.VMEM((4, 9, PARTNERS, W), f32),
            pltpu.VMEM((4, PARTNERS, NT + 2), f32),
            dma((4,)), dma((4,)),
        ],
        compiler_params=pltpu.CompilerParams(vmem_limit_bytes=60 * 2**20),
        name="cross",
    )(section_offsets, far, part, table)


def solution(mesh):
    in_specs = (P("shot", "well", None), P("shot", None), P("well"))
    out_specs = P(("well", "shot"), None, None)
    return jax.shard_map(local, mesh=mesh, in_specs=in_specs, out_specs=out_specs, check_vma=False)
```

```python
import functools
import math

import jax
import jax.numpy as jnp
import ml_dtypes
import numpy as np
from jax import lax
from jax.experimental import pallas as pl
from jax.experimental.pallas import tpu as pltpu
from jax.sharding import PartitionSpec as P

NT = 1024
W = 128
SEC = 16
PARTNERS = 16
PLANE = 8
RECV = 32
OWN_PAIRS = 2
REACH_PAIRS = 10
BLOCKS = REACH_PAIRS + OWN_PAIRS + 1
SEC_REACH = 16
SEC_OWN = 8
CLASSES = 8
SLOTS = 2 * (REACH_PAIRS + OWN_PAIRS)
MESH = pl.DeviceIdType.MESH
f32 = jnp.float32
bf16 = jnp.bfloat16

def packed_table():
    steps = np.arange(2 * W)
    k = np.arange(NT // 2)
    angle = ((steps[:, None] * k[None, :]) % NT).astype(np.float32) * np.float32(2 * math.pi / NT)
    real = np.cos(angle)
    imag = -np.sin(angle)
    imag[:, 0] = np.cos(math.pi * steps)
    scale = np.float32(1.0 / math.sqrt(W))
    return (np.concatenate([real, imag], axis=1) * scale).astype(ml_dtypes.bfloat16)


def place():
    well = lax.axis_index("well")
    shot = lax.axis_index("shot")
    return well // PLANE, well % PLANE, shot // 4, shot % 4


def gather_kernel(
    off_hbm, traces_hbm, gates_hbm, table_hbm, far_hbm, part_hbm,
    near_in, table, gate_vals, spectra, part,
    offs, traces, gates, gate_cols, rows, unit, dealt, held, picked, landed, far_landed, ordered, extra, far_extra,
    load_sem, o_send, o_recv, a_send, a_recv, z_send, z_recv, n_send, n_recv,
    f_send, f_recv, e_send, e_recv, y_send, y_recv, keep_sem, answered,
):
    z, wp, zh, y = place()
    x, core = wp // 2, wp % 2
    well = z * PLANE + wp
    shot = zh * 4 + y
    far_shot = (1 - zh) * 4 + y
    before = jnp.maximum(z - 1, 0)

    steps = [(dx, dc) for dx in (0, 1, 3, 2) for dc in (0, 1)]
    near = [(x + dx) % 4 * 2 + (core + dc) % 2 for dx, dc in steps]
    y_peers = [(y + d) % 4 for d in (1, 3, 2)]

    load_traces = pltpu.make_async_copy(traces_hbm, traces, load_sem.at[3])
    load_traces.start()
    here = pl.multiple_of(z * 256, 256)
    ahead = pl.multiple_of(jnp.minimum(z + 1, 7) * 256, 256)
    load_here = pltpu.make_async_copy(gates_hbm.at[:, pl.ds(here, 256)], gates.at[:, pl.ds(0, 256)], load_sem.at[0])
    load_ahead = pltpu.make_async_copy(gates_hbm.at[:, pl.ds(ahead, 256)], gates.at[:, pl.ds(256, 256)], load_sem.at[1])
    load_off = pltpu.make_async_copy(off_hbm, offs.at[wp], load_sem.at[2])
    load_table = pltpu.make_async_copy(table_hbm, table, load_sem.at[4])
    load_here.start()

    barrier = pltpu.get_barrier_semaphore()

    def greet(to_well, to_shot):
        pl.semaphore_signal(barrier, inc=1, device_id=(to_well, to_shot), device_id_type=MESH)

    @pl.when(z < 7)
    def _():
        for peer in near:
            greet((z + 1) * PLANE + peer, shot)

    for peer in near[1:]:
        greet(z * PLANE + peer, shot)
    for peer in y_peers:
        greet(well, zh * 4 + peer)

    @pl.when(zh == 0)
    def _():
        for peer in near:
            greet(z * PLANE + peer, far_shot)

    def wait_for(more):
        @pl.when(z > 0)
        def _():
            pl.semaphore_wait(barrier, 18 + more)

        @pl.when(z == 0)
        def _():
            pl.semaphore_wait(barrier, 10 + more)

    load_off.start()
    load_ahead.start()
    load_table.start()

    @pl.when(z == 7)
    def _():
        held[pl.ds(16, 16)] = jnp.zeros((16, 16, W), bf16)

    lane = lax.broadcasted_iota(jnp.int32, (RECV, W), 1)
    taper = 0.5 - 0.5 * jnp.cos((lane[:8].astype(f32) + 0.5) * (2 * math.pi / W))
    taper = jnp.concatenate([taper] * (RECV // 8), axis=0)
    load_here.wait()
    gate_cols[...] = jnp.transpose(gates[:, :256].astype(f32))
    columns = gate_cols[pl.ds(pl.multiple_of(wp * RECV, RECV), RECV), :].astype(jnp.int32)
    load_ahead.wait()
    load_off.wait()
    all_gates = gates[...]
    halves = jnp.concatenate([all_gates >> 3, all_gates & 7], axis=0).astype(f32).astype(bf16)
    lanes = lax.broadcasted_iota(jnp.int32, (512, W), 1)
    index = lax.broadcasted_iota(jnp.int32, (512, W), 0)
    for h in (1, 0):
        own = wp * RECV + (zh + h) % 2 * SEC
        start = (own + offs[wp, (zh + h) % 2]) // 2 * 2
        wanted = jnp.where(lanes < 32, start + lanes, own - 32 + lanes)
        one_hot = jnp.where(index == wanted, 1.0, 0.0).astype(bf16)
        block = jnp.dot(halves, one_hot, preferred_element_type=f32)
        extra[h, SEC_OWN] = block.astype(bf16)

    @pl.when(zh == 0)
    def _():
        wait_for(0)

    def remote(source, target, send, receive, to_well, to_shot):
        return pltpu.make_async_remote_copy(
            src_ref=source, dst_ref=target, send_sem=send, recv_sem=receive,
            device_id=(to_well, to_shot), device_id_type=MESH,
        )

    load_traces.wait()

    @pl.when(zh == 1)
    def _():
        wait_for(8)
        for peer in near:
            pl.semaphore_signal(answered, inc=1, device_id=(z * PLANE + peer, far_shot), device_id_type=MESH)

    o_copies = []
    for k in range(1, 8):
        copy = remote(offs.at[wp], offs.at[wp], o_send.at[k], o_recv.at[k], z * PLANE + near[k], shot)
        copy.start()
        o_copies.append(copy)
    for s in range(8):
        data = traces[s].astype(f32)
        gate = jnp.broadcast_to(columns[:, s : s + 1], (RECV, W))
        fine = gate & 127
        tiles = [data[:, k * W : (k + 1) * W] for k in range(8)]
        pick = (gate & 512) != 0
        four = [jnp.where(pick, tiles[k + 4], tiles[k]) for k in range(4)] + [tiles[4]]
        pick = (gate & 256) != 0
        three = [jnp.where(pick, four[k + 2], four[k]) for k in range(3)]
        pick = (gate & 128) != 0
        low = jnp.where(pick, three[1], three[0])
        high = jnp.where(pick, three[2], three[1])
        turned = jnp.where(lane >= fine, low, high)
        for bit in range(3, 7):
            step = 1 << bit
            turned = jnp.where((fine & step) != 0, pltpu.roll(turned, W - step, 1), turned)
        rows[pl.ds(s, RECV, stride=8), :] = turned * jnp.take_along_axis(taper, (lane - (gate & 7)) & 127, axis=1)
    pairs = rows[...].reshape(16, 16, W).astype(bf16)
    unit[...] = pairs
    for i in range(2):
        for m in range(CLASSES):
            dealt[m, i] = pairs[i * CLASSES + m]
    for h in (1, 0):
        extra[h, :SEC_OWN] = unit[pl.ds((zh + h) % 2 * SEC_OWN, SEC_OWN)]

    e_copy = remote(extra.at[1], far_extra, e_send, e_recv, well, far_shot)

    mine = pl.ds(wp * 2, 2)
    mine_ahead = pl.ds(16 + wp * 2, 2)

    def z_copy(k):
        return remote(
            dealt.at[near[k]], held.at[mine_ahead], z_send.at[k], z_recv.at[k], before * PLANE + near[k], shot
        )

    @pl.when(z > 0)
    def _():
        for k in (7, 6, 5, 4, 3, 2, 1, 0):
            z_copy(k).start()

    a_copies = []
    for k in (7, 6, 5, 4, 3, 2, 1):
        to_well = z * PLANE + near[k]
        copy = remote(dealt.at[near[k]], held.at[mine], a_send.at[k], a_recv.at[k], to_well, shot)
        copy.start()
        a_copies.append(copy)
    held[mine] = dealt[wp]

    @pl.when(zh == 1)
    def _():
        e_copy.start()

    for copy in o_copies:
        copy.wait_recv()
    for copy in a_copies:
        copy.wait_recv()

    @pl.when(z < 7)
    def _():
        for k in range(8):
            z_copy(k).wait_recv()

    def pick(h):
        section = (zh + h) % 2
        for k in range(8):
            first = near[k] * 16 + section * SEC_OWN + offs[near[k], section] // 2
            at = (first + (wp + 512 - first) % CLASSES) // CLASSES
            picked[h, k] = held[pl.ds(at, 2)]

    f_copies = []
    for k in (7, 6, 5, 4, 3, 2, 1, 0):
        to_well = z * PLANE + near[k]
        f_copies.append(remote(picked.at[1, k], far_landed.at[wp], f_send.at[k], f_recv.at[k], to_well, far_shot))
    pick(1)

    @pl.when(zh == 1)
    def _():
        for copy in f_copies:
            copy.start()

    pick(0)
    n_copies = []
    for k in (7, 6, 5, 4, 3, 2, 1):
        to_well = z * PLANE + near[k]
        copy = remote(picked.at[0, k], landed.at[wp], n_send.at[k], n_recv.at[k], to_well, shot)
        copy.start()
        n_copies.append(copy)
    landed[wp] = picked[0, 0]

    @pl.when(zh == 0)
    def _():
        pl.semaphore_wait(answered, 8)
        for copy in f_copies:
            copy.start()
        e_copy.start()

    own_first = wp * 16 + zh * SEC_OWN + offs[wp, zh] // 2

    def pass_on(h, kinds):
        more = far_extra if h else extra.at[0]

        def pieces(to_y, target):
            return [
                (ordered.at[h, pl.ds(2 * to_y, REACH_PAIRS)], target.at[pl.ds(0, REACH_PAIRS)]),
                (more.at[pl.ds(2 * to_y, OWN_PAIRS)], target.at[pl.ds(REACH_PAIRS, OWN_PAIRS)]),
                (more.at[pl.ds(SEC_OWN, 1)], target.at[pl.ds(BLOCKS - 1, 1)]),
            ]

        copies = []
        for i, peer in enumerate(y_peers):
            for kind in kinds:
                n = (h * 3 + i) * 3 + kind
                source, to = pieces(peer, far_hbm.at[i] if h else near_in.at[y])[kind]
                copies.append(remote(source, to, y_send.at[n], y_recv.at[n], well, zh * 4 + peer))
        kept = []
        for kind in kinds:
            source, to = pieces(y, near_in.at[4 if h else y])[kind]
            kept.append(pltpu.make_async_copy(source, to, keep_sem.at[h * 3 + kind]))
        for copy in copies + kept:
            copy.start()
        return copies, kept

    def put_in_order(h, arrived):
        for i in range(SEC_REACH):
            ordered[h, i] = arrived[(own_first + i) % CLASSES, i // CLASSES]

    some, kept = pass_on(0, (1, 2))
    for copy in n_copies:
        copy.wait_recv()
    put_in_order(0, landed)
    more, kept_more = pass_on(0, (0,))
    near_copies = some + kept + more + kept_more

    for copy in near_copies:
        copy.wait()
    load_table.wait()
    make_spectra(near_in, (0, 1, 2, 3), table, gate_vals, spectra, y)

    def keep(a, group, reals, imags):
        rows = pl.ds(group * 8, 8)
        for t in range(4):
            part[a, t, rows] = reals[t]
        for t in range(5):
            part[a, 4 + t, rows] = imags[t]

    e_copy.wait_recv()
    some, kept = pass_on(1, (1, 2))
    for copy in f_copies:
        copy.wait_recv()
    put_in_order(1, far_landed)
    more, kept_more = pass_on(1, (0,))
    far_copies = some + more

    for copy in kept + kept_more:
        copy.wait()
    make_spectra(near_in, (4,), table, gate_vals, spectra, y)
    pair_sums(spectra, 5, offs[wp, zh] % 2, keep)
    keep_part = pltpu.make_async_copy(part, part_hbm, load_sem.at[5])
    keep_part.start()
    keep_part.wait()

    @pl.when(z > 0)
    def _():
        for k in range(8):
            z_copy(k).wait_send()

    for copy in a_copies + o_copies + n_copies + f_copies + [e_copy]:
        copy.wait_send()
    for copy in far_copies:
        copy.wait()


def fold(parts):
    row = lax.broadcasted_iota(jnp.int32, (8, W), 0)
    while len(parts) > 1:
        half = len(parts) // 2
        upper = (row & half) == 0
        merged = []
        for i in range(half):
            first, second = parts[i], parts[i + half]
            kept = jnp.where(upper, first, second)
            moved = jnp.where(upper, second, first)
            if half == 4:
                moved = pltpu.roll(moved, 4, 0)
            else:
                moved = jnp.where(upper, pltpu.roll(moved, 8 - half, 0), pltpu.roll(moved, half, 0))
            merged.append(kept + moved)
        parts = merged
    return parts[0]


def make_spectra(data, groups, table, gate_vals, spectra, y, unroll=False):
    lane = lax.broadcasted_iota(jnp.int32, (8, W), 1)
    angle = lane.astype(f32) * (2 * math.pi / W)
    cosines = jnp.cos(angle)
    sines = jnp.sin(angle)
    pairs = {1: 6, 3: 3, 4: 2}[len(groups)]

    for k in groups:
        block = pltpu.roll(data[k, BLOCKS - 1].astype(f32), (W - 4 * y) % W, 1)
        gate = (block[:8] * 8.0 + block[8:]).astype(jnp.int32)
        for slot in range(SLOTS):
            column = slot if slot < 20 else 12 + slot
            gate_vals[slot, k] = jnp.broadcast_to(gate[:, column : column + 1], (8, W))

    @pl.loop(0, SLOTS // 2 // pairs, unroll=unroll)
    def _(step):
        lefts = []
        for p in range(pairs):
            for k in groups:
                both = data[k, pairs * step + p].astype(f32)
                halves = []
                for par in range(2):
                    window = both[par * 8 : par * 8 + 8]
                    fine = gate_vals[2 * (pairs * step + p) + par, k] & 7
                    low = jnp.where(lane >= fine, window, 0.0)
                    halves.append(jnp.concatenate([low, window - low], axis=1))
                lefts.append(jnp.concatenate(halves, axis=0).astype(bf16))
        flat = jnp.dot(jnp.concatenate(lefts, axis=0), table[...], preferred_element_type=f32)
        first = 0
        for p in range(pairs):
            for k in groups:
                for par in range(2):
                    slot = 2 * (pairs * step + p) + par
                    index = ((gate_vals[slot, k] >> 3) * lane) & 127
                    cosine = jnp.take_along_axis(cosines, index, axis=1)
                    sine = jnp.take_along_axis(sines, index, axis=1)
                    rows = slice(k * 8, k * 8 + 8)
                    for t in range(4):
                        real = flat[first : first + 8, t * W : (t + 1) * W]
                        imag = flat[first : first + 8, (4 + t) * W : (5 + t) * W]
                        spectra[slot, t, 0, rows, :] = cosine * real + sine * imag
                        spectra[slot, t, 1, rows, :] = cosine * imag - sine * real
                    first += 8


def pair_sums(spectra, groups, odd, emit):
    lane = lax.broadcasted_iota(jnp.int32, (8, W), 1)

    @pl.loop(0, 4)
    def _(a):
        reals = [[], []]
        imags = [[], []]
        for t in range(4):
            own = [[spectra[20 + a, t, c, k * 8 : k * 8 + 8, :] for c in range(2)] for k in range(groups)]
            for group in range(2):
                sums = []
                for j in range(8):
                    slot = a + odd + group * 8 + j
                    one = two = three = None
                    for k in range(groups):
                        re = spectra[slot, t, 0, k * 8 : k * 8 + 8, :]
                        im = spectra[slot, t, 1, k * 8 : k * 8 + 8, :]
                        first = own[k][0] * re
                        second = own[k][1] * im
                        third = own[k][0] * im - own[k][1] * re
                        one = first if one is None else one + first
                        two = second if two is None else two + second
                        three = third if three is None else three + third
                    sums.append((one, two, three))
                threes = fold([s[2] for s in sums])
                if t == 0:
                    ones = fold([s[0] for s in sums])
                    twos = fold([s[1] for s in sums])
                    reals[group].append(jnp.where(lane == 0, ones, ones + twos))
                    imags[group].append(twos)
                    imags[group].append(jnp.where(lane == 0, 0.0, threes))
                else:
                    reals[group].append(fold([s[0] + s[1] for s in sums]))
                    imags[group].append(threes)
        for group in range(2):
            emit(a, group, reals[group], imags[group])


def cross_kernel(
    off_hbm, data_hbm, part_hbm, table_hbm, out_hbm, off_ref, data, table, gate_vals, spectra, part, out, sem, out_sem
):
    z, wp, zh, y = place()
    load_data = pltpu.make_async_copy(data_hbm, data, sem.at[0])
    load_data.start()
    load_table = pltpu.make_async_copy(table_hbm, table, sem.at[1])
    load_table.start()
    load_off = pltpu.make_async_copy(off_hbm, off_ref, sem.at[2])
    load_off.start()
    load_part = pltpu.make_async_copy(part_hbm, part, sem.at[3])
    load_part.start()
    load_data.wait()
    load_table.wait()
    lane = lax.broadcasted_iota(jnp.int32, (8, W), 1)
    make_spectra(data, (0, 1, 2), table, gate_vals, spectra, y, unroll=True)

    def finish(a, group, reals, imags):
        rows = pl.ds(group * 8, 8)
        for t in range(4):
            out[a, rows, t * W : (t + 1) * W] = reals[t] + part[a, t, rows]
        imags = [imags[t] + part[a, 4 + t, rows] for t in range(5)]
        before = imags[0]
        for t in range(4):
            turned = pltpu.roll(imags[1 + t], 1, 1)
            out[a, rows, (4 + t) * W : (5 + t) * W] = jnp.where(lane == 0, before, turned)
            before = turned
        out[a, rows, 8 * W : 8 * W + 2] = jnp.where(lane == 0, before, 0.0)[:, :2]
        if group == 1:
            pltpu.make_async_copy(out.at[a], out_hbm.at[a], out_sem.at[a]).start()

    load_off.wait()
    load_part.wait()
    pair_sums(spectra, 3, off_ref[zh] & 1, finish)
    for a in range(4):
        pltpu.make_async_copy(out.at[a], out_hbm.at[a], out_sem.at[a]).wait()


def local(traces, gate_starts, section_offsets):
    hbm = pl.BlockSpec(memory_space=pltpu.HBM)
    any_space = pl.BlockSpec(memory_space=pl.ANY)
    dma = pltpu.SemaphoreType.DMA
    table = jnp.asarray(packed_table())
    far, part = pl.pallas_call(
        gather_kernel,
        out_shape=(
            jax.ShapeDtypeStruct((3, BLOCKS, 16, W), bf16),
            jax.ShapeDtypeStruct((4, 9, PARTNERS, W), f32),
        ),
        in_specs=[hbm, hbm, hbm, any_space],
        out_specs=(any_space, any_space),
        scratch_shapes=[
            pltpu.VMEM((5, BLOCKS, 16, W), bf16),
            pltpu.VMEM((2 * W, NT), bf16),
            pltpu.VMEM((SLOTS, 5, 8, W), jnp.int32),
            pltpu.VMEM((SLOTS, 4, 2, 40, W), f32),
            pltpu.VMEM((4, 9, PARTNERS, W), f32),
            pltpu.SMEM((PLANE, 2), jnp.int32),
            pltpu.VMEM((8, RECV, NT), bf16),
            pltpu.VMEM((8, 512), jnp.int32),
            pltpu.VMEM((256, 8), f32),
            pltpu.VMEM((RECV * 8, W), f32),
            pltpu.VMEM((16, 16, W), bf16),
            pltpu.VMEM((CLASSES, 2, 16, W), bf16),
            pltpu.VMEM((32, 16, W), bf16),
            pltpu.VMEM((2, PLANE, 2, 16, W), bf16),
            pltpu.VMEM((CLASSES, 2, 16, W), bf16),
            pltpu.VMEM((CLASSES, 2, 16, W), bf16),
            pltpu.VMEM((2, SEC_REACH, 16, W), bf16),
            pltpu.VMEM((2, SEC_OWN + 1, 16, W), bf16),
            pltpu.VMEM((SEC_OWN + 1, 16, W), bf16),
            dma((6,)), dma((8,)), dma((8,)), dma((8,)), dma((8,)), dma((8,)), dma((8,)),
            dma((8,)), dma((8,)), dma((8,)), dma((8,)), dma, dma, dma((18,)), dma((18,)), dma((6,)),
            pltpu.SemaphoreType.REGULAR,
        ],
        compiler_params=pltpu.CompilerParams(
            collective_id=0, has_side_effects=True, vmem_limit_bytes=60 * 2**20
        ),
        name="gather",
    )(section_offsets, traces, gate_starts, table)
    return cross_call(section_offsets, far, part, table)


def cross_call(section_offsets, far, part, table):
    any_space = pl.BlockSpec(memory_space=pl.ANY)
    dma = pltpu.SemaphoreType.DMA
    return pl.pallas_call(
        cross_kernel,
        out_shape=jax.ShapeDtypeStruct((4, PARTNERS, NT + 2), f32),
        in_specs=[any_space, any_space, any_space, any_space],
        out_specs=any_space,
        scratch_shapes=[
            pltpu.SMEM((2,), jnp.int32),
            pltpu.VMEM((3, BLOCKS, 16, W), bf16),
            pltpu.VMEM((2 * W, NT), bf16),
            pltpu.VMEM((SLOTS, 3, 8, W), jnp.int32),
            pltpu.VMEM((SLOTS, 4, 2, 24, W), f32),
            pltpu.VMEM((4, 9, PARTNERS, W), f32),
            pltpu.VMEM((4, PARTNERS, NT + 2), f32),
            dma((4,)), dma((4,)),
        ],
        compiler_params=pltpu.CompilerParams(vmem_limit_bytes=60 * 2**20),
        name="cross",
    )(section_offsets, far, part, table)


def solution(mesh):
    in_specs = (P("shot", "well", None), P("shot", None), P("well"))
    out_specs = P(("well", "shot"), None, None)
    return jax.shard_map(local, mesh=mesh, in_specs=in_specs, out_specs=out_specs, check_vma=False)
```

```python
import functools
import math

import jax
import jax.numpy as jnp
import ml_dtypes
import numpy as np
from jax import lax
from jax.experimental import pallas as pl
from jax.experimental.pallas import tpu as pltpu
from jax.sharding import PartitionSpec as P

NT = 1024
W = 128
SEC = 16
PARTNERS = 16
PLANE = 8
RECV = 32
OWN_PAIRS = 2
REACH_PAIRS = 10
BLOCKS = REACH_PAIRS + OWN_PAIRS + 1
SEC_REACH = 16
SEC_OWN = 8
CLASSES = 8
SLOTS = 2 * (REACH_PAIRS + OWN_PAIRS)
MESH = pl.DeviceIdType.MESH
f32 = jnp.float32
bf16 = jnp.bfloat16

def packed_table():
    steps = np.arange(2 * W)
    k = np.arange(NT // 2)
    angle = ((steps[:, None] * k[None, :]) % NT).astype(np.float32) * np.float32(2 * math.pi / NT)
    real = np.cos(angle)
    imag = -np.sin(angle)
    imag[:, 0] = np.cos(math.pi * steps)
    scale = np.float32(1.0 / math.sqrt(W))
    return (np.concatenate([real, imag], axis=1) * scale).astype(ml_dtypes.bfloat16)


def place():
    well = lax.axis_index("well")
    shot = lax.axis_index("shot")
    return well // PLANE, well % PLANE, shot // 4, shot % 4


def gather_kernel(
    off_hbm, traces_hbm, gates_hbm, table_hbm, far_hbm, part_hbm,
    near_in, table, gate_vals, spectra, part,
    offs, traces, gates, gate_cols, rows, unit, dealt, held, picked, landed, far_landed, ordered, extra, far_extra,
    load_sem, o_send, o_recv, a_send, a_recv, z_send, z_recv, n_send, n_recv,
    f_send, f_recv, e_send, e_recv, y_send, y_recv, keep_sem, answered,
):
    z, wp, zh, y = place()
    x, core = wp // 2, wp % 2
    well = z * PLANE + wp
    shot = zh * 4 + y
    far_shot = (1 - zh) * 4 + y
    before = jnp.maximum(z - 1, 0)

    steps = [(dx, dc) for dx in (0, 1, 3, 2) for dc in (0, 1)]
    near = [(x + dx) % 4 * 2 + (core + dc) % 2 for dx, dc in steps]
    y_peers = [(y + d) % 4 for d in (2, 1, 3)]

    load_traces = pltpu.make_async_copy(traces_hbm, traces, load_sem.at[3])
    load_traces.start()
    here = pl.multiple_of(z * 256, 256)
    ahead = pl.multiple_of(jnp.minimum(z + 1, 7) * 256, 256)
    load_here = pltpu.make_async_copy(gates_hbm.at[:, pl.ds(here, 256)], gates.at[:, pl.ds(0, 256)], load_sem.at[0])
    load_ahead = pltpu.make_async_copy(gates_hbm.at[:, pl.ds(ahead, 256)], gates.at[:, pl.ds(256, 256)], load_sem.at[1])
    load_off = pltpu.make_async_copy(off_hbm, offs.at[wp], load_sem.at[2])
    load_table = pltpu.make_async_copy(table_hbm, table, load_sem.at[4])
    load_here.start()

    barrier = pltpu.get_barrier_semaphore()

    def greet(to_well, to_shot):
        pl.semaphore_signal(barrier, inc=1, device_id=(to_well, to_shot), device_id_type=MESH)

    @pl.when(z < 7)
    def _():
        for peer in near:
            greet((z + 1) * PLANE + peer, shot)

    for peer in near[1:]:
        greet(z * PLANE + peer, shot)
    for peer in y_peers:
        greet(well, zh * 4 + peer)

    @pl.when(zh == 0)
    def _():
        for peer in near:
            greet(z * PLANE + peer, far_shot)

    def wait_for(more):
        @pl.when(z > 0)
        def _():
            pl.semaphore_wait(barrier, 18 + more)

        @pl.when(z == 0)
        def _():
            pl.semaphore_wait(barrier, 10 + more)

    load_off.start()
    load_ahead.start()
    load_table.start()

    @pl.when(z == 7)
    def _():
        held[pl.ds(16, 16)] = jnp.zeros((16, 16, W), bf16)

    lane = lax.broadcasted_iota(jnp.int32, (RECV, W), 1)
    taper = 0.5 - 0.5 * jnp.cos((lane[:8].astype(f32) + 0.5) * (2 * math.pi / W))
    taper = jnp.concatenate([taper] * (RECV // 8), axis=0)
    load_here.wait()
    gate_cols[...] = jnp.transpose(gates[:, :256].astype(f32))
    columns = gate_cols[pl.ds(pl.multiple_of(wp * RECV, RECV), RECV), :].astype(jnp.int32)
    load_ahead.wait()
    load_off.wait()
    all_gates = gates[...]
    halves = jnp.concatenate([all_gates >> 3, all_gates & 7], axis=0).astype(f32).astype(bf16)
    lanes = lax.broadcasted_iota(jnp.int32, (512, W), 1)
    index = lax.broadcasted_iota(jnp.int32, (512, W), 0)
    for h in (1, 0):
        own = wp * RECV + (zh + h) % 2 * SEC
        start = (own + offs[wp, (zh + h) % 2]) // 2 * 2
        wanted = jnp.where(lanes < 32, start + lanes, own - 32 + lanes)
        one_hot = jnp.where(index == wanted, 1.0, 0.0).astype(bf16)
        block = jnp.dot(halves, one_hot, preferred_element_type=f32)
        extra[h, SEC_OWN] = block.astype(bf16)

    @pl.when(zh == 0)
    def _():
        wait_for(0)

    def remote(source, target, send, receive, to_well, to_shot):
        return pltpu.make_async_remote_copy(
            src_ref=source, dst_ref=target, send_sem=send, recv_sem=receive,
            device_id=(to_well, to_shot), device_id_type=MESH,
        )

    load_traces.wait()

    @pl.when(zh == 1)
    def _():
        wait_for(8)
        for peer in near:
            pl.semaphore_signal(answered, inc=1, device_id=(z * PLANE + peer, far_shot), device_id_type=MESH)

    o_copies = []
    for k in range(1, 8):
        copy = remote(offs.at[wp], offs.at[wp], o_send.at[k], o_recv.at[k], z * PLANE + near[k], shot)
        copy.start()
        o_copies.append(copy)
    for s in range(8):
        data = traces[s].astype(f32)
        gate = jnp.broadcast_to(columns[:, s : s + 1], (RECV, W))
        fine = gate & 127
        tiles = [data[:, k * W : (k + 1) * W] for k in range(8)]
        pick = (gate & 512) != 0
        four = [jnp.where(pick, tiles[k + 4], tiles[k]) for k in range(4)] + [tiles[4]]
        pick = (gate & 256) != 0
        three = [jnp.where(pick, four[k + 2], four[k]) for k in range(3)]
        pick = (gate & 128) != 0
        low = jnp.where(pick, three[1], three[0])
        high = jnp.where(pick, three[2], three[1])
        turned = jnp.where(lane >= fine, low, high)
        for bit in range(3, 7):
            step = 1 << bit
            turned = jnp.where((fine & step) != 0, pltpu.roll(turned, W - step, 1), turned)
        rows[pl.ds(s, RECV, stride=8), :] = turned * jnp.take_along_axis(taper, (lane - (gate & 7)) & 127, axis=1)
    pairs = rows[...].reshape(16, 16, W).astype(bf16)
    unit[...] = pairs
    for i in range(2):
        for m in range(CLASSES):
            dealt[m, i] = pairs[i * CLASSES + m]
    for h in (1, 0):
        extra[h, :SEC_OWN] = unit[pl.ds((zh + h) % 2 * SEC_OWN, SEC_OWN)]

    e_copy = remote(extra.at[1], far_extra, e_send, e_recv, well, far_shot)

    mine = pl.ds(wp * 2, 2)
    mine_ahead = pl.ds(16 + wp * 2, 2)

    def z_copy(k):
        return remote(
            dealt.at[near[k]], held.at[mine_ahead], z_send.at[k], z_recv.at[k], before * PLANE + near[k], shot
        )

    @pl.when(z > 0)
    def _():
        for k in (7, 6, 5, 4, 3, 2, 1, 0):
            z_copy(k).start()

    a_copies = []
    for k in (7, 6, 5, 4, 3, 2, 1):
        to_well = z * PLANE + near[k]
        copy = remote(dealt.at[near[k]], held.at[mine], a_send.at[k], a_recv.at[k], to_well, shot)
        copy.start()
        a_copies.append(copy)
    held[mine] = dealt[wp]

    @pl.when(zh == 1)
    def _():
        e_copy.start()

    for copy in o_copies:
        copy.wait_recv()
    for copy in a_copies:
        copy.wait_recv()

    @pl.when(z < 7)
    def _():
        for k in range(8):
            z_copy(k).wait_recv()

    def pick(h):
        section = (zh + h) % 2
        for k in range(8):
            first = near[k] * 16 + section * SEC_OWN + offs[near[k], section] // 2
            at = (first + (wp + 512 - first) % CLASSES) // CLASSES
            picked[h, k] = held[pl.ds(at, 2)]

    f_copies = []
    for k in (7, 6, 5, 4, 3, 2, 1, 0):
        to_well = z * PLANE + near[k]
        f_copies.append(remote(picked.at[1, k], far_landed.at[wp], f_send.at[k], f_recv.at[k], to_well, far_shot))
    pick(1)

    @pl.when((zh == 1) & (z < 6))
    def _():
        for copy in f_copies:
            copy.start()

    pick(0)
    n_copies = []
    for k in (7, 6, 5, 4, 3, 2, 1):
        to_well = z * PLANE + near[k]
        copy = remote(picked.at[0, k], landed.at[wp], n_send.at[k], n_recv.at[k], to_well, shot)
        copy.start()
        n_copies.append(copy)
    landed[wp] = picked[0, 0]

    @pl.when((zh == 0) & (z >= 4))
    def _():
        pl.semaphore_wait(answered, 8)
        for copy in f_copies:
            copy.start()
        e_copy.start()

    own_first = wp * 16 + zh * SEC_OWN + offs[wp, zh] // 2

    def pass_on(h, kinds):
        more = far_extra if h else extra.at[0]

        def pieces(to_y, target):
            return [
                (ordered.at[h, pl.ds(2 * to_y, REACH_PAIRS)], target.at[pl.ds(0, REACH_PAIRS)]),
                (more.at[pl.ds(2 * to_y, OWN_PAIRS)], target.at[pl.ds(REACH_PAIRS, OWN_PAIRS)]),
                (more.at[pl.ds(SEC_OWN, 1)], target.at[pl.ds(BLOCKS - 1, 1)]),
            ]

        copies = []
        for i, peer in enumerate(y_peers):
            for kind in kinds:
                n = (h * 3 + i) * 3 + kind
                source, to = pieces(peer, far_hbm.at[i] if h else near_in.at[y])[kind]
                copies.append(remote(source, to, y_send.at[n], y_recv.at[n], well, zh * 4 + peer))
        kept = []
        for kind in kinds:
            source, to = pieces(y, near_in.at[4 if h else y])[kind]
            kept.append(pltpu.make_async_copy(source, to, keep_sem.at[h * 3 + kind]))
        return copies, kept

    def start(copies):
        for copy in copies:
            copy.start()

    def put_in_order(h, arrived):
        for i in range(SEC_REACH):
            ordered[h, i] = arrived[(own_first + i) % CLASSES, i // CLASSES]

    some, kept = pass_on(0, (1, 2))
    start(some + kept)
    for copy in n_copies:
        copy.wait_recv()

    @pl.when((zh == 1) & (z >= 6))
    def _():
        for copy in f_copies:
            copy.start()

    put_in_order(0, landed)
    more, kept_more = pass_on(0, (0,))
    start(more + kept_more)
    near_copies = some + kept + more + kept_more

    for copy in near_copies:
        copy.wait()
    load_table.wait()
    make_spectra(near_in, (0, 1, 2, 3), table, gate_vals, spectra, y)

    @pl.when((zh == 0) & (z < 4))
    def _():
        pl.semaphore_wait(answered, 8)
        for copy in f_copies:
            copy.start()
        e_copy.start()

    def keep(a, group, reals, imags):
        rows = pl.ds(group * 8, 8)
        for t in range(4):
            part[a, t, rows] = reals[t]
        for t in range(5):
            part[a, 4 + t, rows] = imags[t]

    some, kept = pass_on(1, (1, 2))
    more, kept_more = pass_on(1, (0,))

    def pass_extra():
        e_copy.wait_recv()
        start(some + kept)

    def pass_pairs():
        for copy in f_copies:
            copy.wait_recv()
        put_in_order(1, far_landed)
        start(more + kept_more)

    @pl.when(zh == 0)
    def _():
        pass_extra()
        pass_pairs()

    @pl.when(zh == 1)
    def _():
        pass_pairs()
        pass_extra()

    far_copies = some + more

    for copy in kept + kept_more:
        copy.wait()
    make_spectra(near_in, (4,), table, gate_vals, spectra, y)
    pair_sums(spectra, 5, offs[wp, zh] % 2, keep)
    keep_part = pltpu.make_async_copy(part, part_hbm, load_sem.at[5])
    keep_part.start()
    keep_part.wait()

    @pl.when(z > 0)
    def _():
        for k in range(8):
            z_copy(k).wait_send()

    for copy in a_copies + o_copies + n_copies + f_copies + [e_copy]:
        copy.wait_send()
    for copy in far_copies:
        copy.wait()


def fold(parts):
    row = lax.broadcasted_iota(jnp.int32, (8, W), 0)
    while len(parts) > 1:
        half = len(parts) // 2
        upper = (row & half) == 0
        merged = []
        for i in range(half):
            first, second = parts[i], parts[i + half]
            kept = jnp.where(upper, first, second)
            moved = jnp.where(upper, second, first)
            if half == 4:
                moved = pltpu.roll(moved, 4, 0)
            else:
                moved = jnp.where(upper, pltpu.roll(moved, 8 - half, 0), pltpu.roll(moved, half, 0))
            merged.append(kept + moved)
        parts = merged
    return parts[0]


def make_spectra(data, groups, table, gate_vals, spectra, y, unroll=False, ready=None, circle=None):
    lane = lax.broadcasted_iota(jnp.int32, (8, W), 1)
    if circle is None:
        angle = lane.astype(f32) * (2 * math.pi / W)
        circle = (jnp.cos(angle), jnp.sin(angle))
    cosines, sines = circle
    pairs = {1: 6, 3: 3, 4: 2}[len(groups)]

    for k in groups:
        block = pltpu.roll(data[k, BLOCKS - 1].astype(f32), (W - 4 * y) % W, 1)
        gate = (block[:8] * 8.0 + block[8:]).astype(jnp.int32)
        for slot in range(SLOTS):
            column = slot if slot < 20 else 12 + slot
            gate_vals[slot, k] = jnp.broadcast_to(gate[:, column : column + 1], (8, W))

    if ready is not None:
        ready.wait()

    @pl.loop(0, SLOTS // 2 // pairs, unroll=unroll)
    def _(step):
        lefts = []
        for p in range(pairs):
            for k in groups:
                both = data[k, pairs * step + p].astype(f32)
                halves = []
                for par in range(2):
                    window = both[par * 8 : par * 8 + 8]
                    fine = gate_vals[2 * (pairs * step + p) + par, k] & 7
                    low = jnp.where(lane >= fine, window, 0.0)
                    halves.append(jnp.concatenate([low, window - low], axis=1))
                lefts.append(jnp.concatenate(halves, axis=0).astype(bf16))
        flat = jnp.dot(jnp.concatenate(lefts, axis=0), table[...], preferred_element_type=f32)
        first = 0
        for p in range(pairs):
            for k in groups:
                for par in range(2):
                    slot = 2 * (pairs * step + p) + par
                    index = ((gate_vals[slot, k] >> 3) * lane) & 127
                    cosine = jnp.take_along_axis(cosines, index, axis=1)
                    sine = jnp.take_along_axis(sines, index, axis=1)
                    rows = slice(k * 8, k * 8 + 8)
                    for t in range(4):
                        real = flat[first : first + 8, t * W : (t + 1) * W]
                        imag = flat[first : first + 8, (4 + t) * W : (5 + t) * W]
                        spectra[slot, t, 0, rows, :] = cosine * real + sine * imag
                        spectra[slot, t, 1, rows, :] = cosine * imag - sine * real
                    first += 8


def pair_sums(spectra, groups, odd, emit):
    lane = lax.broadcasted_iota(jnp.int32, (8, W), 1)

    @pl.loop(0, 4)
    def _(a):
        reals = [[], []]
        imags = [[], []]
        for t in range(4):
            own = [[spectra[20 + a, t, c, k * 8 : k * 8 + 8, :] for c in range(2)] for k in range(groups)]
            for group in range(2):
                sums = []
                for j in range(8):
                    slot = a + odd + group * 8 + j
                    one = two = three = None
                    for k in range(groups):
                        re = spectra[slot, t, 0, k * 8 : k * 8 + 8, :]
                        im = spectra[slot, t, 1, k * 8 : k * 8 + 8, :]
                        first = own[k][0] * re
                        second = own[k][1] * im
                        third = own[k][0] * im - own[k][1] * re
                        one = first if one is None else one + first
                        two = second if two is None else two + second
                        three = third if three is None else three + third
                    sums.append((one, two, three))
                threes = fold([s[2] for s in sums])
                if t == 0:
                    ones = fold([s[0] for s in sums])
                    twos = fold([s[1] for s in sums])
                    reals[group].append(jnp.where(lane == 0, ones, ones + twos))
                    imags[group].append(twos)
                    imags[group].append(jnp.where(lane == 0, 0.0, threes))
                else:
                    reals[group].append(fold([s[0] + s[1] for s in sums]))
                    imags[group].append(threes)
        for group in range(2):
            emit(a, group, reals[group], imags[group])


def cross_kernel(
    off_hbm, data_hbm, part_hbm, table_hbm, out_hbm, off_ref, data, table, gate_vals, spectra, part, out, sem, out_sem
):
    z, wp, zh, y = place()
    load_data = pltpu.make_async_copy(data_hbm, data, sem.at[0])
    load_data.start()
    load_table = pltpu.make_async_copy(table_hbm, table, sem.at[1])
    load_table.start()
    load_off = pltpu.make_async_copy(off_hbm, off_ref, sem.at[2])
    load_off.start()
    load_part = pltpu.make_async_copy(part_hbm, part, sem.at[3])
    load_part.start()
    lane = lax.broadcasted_iota(jnp.int32, (8, W), 1)
    angle = lane.astype(f32) * (2 * math.pi / W)
    circle = (jnp.cos(angle), jnp.sin(angle))
    load_data.wait()
    lane = lax.broadcasted_iota(jnp.int32, (8, W), 1)
    make_spectra(data, (0, 1, 2), table, gate_vals, spectra, y, unroll=True, ready=load_table, circle=circle)

    def finish(a, group, reals, imags):
        rows = pl.ds(group * 8, 8)
        for t in range(4):
            out[a, rows, t * W : (t + 1) * W] = reals[t] + part[a, t, rows]
        imags = [imags[t] + part[a, 4 + t, rows] for t in range(5)]
        before = imags[0]
        for t in range(4):
            turned = pltpu.roll(imags[1 + t], 1, 1)
            out[a, rows, (4 + t) * W : (5 + t) * W] = jnp.where(lane == 0, before, turned)
            before = turned
        out[a, rows, 8 * W : 8 * W + 2] = jnp.where(lane == 0, before, 0.0)[:, :2]
        if group == 1:
            pltpu.make_async_copy(out.at[a], out_hbm.at[a], out_sem.at[a]).start()

    load_off.wait()
    load_part.wait()
    pair_sums(spectra, 3, off_ref[zh] & 1, finish)
    for a in range(4):
        pltpu.make_async_copy(out.at[a], out_hbm.at[a], out_sem.at[a]).wait()


def local(traces, gate_starts, section_offsets):
    hbm = pl.BlockSpec(memory_space=pltpu.HBM)
    any_space = pl.BlockSpec(memory_space=pl.ANY)
    dma = pltpu.SemaphoreType.DMA
    table = jnp.asarray(packed_table())
    far, part = pl.pallas_call(
        gather_kernel,
        out_shape=(
            jax.ShapeDtypeStruct((3, BLOCKS, 16, W), bf16),
            jax.ShapeDtypeStruct((4, 9, PARTNERS, W), f32),
        ),
        in_specs=[hbm, hbm, hbm, any_space],
        out_specs=(any_space, any_space),
        scratch_shapes=[
            pltpu.VMEM((5, BLOCKS, 16, W), bf16),
            pltpu.VMEM((2 * W, NT), bf16),
            pltpu.VMEM((SLOTS, 5, 8, W), jnp.int32),
            pltpu.VMEM((SLOTS, 4, 2, 40, W), f32),
            pltpu.VMEM((4, 9, PARTNERS, W), f32),
            pltpu.SMEM((PLANE, 2), jnp.int32),
            pltpu.VMEM((8, RECV, NT), bf16),
            pltpu.VMEM((8, 512), jnp.int32),
            pltpu.VMEM((256, 8), f32),
            pltpu.VMEM((RECV * 8, W), f32),
            pltpu.VMEM((16, 16, W), bf16),
            pltpu.VMEM((CLASSES, 2, 16, W), bf16),
            pltpu.VMEM((32, 16, W), bf16),
            pltpu.VMEM((2, PLANE, 2, 16, W), bf16),
            pltpu.VMEM((CLASSES, 2, 16, W), bf16),
            pltpu.VMEM((CLASSES, 2, 16, W), bf16),
            pltpu.VMEM((2, SEC_REACH, 16, W), bf16),
            pltpu.VMEM((2, SEC_OWN + 1, 16, W), bf16),
            pltpu.VMEM((SEC_OWN + 1, 16, W), bf16),
            dma((6,)), dma((8,)), dma((8,)), dma((8,)), dma((8,)), dma((8,)), dma((8,)),
            dma((8,)), dma((8,)), dma((8,)), dma((8,)), dma, dma, dma((18,)), dma((18,)), dma((6,)),
            pltpu.SemaphoreType.REGULAR,
        ],
        compiler_params=pltpu.CompilerParams(
            collective_id=0, has_side_effects=True, vmem_limit_bytes=60 * 2**20
        ),
        name="gather",
    )(section_offsets, traces, gate_starts, table)
    return cross_call(section_offsets, far, part, table)


def cross_call(section_offsets, far, part, table):
    any_space = pl.BlockSpec(memory_space=pl.ANY)
    dma = pltpu.SemaphoreType.DMA
    return pl.pallas_call(
        cross_kernel,
        out_shape=jax.ShapeDtypeStruct((4, PARTNERS, NT + 2), f32),
        in_specs=[any_space, any_space, any_space, any_space],
        out_specs=any_space,
        scratch_shapes=[
            pltpu.SMEM((2,), jnp.int32),
            pltpu.VMEM((3, BLOCKS, 16, W), bf16),
            pltpu.VMEM((2 * W, NT), bf16),
            pltpu.VMEM((SLOTS, 3, 8, W), jnp.int32),
            pltpu.VMEM((SLOTS, 4, 2, 24, W), f32),
            pltpu.VMEM((4, 9, PARTNERS, W), f32),
            pltpu.VMEM((4, PARTNERS, NT + 2), f32),
            dma((4,)), dma((4,)),
        ],
        compiler_params=pltpu.CompilerParams(vmem_limit_bytes=60 * 2**20),
        name="cross",
    )(section_offsets, far, part, table)


def solution(mesh):
    in_specs = (P("shot", "well", None), P("shot", None), P("well"))
    out_specs = P(("well", "shot"), None, None)
    return jax.shard_map(local, mesh=mesh, in_specs=in_specs, out_specs=out_specs, check_vma=False)
```

```python
import functools
import math

import jax
import jax.numpy as jnp
import ml_dtypes
import numpy as np
from jax import lax
from jax.experimental import pallas as pl
from jax.experimental.pallas import tpu as pltpu
from jax.sharding import PartitionSpec as P

NT = 1024
W = 128
SEC = 16
PARTNERS = 16
PLANE = 8
RECV = 32
OWN_PAIRS = 2
REACH_PAIRS = 10
BLOCKS = REACH_PAIRS + OWN_PAIRS + 1
SEC_REACH = 16
SEC_OWN = 8
CLASSES = 8
SLOTS = 2 * (REACH_PAIRS + OWN_PAIRS)
MESH = pl.DeviceIdType.MESH
f32 = jnp.float32
bf16 = jnp.bfloat16

def packed_table():
    steps = np.arange(2 * W)
    k = np.arange(NT // 2)
    angle = ((steps[:, None] * k[None, :]) % NT).astype(np.float32) * np.float32(2 * math.pi / NT)
    real = np.cos(angle)
    imag = -np.sin(angle)
    imag[:, 0] = np.cos(math.pi * steps)
    scale = np.float32(1.0 / math.sqrt(W))
    return (np.concatenate([real, imag], axis=1) * scale).astype(ml_dtypes.bfloat16)


def place():
    well = lax.axis_index("well")
    shot = lax.axis_index("shot")
    return well // PLANE, well % PLANE, shot // 4, shot % 4


def gather_kernel(
    off_hbm, traces_hbm, gates_hbm, table_hbm, far_hbm, part_hbm,
    near_in, table, gate_vals, spectra, part,
    offs, traces, gates, gate_cols, rows, unit, dealt, held, picked, landed, far_landed, ordered, extra, far_extra,
    load_sem, o_send, o_recv, a_send, a_recv, z_send, z_recv, n_send, n_recv,
    f_send, f_recv, e_send, e_recv, y_send, y_recv, keep_sem, answered,
):
    z, wp, zh, y = place()
    x, core = wp // 2, wp % 2
    well = z * PLANE + wp
    shot = zh * 4 + y
    far_shot = (1 - zh) * 4 + y
    before = jnp.maximum(z - 1, 0)

    steps = [(dx, dc) for dx in (0, 1, 3, 2) for dc in (0, 1)]
    near = [(x + dx) % 4 * 2 + (core + dc) % 2 for dx, dc in steps]
    y_peers = [(y + d) % 4 for d in (2, 1, 3)]

    load_traces = pltpu.make_async_copy(traces_hbm, traces, load_sem.at[3])
    here = pl.multiple_of(z * 256, 256)
    ahead = pl.multiple_of(jnp.minimum(z + 1, 7) * 256, 256)
    load_here = pltpu.make_async_copy(gates_hbm.at[:, pl.ds(here, 256)], gates.at[:, pl.ds(0, 256)], load_sem.at[0])
    load_ahead = pltpu.make_async_copy(gates_hbm.at[:, pl.ds(ahead, 256)], gates.at[:, pl.ds(256, 256)], load_sem.at[1])
    load_off = pltpu.make_async_copy(off_hbm, offs.at[wp], load_sem.at[2])
    load_table = pltpu.make_async_copy(table_hbm, table, load_sem.at[4])
    load_here.start()
    load_off.start()
    load_ahead.start()
    load_traces.start()

    barrier = pltpu.get_barrier_semaphore()

    def greet(to_well, to_shot):
        pl.semaphore_signal(barrier, inc=1, device_id=(to_well, to_shot), device_id_type=MESH)

    @pl.when(z < 7)
    def _():
        for peer in near:
            greet((z + 1) * PLANE + peer, shot)

    for peer in near[1:]:
        greet(z * PLANE + peer, shot)
    for peer in y_peers:
        greet(well, zh * 4 + peer)

    @pl.when(zh == 0)
    def _():
        for peer in near:
            greet(z * PLANE + peer, far_shot)

    def wait_for(more):
        @pl.when(z > 0)
        def _():
            pl.semaphore_wait(barrier, 18 + more)

        @pl.when(z == 0)
        def _():
            pl.semaphore_wait(barrier, 10 + more)

    load_table.start()

    @pl.when(z == 7)
    def _():
        held[pl.ds(16, 16)] = jnp.zeros((16, 16, W), bf16)

    lane = lax.broadcasted_iota(jnp.int32, (RECV, W), 1)
    taper = 0.5 - 0.5 * jnp.cos((lane[:8].astype(f32) + 0.5) * (2 * math.pi / W))
    taper = jnp.concatenate([taper] * (RECV // 8), axis=0)
    load_here.wait()
    gate_cols[...] = jnp.transpose(gates[:, :256].astype(f32))
    columns = gate_cols[pl.ds(pl.multiple_of(wp * RECV, RECV), RECV), :].astype(jnp.int32)
    load_ahead.wait()
    load_off.wait()
    all_gates = gates[...]
    halves = jnp.concatenate([all_gates >> 3, all_gates & 7], axis=0).astype(f32).astype(bf16)
    lanes = lax.broadcasted_iota(jnp.int32, (512, W), 1)
    index = lax.broadcasted_iota(jnp.int32, (512, W), 0)
    for h in (1, 0):
        own = wp * RECV + (zh + h) % 2 * SEC
        start = (own + offs[wp, (zh + h) % 2]) // 2 * 2
        wanted = jnp.where(lanes < 32, start + lanes, own - 32 + lanes)
        one_hot = jnp.where(index == wanted, 1.0, 0.0).astype(bf16)
        block = jnp.dot(halves, one_hot, preferred_element_type=f32)
        extra[h, SEC_OWN] = block.astype(bf16)

    @pl.when(zh == 0)
    def _():
        wait_for(0)

    def remote(source, target, send, receive, to_well, to_shot):
        return pltpu.make_async_remote_copy(
            src_ref=source, dst_ref=target, send_sem=send, recv_sem=receive,
            device_id=(to_well, to_shot), device_id_type=MESH,
        )

    load_traces.wait()

    @pl.when(zh == 1)
    def _():
        wait_for(8)
        for peer in near:
            pl.semaphore_signal(answered, inc=1, device_id=(z * PLANE + peer, far_shot), device_id_type=MESH)

    o_copies = []
    for k in range(1, 8):
        copy = remote(offs.at[wp], offs.at[wp], o_send.at[k], o_recv.at[k], z * PLANE + near[k], shot)
        copy.start()
        o_copies.append(copy)
    for s in range(8):
        data = traces[s].astype(f32)
        gate = jnp.broadcast_to(columns[:, s : s + 1], (RECV, W))
        fine = gate & 127
        tiles = [data[:, k * W : (k + 1) * W] for k in range(8)]
        pick = (gate & 512) != 0
        four = [jnp.where(pick, tiles[k + 4], tiles[k]) for k in range(4)] + [tiles[4]]
        pick = (gate & 256) != 0
        three = [jnp.where(pick, four[k + 2], four[k]) for k in range(3)]
        pick = (gate & 128) != 0
        low = jnp.where(pick, three[1], three[0])
        high = jnp.where(pick, three[2], three[1])
        turned = jnp.where(lane >= fine, low, high)
        for bit in range(3, 7):
            step = 1 << bit
            turned = jnp.where((fine & step) != 0, pltpu.roll(turned, W - step, 1), turned)
        rows[pl.ds(s, RECV, stride=8), :] = turned * jnp.take_along_axis(taper, (lane - (gate & 7)) & 127, axis=1)
    pairs = rows[...].reshape(16, 16, W).astype(bf16)
    unit[...] = pairs
    for i in range(2):
        for m in range(CLASSES):
            dealt[m, i] = pairs[i * CLASSES + m]
    for h in (1, 0):
        extra[h, :SEC_OWN] = unit[pl.ds((zh + h) % 2 * SEC_OWN, SEC_OWN)]

    e_copy = remote(extra.at[1], far_extra, e_send, e_recv, well, far_shot)

    mine = pl.ds(wp * 2, 2)
    mine_ahead = pl.ds(16 + wp * 2, 2)

    def z_copy(k):
        return remote(
            dealt.at[near[k]], held.at[mine_ahead], z_send.at[k], z_recv.at[k], before * PLANE + near[k], shot
        )

    @pl.when(z > 0)
    def _():
        for k in (7, 6, 5, 4, 3, 2, 1, 0):
            z_copy(k).start()

    a_copies = []
    for k in (7, 6, 5, 4, 3, 2, 1):
        to_well = z * PLANE + near[k]
        copy = remote(dealt.at[near[k]], held.at[mine], a_send.at[k], a_recv.at[k], to_well, shot)
        copy.start()
        a_copies.append(copy)
    held[mine] = dealt[wp]

    @pl.when(zh == 1)
    def _():
        e_copy.start()

    for copy in o_copies:
        copy.wait_recv()
    for copy in a_copies:
        copy.wait_recv()

    @pl.when(z < 7)
    def _():
        for k in range(8):
            z_copy(k).wait_recv()

    def pick(h):
        section = (zh + h) % 2
        for k in range(8):
            first = near[k] * 16 + section * SEC_OWN + offs[near[k], section] // 2
            at = (first + (wp + 512 - first) % CLASSES) // CLASSES
            picked[h, k] = held[pl.ds(at, 2)]

    f_copies = []
    for k in (7, 6, 5, 4, 3, 2, 1, 0):
        to_well = z * PLANE + near[k]
        f_copies.append(remote(picked.at[1, k], far_landed.at[wp], f_send.at[k], f_recv.at[k], to_well, far_shot))
    pick(1)

    @pl.when((zh == 1) & (z < 6))
    def _():
        for copy in f_copies:
            copy.start()

    pick(0)
    n_copies = []
    for k in (7, 6, 5, 4, 3, 2, 1):
        to_well = z * PLANE + near[k]
        copy = remote(picked.at[0, k], landed.at[wp], n_send.at[k], n_recv.at[k], to_well, shot)
        copy.start()
        n_copies.append(copy)
    landed[wp] = picked[0, 0]

    @pl.when((zh == 0) & (z >= 4))
    def _():
        pl.semaphore_wait(answered, 8)
        for copy in f_copies:
            copy.start()
        e_copy.start()

    own_first = wp * 16 + zh * SEC_OWN + offs[wp, zh] // 2

    def pass_on(h, kinds):
        more = far_extra if h else extra.at[0]

        def pieces(to_y, target):
            return [
                (ordered.at[h, pl.ds(2 * to_y, REACH_PAIRS)], target.at[pl.ds(0, REACH_PAIRS)]),
                (more.at[pl.ds(2 * to_y, OWN_PAIRS)], target.at[pl.ds(REACH_PAIRS, OWN_PAIRS)]),
                (more.at[pl.ds(SEC_OWN, 1)], target.at[pl.ds(BLOCKS - 1, 1)]),
            ]

        copies = []
        for i, peer in enumerate(y_peers):
            for kind in kinds:
                n = (h * 3 + i) * 3 + kind
                source, to = pieces(peer, far_hbm.at[i] if h else near_in.at[y])[kind]
                copies.append(remote(source, to, y_send.at[n], y_recv.at[n], well, zh * 4 + peer))
        kept = []
        for kind in kinds:
            source, to = pieces(y, near_in.at[4 if h else y])[kind]
            kept.append(pltpu.make_async_copy(source, to, keep_sem.at[h * 3 + kind]))
        return copies, kept

    def start(copies):
        for copy in copies:
            copy.start()

    def put_in_order(h, arrived):
        for i in range(SEC_REACH):
            ordered[h, i] = arrived[(own_first + i) % CLASSES, i // CLASSES]

    some, kept = pass_on(0, (1, 2))
    start(some + kept)
    for copy in n_copies:
        copy.wait_recv()

    @pl.when((zh == 1) & (z >= 6))
    def _():
        for copy in f_copies:
            copy.start()

    put_in_order(0, landed)
    more, kept_more = pass_on(0, (0,))
    start(more + kept_more)
    near_copies = some + kept + more + kept_more

    for copy in near_copies:
        copy.wait()
    load_table.wait()
    make_spectra(near_in, (0, 1, 2, 3), table, gate_vals, spectra, y)

    @pl.when((zh == 0) & (z < 4))
    def _():
        pl.semaphore_wait(answered, 8)
        for copy in f_copies:
            copy.start()
        e_copy.start()

    def keep(a, group, reals, imags):
        rows = pl.ds(group * 8, 8)
        for t in range(4):
            part[a, t, rows] = reals[t]
        for t in range(5):
            part[a, 4 + t, rows] = imags[t]

    some, kept = pass_on(1, (1, 2))
    more, kept_more = pass_on(1, (0,))

    def pass_extra():
        e_copy.wait_recv()
        start(some + kept)

    def pass_pairs():
        for copy in f_copies:
            copy.wait_recv()
        put_in_order(1, far_landed)
        start(more + kept_more)

    @pl.when(zh == 0)
    def _():
        pass_extra()
        pass_pairs()

    @pl.when(zh == 1)
    def _():
        pass_pairs()
        pass_extra()

    far_copies = some + more

    for copy in kept + kept_more:
        copy.wait()
    make_spectra(near_in, (4,), table, gate_vals, spectra, y)
    pair_sums(spectra, 5, offs[wp, zh] % 2, keep)
    keep_part = pltpu.make_async_copy(part, part_hbm, load_sem.at[5])
    keep_part.start()
    keep_part.wait()

    @pl.when(z > 0)
    def _():
        for k in range(8):
            z_copy(k).wait_send()

    for copy in a_copies + o_copies + n_copies + f_copies + [e_copy]:
        copy.wait_send()
    for copy in far_copies:
        copy.wait()


def fold(parts):
    row = lax.broadcasted_iota(jnp.int32, (8, W), 0)
    for step in (1, 2, 4):
        upper = (row & step) == 0
        merged = []
        for first, second in zip(parts[::2], parts[1::2]):
            moved = pltpu.roll(jnp.where(upper, second, first), 8 - step, 0)
            merged.append(jnp.where(upper, first, second) + moved)
        parts = merged
    return parts[0]


def make_spectra(data, groups, table, gate_vals, spectra, y, unroll=False, ready=None, circle=None):
    lane = lax.broadcasted_iota(jnp.int32, (8, W), 1)
    if circle is None:
        angle = lane.astype(f32) * (2 * math.pi / W)
        circle = (jnp.cos(angle), jnp.sin(angle))
    cosines, sines = circle
    pairs = {1: 6, 3: 3, 4: 2}[len(groups)]

    for k in groups:
        block = pltpu.roll(data[k, BLOCKS - 1].astype(f32), (W - 4 * y) % W, 1)
        gate = (block[:8] * 8.0 + block[8:]).astype(jnp.int32)
        for slot in range(SLOTS):
            column = slot if slot < 20 else 12 + slot
            gate_vals[slot, k] = jnp.broadcast_to(gate[:, column : column + 1], (8, W))

    if ready is not None:
        ready.wait()

    @pl.loop(0, SLOTS // 2 // pairs, unroll=unroll)
    def _(step):
        lefts = []
        for p in range(pairs):
            for k in groups:
                both = data[k, pairs * step + p].astype(f32)
                halves = []
                for par in range(2):
                    window = both[par * 8 : par * 8 + 8]
                    fine = gate_vals[2 * (pairs * step + p) + par, k] & 7
                    low = jnp.where(lane >= fine, window, 0.0)
                    halves.append(jnp.concatenate([low, window - low], axis=1))
                lefts.append(jnp.concatenate(halves, axis=0).astype(bf16))
        flat = jnp.dot(jnp.concatenate(lefts, axis=0), table[...], preferred_element_type=f32)
        first = 0
        for p in range(pairs):
            for k in groups:
                for par in range(2):
                    slot = 2 * (pairs * step + p) + par
                    index = ((gate_vals[slot, k] >> 3) * lane) & 127
                    cosine = jnp.take_along_axis(cosines, index, axis=1)
                    sine = jnp.take_along_axis(sines, index, axis=1)
                    rows = slice(k * 8, k * 8 + 8)
                    for t in range(4):
                        real = flat[first : first + 8, t * W : (t + 1) * W]
                        imag = flat[first : first + 8, (4 + t) * W : (5 + t) * W]
                        spectra[slot, t, 0, rows, :] = cosine * real + sine * imag
                        spectra[slot, t, 1, rows, :] = cosine * imag - sine * real
                    first += 8


def pair_sums(spectra, groups, odd, emit):
    lane = lax.broadcasted_iota(jnp.int32, (8, W), 1)

    @pl.loop(0, 4)
    def _(a):
        reals = [[], []]
        imags = [[], []]
        for t in range(4):
            own = [[spectra[20 + a, t, c, k * 8 : k * 8 + 8, :] for c in range(2)] for k in range(groups)]
            for group in range(2):
                sums = []
                for j in range(8):
                    slot = a + odd + group * 8 + j
                    one = two = three = None
                    for k in range(groups):
                        re = spectra[slot, t, 0, k * 8 : k * 8 + 8, :]
                        im = spectra[slot, t, 1, k * 8 : k * 8 + 8, :]
                        first = own[k][0] * re
                        second = own[k][1] * im
                        third = own[k][0] * im - own[k][1] * re
                        one = first if one is None else one + first
                        two = second if two is None else two + second
                        three = third if three is None else three + third
                    sums.append((one, two, three))
                threes = fold([s[2] for s in sums])
                if t == 0:
                    ones = fold([s[0] for s in sums])
                    twos = fold([s[1] for s in sums])
                    reals[group].append(jnp.where(lane == 0, ones, ones + twos))
                    imags[group].append(twos)
                    imags[group].append(jnp.where(lane == 0, 0.0, threes))
                else:
                    reals[group].append(fold([s[0] + s[1] for s in sums]))
                    imags[group].append(threes)
        for group in range(2):
            emit(a, group, reals[group], imags[group])


def cross_kernel(
    off_hbm, data_hbm, part_hbm, table_hbm, out_hbm, off_ref, data, table, gate_vals, spectra, part, out, sem, out_sem
):
    z, wp, zh, y = place()
    load_data = pltpu.make_async_copy(data_hbm, data, sem.at[0])
    load_data.start()
    load_table = pltpu.make_async_copy(table_hbm, table, sem.at[1])
    load_table.start()
    load_off = pltpu.make_async_copy(off_hbm, off_ref, sem.at[2])
    load_off.start()
    load_part = pltpu.make_async_copy(part_hbm, part, sem.at[3])
    load_part.start()
    lane = lax.broadcasted_iota(jnp.int32, (8, W), 1)
    angle = lane.astype(f32) * (2 * math.pi / W)
    circle = (jnp.cos(angle), jnp.sin(angle))
    load_data.wait()
    lane = lax.broadcasted_iota(jnp.int32, (8, W), 1)
    make_spectra(data, (0, 1, 2), table, gate_vals, spectra, y, unroll=True, ready=load_table, circle=circle)

    def finish(a, group, reals, imags):
        rows = pl.ds(group * 8, 8)
        for t in range(4):
            out[a, rows, t * W : (t + 1) * W] = reals[t] + part[a, t, rows]
        imags = [imags[t] + part[a, 4 + t, rows] for t in range(5)]
        before = imags[0]
        for t in range(4):
            turned = pltpu.roll(imags[1 + t], 1, 1)
            out[a, rows, (4 + t) * W : (5 + t) * W] = jnp.where(lane == 0, before, turned)
            before = turned
        out[a, rows, 8 * W : 8 * W + 2] = jnp.where(lane == 0, before, 0.0)[:, :2]
        if group == 1:
            pltpu.make_async_copy(out.at[a], out_hbm.at[a], out_sem.at[a]).start()

    load_off.wait()
    load_part.wait()
    pair_sums(spectra, 3, off_ref[zh] & 1, finish)
    for a in range(4):
        pltpu.make_async_copy(out.at[a], out_hbm.at[a], out_sem.at[a]).wait()


def local(traces, gate_starts, section_offsets):
    hbm = pl.BlockSpec(memory_space=pltpu.HBM)
    any_space = pl.BlockSpec(memory_space=pl.ANY)
    dma = pltpu.SemaphoreType.DMA
    table = jnp.asarray(packed_table())
    far, part = pl.pallas_call(
        gather_kernel,
        out_shape=(
            jax.ShapeDtypeStruct((3, BLOCKS, 16, W), bf16),
            jax.ShapeDtypeStruct((4, 9, PARTNERS, W), f32),
        ),
        in_specs=[hbm, hbm, hbm, any_space],
        out_specs=(any_space, any_space),
        scratch_shapes=[
            pltpu.VMEM((5, BLOCKS, 16, W), bf16),
            pltpu.VMEM((2 * W, NT), bf16),
            pltpu.VMEM((SLOTS, 5, 8, W), jnp.int32),
            pltpu.VMEM((SLOTS, 4, 2, 40, W), f32),
            pltpu.VMEM((4, 9, PARTNERS, W), f32),
            pltpu.SMEM((PLANE, 2), jnp.int32),
            pltpu.VMEM((8, RECV, NT), bf16),
            pltpu.VMEM((8, 512), jnp.int32),
            pltpu.VMEM((256, 8), f32),
            pltpu.VMEM((RECV * 8, W), f32),
            pltpu.VMEM((16, 16, W), bf16),
            pltpu.VMEM((CLASSES, 2, 16, W), bf16),
            pltpu.VMEM((32, 16, W), bf16),
            pltpu.VMEM((2, PLANE, 2, 16, W), bf16),
            pltpu.VMEM((CLASSES, 2, 16, W), bf16),
            pltpu.VMEM((CLASSES, 2, 16, W), bf16),
            pltpu.VMEM((2, SEC_REACH, 16, W), bf16),
            pltpu.VMEM((2, SEC_OWN + 1, 16, W), bf16),
            pltpu.VMEM((SEC_OWN + 1, 16, W), bf16),
            dma((6,)), dma((8,)), dma((8,)), dma((8,)), dma((8,)), dma((8,)), dma((8,)),
            dma((8,)), dma((8,)), dma((8,)), dma((8,)), dma, dma, dma((18,)), dma((18,)), dma((6,)),
            pltpu.SemaphoreType.REGULAR,
        ],
        compiler_params=pltpu.CompilerParams(
            collective_id=0, has_side_effects=True, vmem_limit_bytes=60 * 2**20
        ),
        name="gather",
    )(section_offsets, traces, gate_starts, table)
    return cross_call(section_offsets, far, part, table)


def cross_call(section_offsets, far, part, table):
    any_space = pl.BlockSpec(memory_space=pl.ANY)
    dma = pltpu.SemaphoreType.DMA
    return pl.pallas_call(
        cross_kernel,
        out_shape=jax.ShapeDtypeStruct((4, PARTNERS, NT + 2), f32),
        in_specs=[any_space, any_space, any_space, any_space],
        out_specs=any_space,
        scratch_shapes=[
            pltpu.SMEM((2,), jnp.int32),
            pltpu.VMEM((3, BLOCKS, 16, W), bf16),
            pltpu.VMEM((2 * W, NT), bf16),
            pltpu.VMEM((SLOTS, 3, 8, W), jnp.int32),
            pltpu.VMEM((SLOTS, 4, 2, 24, W), f32),
            pltpu.VMEM((4, 9, PARTNERS, W), f32),
            pltpu.VMEM((4, PARTNERS, NT + 2), f32),
            dma((4,)), dma((4,)),
        ],
        compiler_params=pltpu.CompilerParams(vmem_limit_bytes=60 * 2**20),
        name="cross",
    )(section_offsets, far, part, table)


def solution(mesh):
    in_specs = (P("shot", "well", None), P("shot", None), P("well"))
    out_specs = P(("well", "shot"), None, None)
    return jax.shard_map(local, mesh=mesh, in_specs=in_specs, out_specs=out_specs, check_vma=False)
```

```python
import functools
import math

import jax
import jax.numpy as jnp
import ml_dtypes
import numpy as np
from jax import lax
from jax.experimental import pallas as pl
from jax.experimental.pallas import tpu as pltpu
from jax.sharding import PartitionSpec as P

NT = 1024
W = 128
SEC = 16
PARTNERS = 16
PLANE = 8
RECV = 32
OWN_PAIRS = 2
REACH_PAIRS = 10
BLOCKS = REACH_PAIRS + OWN_PAIRS + 1
SEC_REACH = 16
SEC_OWN = 8
CLASSES = 8
SLOTS = 2 * (REACH_PAIRS + OWN_PAIRS)
MESH = pl.DeviceIdType.MESH
f32 = jnp.float32
bf16 = jnp.bfloat16

def packed_table():
    steps = np.arange(2 * W)
    k = np.arange(NT // 2)
    angle = ((steps[:, None] * k[None, :]) % NT).astype(np.float32) * np.float32(2 * math.pi / NT)
    real = np.cos(angle)
    imag = -np.sin(angle)
    imag[:, 0] = np.cos(math.pi * steps)
    scale = np.float32(1.0 / math.sqrt(W))
    return (np.concatenate([real, imag], axis=1) * scale).astype(ml_dtypes.bfloat16)


def place():
    well = lax.axis_index("well")
    shot = lax.axis_index("shot")
    return well // PLANE, well % PLANE, shot // 4, shot % 4


def gather_kernel(
    off_hbm, traces_hbm, gates_hbm, table_hbm, far_hbm, part_hbm,
    near_in, table, gate_vals, spectra, part,
    offs, traces, gates, gate_cols, rows, unit, dealt, held, picked, landed, far_landed, ordered, extra, far_extra,
    load_sem, o_send, o_recv, a_send, a_recv, z_send, z_recv, n_send, n_recv,
    f_send, f_recv, e_send, e_recv, y_send, y_recv, keep_sem, answered,
):
    z, wp, zh, y = place()
    x, core = wp // 2, wp % 2
    well = z * PLANE + wp
    shot = zh * 4 + y
    far_shot = (1 - zh) * 4 + y
    before = jnp.maximum(z - 1, 0)

    steps = [(dx, dc) for dx in (0, 1, 3, 2) for dc in (0, 1)]
    near = [(x + dx) % 4 * 2 + (core + dc) % 2 for dx, dc in steps]
    y_peers = [(y + d) % 4 for d in (2, 1, 3)]

    load_traces = pltpu.make_async_copy(traces_hbm, traces, load_sem.at[3])
    here = pl.multiple_of(z * 256, 256)
    ahead = pl.multiple_of(jnp.minimum(z + 1, 7) * 256, 256)
    load_here = pltpu.make_async_copy(gates_hbm.at[:, pl.ds(here, 256)], gates.at[:, pl.ds(0, 256)], load_sem.at[0])
    load_ahead = pltpu.make_async_copy(gates_hbm.at[:, pl.ds(ahead, 256)], gates.at[:, pl.ds(256, 256)], load_sem.at[1])
    load_off = pltpu.make_async_copy(off_hbm, offs.at[wp], load_sem.at[2])
    load_table = pltpu.make_async_copy(table_hbm, table, load_sem.at[4])
    load_here.start()
    load_off.start()
    load_ahead.start()
    load_traces.start()

    barrier = pltpu.get_barrier_semaphore()

    def greet(to_well, to_shot):
        pl.semaphore_signal(barrier, inc=1, device_id=(to_well, to_shot), device_id_type=MESH)

    @pl.when(z < 7)
    def _():
        for peer in near:
            greet((z + 1) * PLANE + peer, shot)

    for peer in near[1:]:
        greet(z * PLANE + peer, shot)
    for peer in y_peers:
        greet(well, zh * 4 + peer)

    @pl.when(zh == 0)
    def _():
        for peer in near:
            greet(z * PLANE + peer, far_shot)

    def wait_for(more):
        @pl.when(z > 0)
        def _():
            pl.semaphore_wait(barrier, 18 + more)

        @pl.when(z == 0)
        def _():
            pl.semaphore_wait(barrier, 10 + more)

    load_table.start()

    @pl.when(z == 7)
    def _():
        held[pl.ds(16, 16)] = jnp.zeros((16, 16, W), bf16)

    lane = lax.broadcasted_iota(jnp.int32, (RECV, W), 1)
    taper = 0.5 - 0.5 * jnp.cos((lane[:8].astype(f32) + 0.5) * (2 * math.pi / W))
    taper = jnp.concatenate([taper] * (RECV // 8), axis=0)
    load_here.wait()
    gate_cols[...] = jnp.transpose(gates[:, :256].astype(f32))
    columns = gate_cols[pl.ds(pl.multiple_of(wp * RECV, RECV), RECV), :].astype(jnp.int32)
    load_ahead.wait()
    load_off.wait()
    all_gates = gates[...]
    halves = jnp.concatenate([all_gates >> 3, all_gates & 7], axis=0).astype(f32).astype(bf16)
    lanes = lax.broadcasted_iota(jnp.int32, (512, W), 1)
    index = lax.broadcasted_iota(jnp.int32, (512, W), 0)
    for h in (1, 0):
        own = wp * RECV + (zh + h) % 2 * SEC
        start = (own + offs[wp, (zh + h) % 2]) // 2 * 2
        wanted = jnp.where(lanes < 32, start + lanes, own - 32 + lanes)
        one_hot = jnp.where(index == wanted, 1.0, 0.0).astype(bf16)
        block = jnp.dot(halves, one_hot, preferred_element_type=f32)
        extra[h, SEC_OWN] = block.astype(bf16)

    @pl.when(zh == 0)
    def _():
        wait_for(0)

    def remote(source, target, send, receive, to_well, to_shot):
        return pltpu.make_async_remote_copy(
            src_ref=source, dst_ref=target, send_sem=send, recv_sem=receive,
            device_id=(to_well, to_shot), device_id_type=MESH,
        )

    load_traces.wait()

    @pl.when(zh == 1)
    def _():
        wait_for(8)
        for peer in near:
            pl.semaphore_signal(answered, inc=1, device_id=(z * PLANE + peer, far_shot), device_id_type=MESH)

    o_copies = []
    for k in range(1, 8):
        copy = remote(offs.at[wp], offs.at[wp], o_send.at[k], o_recv.at[k], z * PLANE + near[k], shot)
        copy.start()
        o_copies.append(copy)
    for s in range(8):
        data = traces[s].astype(f32)
        gate = jnp.broadcast_to(columns[:, s : s + 1], (RECV, W))
        fine = gate & 127
        tiles = [data[:, k * W : (k + 1) * W] for k in range(8)]
        pick = (gate & 512) != 0
        four = [jnp.where(pick, tiles[k + 4], tiles[k]) for k in range(4)] + [tiles[4]]
        pick = (gate & 256) != 0
        three = [jnp.where(pick, four[k + 2], four[k]) for k in range(3)]
        pick = (gate & 128) != 0
        low = jnp.where(pick, three[1], three[0])
        high = jnp.where(pick, three[2], three[1])
        turned = jnp.where(lane >= fine, low, high)
        for bit in range(3, 7):
            step = 1 << bit
            turned = jnp.where((fine & step) != 0, pltpu.roll(turned, W - step, 1), turned)
        rows[pl.ds(s, RECV, stride=8), :] = turned * jnp.take_along_axis(taper, (lane - (gate & 7)) & 127, axis=1)
    pairs = rows[...].reshape(16, 16, W).astype(bf16)
    unit[...] = pairs
    for i in range(2):
        for m in range(CLASSES):
            dealt[m, i] = pairs[i * CLASSES + m]
    for h in (1, 0):
        extra[h, :SEC_OWN] = unit[pl.ds((zh + h) % 2 * SEC_OWN, SEC_OWN)]

    e_copy = remote(extra.at[1], far_extra, e_send, e_recv, well, far_shot)

    mine = pl.ds(wp * 2, 2)
    mine_ahead = pl.ds(16 + wp * 2, 2)

    def z_copy(k):
        return remote(
            dealt.at[near[k]], held.at[mine_ahead], z_send.at[k], z_recv.at[k], before * PLANE + near[k], shot
        )

    @pl.when(z > 0)
    def _():
        for k in (7, 6, 5, 4, 3, 2, 1, 0):
            z_copy(k).start()

    a_copies = []
    for k in (7, 6, 5, 4, 3, 2, 1):
        to_well = z * PLANE + near[k]
        copy = remote(dealt.at[near[k]], held.at[mine], a_send.at[k], a_recv.at[k], to_well, shot)
        copy.start()
        a_copies.append(copy)
    held[mine] = dealt[wp]

    @pl.when(zh == 1)
    def _():
        e_copy.start()

    for copy in o_copies:
        copy.wait_recv()
    for copy in a_copies:
        copy.wait_recv()

    @pl.when(z < 7)
    def _():
        for k in range(8):
            z_copy(k).wait_recv()

    def pick(h, k):
        section = (zh + h) % 2
        first = near[k] * 16 + section * SEC_OWN + offs[near[k], section] // 2
        at = (first + (wp + 512 - first) % CLASSES) // CLASSES
        picked[h, k] = held[pl.ds(at, 2)]

    f_copies = []
    for k in (7, 6, 5, 4, 3, 2, 1, 0):
        to_well = z * PLANE + near[k]
        f_copies.append(remote(picked.at[1, k], far_landed.at[wp], f_send.at[k], f_recv.at[k], to_well, far_shot))


    @pl.when((zh == 1) & (z < 6))
    def _():
        for copy, k in zip(f_copies, (7, 6, 5, 4, 3, 2, 1, 0)):
            pick(1, k)
            copy.start()

    @pl.when((zh == 0) | (z >= 6))
    def _():
        for k in range(8):
            pick(1, k)

    pick(0, 0)
    n_copies = []
    for k in (7, 6, 5, 4, 3, 2, 1):
        to_well = z * PLANE + near[k]
        pick(0, k)
        copy = remote(picked.at[0, k], landed.at[wp], n_send.at[k], n_recv.at[k], to_well, shot)
        copy.start()
        n_copies.append(copy)
    landed[wp] = picked[0, 0]

    @pl.when((zh == 0) & (z >= 4))
    def _():
        pl.semaphore_wait(answered, 8)
        for copy in f_copies:
            copy.start()
        e_copy.start()

    own_first = wp * 16 + zh * SEC_OWN + offs[wp, zh] // 2

    def pass_on(h, kinds):
        more = far_extra if h else extra.at[0]

        def pieces(to_y, target):
            return [
                (ordered.at[h, pl.ds(2 * to_y, REACH_PAIRS)], target.at[pl.ds(0, REACH_PAIRS)]),
                (more.at[pl.ds(2 * to_y, OWN_PAIRS)], target.at[pl.ds(REACH_PAIRS, OWN_PAIRS)]),
                (more.at[pl.ds(SEC_OWN, 1)], target.at[pl.ds(BLOCKS - 1, 1)]),
            ]

        copies = []
        for i, peer in enumerate(y_peers):
            for kind in kinds:
                n = (h * 3 + i) * 3 + kind
                source, to = pieces(peer, far_hbm.at[i] if h else near_in.at[y])[kind]
                copies.append(remote(source, to, y_send.at[n], y_recv.at[n], well, zh * 4 + peer))
        kept = []
        for kind in kinds:
            source, to = pieces(y, near_in.at[4 if h else y])[kind]
            kept.append(pltpu.make_async_copy(source, to, keep_sem.at[h * 3 + kind]))
        return copies, kept

    def start(copies):
        for copy in copies:
            copy.start()

    def put_in_order(h, arrived):
        for i in range(SEC_REACH):
            ordered[h, i] = arrived[(own_first + i) % CLASSES, i // CLASSES]

    some, kept = pass_on(0, (1, 2))
    start(some + kept)
    for copy in n_copies:
        copy.wait_recv()

    @pl.when((zh == 1) & (z >= 6))
    def _():
        for copy in f_copies:
            copy.start()

    put_in_order(0, landed)
    more, kept_more = pass_on(0, (0,))
    start(more + kept_more)
    near_copies = some + kept + more + kept_more

    for copy in near_copies:
        copy.wait()
    load_table.wait()
    make_spectra(near_in, (0, 1, 2, 3), table, gate_vals, spectra, y)

    @pl.when((zh == 0) & (z < 4))
    def _():
        pl.semaphore_wait(answered, 8)
        for copy in f_copies:
            copy.start()
        e_copy.start()

    def keep(a, group, reals, imags):
        rows = pl.ds(group * 8, 8)
        for t in range(4):
            part[a, t, rows] = reals[t]
        for t in range(5):
            part[a, 4 + t, rows] = imags[t]

    some, kept = pass_on(1, (1, 2))
    more, kept_more = pass_on(1, (0,))

    def pass_extra():
        e_copy.wait_recv()
        start(some + kept)

    def pass_pairs():
        for copy in f_copies:
            copy.wait_recv()
        put_in_order(1, far_landed)
        start(more + kept_more)

    @pl.when(zh == 0)
    def _():
        pass_extra()
        pass_pairs()

    @pl.when(zh == 1)
    def _():
        pass_pairs()
        pass_extra()

    far_copies = some + more

    for copy in kept + kept_more:
        copy.wait()
    make_spectra(near_in, (4,), table, gate_vals, spectra, y)
    pair_sums(spectra, 5, offs[wp, zh] % 2, keep)
    keep_part = pltpu.make_async_copy(part, part_hbm, load_sem.at[5])
    keep_part.start()
    keep_part.wait()

    @pl.when(z > 0)
    def _():
        for k in range(8):
            z_copy(k).wait_send()

    for copy in a_copies + o_copies + n_copies + f_copies + [e_copy]:
        copy.wait_send()
    for copy in far_copies:
        copy.wait()


def fold(parts):
    row = lax.broadcasted_iota(jnp.int32, (8, W), 0)
    for step in (1, 2, 4):
        upper = (row & step) == 0
        merged = []
        for first, second in zip(parts[::2], parts[1::2]):
            moved = pltpu.roll(jnp.where(upper, second, first), 8 - step, 0)
            merged.append(jnp.where(upper, first, second) + moved)
        parts = merged
    return parts[0]


def make_spectra(data, groups, table, gate_vals, spectra, y, unroll=False, ready=None, circle=None):
    lane = lax.broadcasted_iota(jnp.int32, (8, W), 1)
    if circle is None:
        angle = lane.astype(f32) * (2 * math.pi / W)
        circle = (jnp.cos(angle), jnp.sin(angle))
    cosines, sines = circle
    pairs = {1: 6, 3: 3, 4: 2}[len(groups)]

    for k in groups:
        block = pltpu.roll(data[k, BLOCKS - 1].astype(f32), (W - 4 * y) % W, 1)
        gate = (block[:8] * 8.0 + block[8:]).astype(jnp.int32)
        for slot in range(SLOTS):
            column = slot if slot < 20 else 12 + slot
            gate_vals[slot, k] = jnp.broadcast_to(gate[:, column : column + 1], (8, W))

    if ready is not None:
        ready.wait()

    @pl.loop(0, SLOTS // 2 // pairs, unroll=unroll)
    def _(step):
        lefts = []
        for p in range(pairs):
            for k in groups:
                both = data[k, pairs * step + p].astype(f32)
                halves = []
                for par in range(2):
                    window = both[par * 8 : par * 8 + 8]
                    fine = gate_vals[2 * (pairs * step + p) + par, k] & 7
                    low = jnp.where(lane >= fine, window, 0.0)
                    halves.append(jnp.concatenate([low, window - low], axis=1))
                lefts.append(jnp.concatenate(halves, axis=0).astype(bf16))
        flat = jnp.dot(jnp.concatenate(lefts, axis=0), table[...], preferred_element_type=f32)
        first = 0
        for p in range(pairs):
            for k in groups:
                for par in range(2):
                    slot = 2 * (pairs * step + p) + par
                    index = ((gate_vals[slot, k] >> 3) * lane) & 127
                    cosine = jnp.take_along_axis(cosines, index, axis=1)
                    sine = jnp.take_along_axis(sines, index, axis=1)
                    rows = slice(k * 8, k * 8 + 8)
                    for t in range(4):
                        real = flat[first : first + 8, t * W : (t + 1) * W]
                        imag = flat[first : first + 8, (4 + t) * W : (5 + t) * W]
                        spectra[slot, t, 0, rows, :] = cosine * real + sine * imag
                        spectra[slot, t, 1, rows, :] = cosine * imag - sine * real
                    first += 8


def pair_sums(spectra, groups, odd, emit):
    lane = lax.broadcasted_iota(jnp.int32, (8, W), 1)

    @pl.loop(0, 4)
    def _(a):
        reals = [[], []]
        imags = [[], []]
        for t in range(4):
            own = [[spectra[20 + a, t, c, k * 8 : k * 8 + 8, :] for c in range(2)] for k in range(groups)]
            for group in range(2):
                sums = []
                for j in range(8):
                    slot = a + odd + group * 8 + j
                    one = two = three = None
                    for k in range(groups):
                        re = spectra[slot, t, 0, k * 8 : k * 8 + 8, :]
                        im = spectra[slot, t, 1, k * 8 : k * 8 + 8, :]
                        first = own[k][0] * re
                        second = own[k][1] * im
                        third = own[k][0] * im - own[k][1] * re
                        one = first if one is None else one + first
                        two = second if two is None else two + second
                        three = third if three is None else three + third
                    sums.append((one, two, three))
                threes = fold([s[2] for s in sums])
                if t == 0:
                    ones = fold([s[0] for s in sums])
                    twos = fold([s[1] for s in sums])
                    reals[group].append(jnp.where(lane == 0, ones, ones + twos))
                    imags[group].append(twos)
                    imags[group].append(jnp.where(lane == 0, 0.0, threes))
                else:
                    reals[group].append(fold([s[0] + s[1] for s in sums]))
                    imags[group].append(threes)
        for group in range(2):
            emit(a, group, reals[group], imags[group])


def cross_kernel(
    off_hbm, data_hbm, part_hbm, table_hbm, out_hbm, off_ref, data, table, gate_vals, spectra, part, out, sem, out_sem
):
    z, wp, zh, y = place()
    load_data = pltpu.make_async_copy(data_hbm, data, sem.at[0])
    load_data.start()
    load_table = pltpu.make_async_copy(table_hbm, table, sem.at[1])
    load_table.start()
    load_off = pltpu.make_async_copy(off_hbm, off_ref, sem.at[2])
    load_off.start()
    load_part = pltpu.make_async_copy(part_hbm, part, sem.at[3])
    load_part.start()
    lane = lax.broadcasted_iota(jnp.int32, (8, W), 1)
    angle = lane.astype(f32) * (2 * math.pi / W)
    circle = (jnp.cos(angle), jnp.sin(angle))
    load_data.wait()
    lane = lax.broadcasted_iota(jnp.int32, (8, W), 1)
    make_spectra(data, (0, 1, 2), table, gate_vals, spectra, y, unroll=True, ready=load_table, circle=circle)

    def finish(a, group, reals, imags):
        rows = pl.ds(group * 8, 8)
        for t in range(4):
            out[a, rows, t * W : (t + 1) * W] = reals[t] + part[a, t, rows]
        imags = [imags[t] + part[a, 4 + t, rows] for t in range(5)]
        before = imags[0]
        for t in range(4):
            turned = pltpu.roll(imags[1 + t], 1, 1)
            out[a, rows, (4 + t) * W : (5 + t) * W] = jnp.where(lane == 0, before, turned)
            before = turned
        out[a, rows, 8 * W : 8 * W + 2] = jnp.where(lane == 0, before, 0.0)[:, :2]
        if group == 1:
            pltpu.make_async_copy(out.at[a], out_hbm.at[a], out_sem.at[a]).start()

    load_off.wait()
    load_part.wait()
    pair_sums(spectra, 3, off_ref[zh] & 1, finish)
    for a in range(4):
        pltpu.make_async_copy(out.at[a], out_hbm.at[a], out_sem.at[a]).wait()


def local(traces, gate_starts, section_offsets):
    hbm = pl.BlockSpec(memory_space=pltpu.HBM)
    any_space = pl.BlockSpec(memory_space=pl.ANY)
    dma = pltpu.SemaphoreType.DMA
    table = jnp.asarray(packed_table())
    far, part = pl.pallas_call(
        gather_kernel,
        out_shape=(
            jax.ShapeDtypeStruct((3, BLOCKS, 16, W), bf16),
            jax.ShapeDtypeStruct((4, 9, PARTNERS, W), f32),
        ),
        in_specs=[hbm, hbm, hbm, any_space],
        out_specs=(any_space, any_space),
        scratch_shapes=[
            pltpu.VMEM((5, BLOCKS, 16, W), bf16),
            pltpu.VMEM((2 * W, NT), bf16),
            pltpu.VMEM((SLOTS, 5, 8, W), jnp.int32),
            pltpu.VMEM((SLOTS, 4, 2, 40, W), f32),
            pltpu.VMEM((4, 9, PARTNERS, W), f32),
            pltpu.SMEM((PLANE, 2), jnp.int32),
            pltpu.VMEM((8, RECV, NT), bf16),
            pltpu.VMEM((8, 512), jnp.int32),
            pltpu.VMEM((256, 8), f32),
            pltpu.VMEM((RECV * 8, W), f32),
            pltpu.VMEM((16, 16, W), bf16),
            pltpu.VMEM((CLASSES, 2, 16, W), bf16),
            pltpu.VMEM((32, 16, W), bf16),
            pltpu.VMEM((2, PLANE, 2, 16, W), bf16),
            pltpu.VMEM((CLASSES, 2, 16, W), bf16),
            pltpu.VMEM((CLASSES, 2, 16, W), bf16),
            pltpu.VMEM((2, SEC_REACH, 16, W), bf16),
            pltpu.VMEM((2, SEC_OWN + 1, 16, W), bf16),
            pltpu.VMEM((SEC_OWN + 1, 16, W), bf16),
            dma((6,)), dma((8,)), dma((8,)), dma((8,)), dma((8,)), dma((8,)), dma((8,)),
            dma((8,)), dma((8,)), dma((8,)), dma((8,)), dma, dma, dma((18,)), dma((18,)), dma((6,)),
            pltpu.SemaphoreType.REGULAR,
        ],
        compiler_params=pltpu.CompilerParams(
            collective_id=0, has_side_effects=True, vmem_limit_bytes=60 * 2**20
        ),
        name="gather",
    )(section_offsets, traces, gate_starts, table)
    return cross_call(section_offsets, far, part, table)


def cross_call(section_offsets, far, part, table):
    any_space = pl.BlockSpec(memory_space=pl.ANY)
    dma = pltpu.SemaphoreType.DMA
    return pl.pallas_call(
        cross_kernel,
        out_shape=jax.ShapeDtypeStruct((4, PARTNERS, NT + 2), f32),
        in_specs=[any_space, any_space, any_space, any_space],
        out_specs=any_space,
        scratch_shapes=[
            pltpu.SMEM((2,), jnp.int32),
            pltpu.VMEM((3, BLOCKS, 16, W), bf16),
            pltpu.VMEM((2 * W, NT), bf16),
            pltpu.VMEM((SLOTS, 3, 8, W), jnp.int32),
            pltpu.VMEM((SLOTS, 4, 2, 24, W), f32),
            pltpu.VMEM((4, 9, PARTNERS, W), f32),
            pltpu.VMEM((4, PARTNERS, NT + 2), f32),
            dma((4,)), dma((4,)),
        ],
        compiler_params=pltpu.CompilerParams(vmem_limit_bytes=60 * 2**20),
        name="cross",
    )(section_offsets, far, part, table)


def solution(mesh):
    in_specs = (P("shot", "well", None), P("shot", None), P("well"))
    out_specs = P(("well", "shot"), None, None)
    return jax.shard_map(local, mesh=mesh, in_specs=in_specs, out_specs=out_specs, check_vma=False)
```
